512 devices in a mesh: dp: 4 (over x_hi, core), ctx: 128 (over y, z, x_lo).
Axes of the slice: x: 4 (x_hi: 2, x_lo: 2; x = x_hi * 2 + x_lo), y: 4, z: 16, core: 2. Of those that a mesh axis runs over, the one named last changes fastest.
Arguments:
- queries: bfloat16 [4, 16384, 704], P('dp', 'ctx'), may hold values from -6 to 6
- keys: bfloat16 [4, 16384, 704], P('dp', 'ctx'), may hold values from -6 to 6
- values: bfloat16 [4, 16384, 704], P('dp', 'ctx'), may hold values from -24 to 24
- patch_ids: int32 [4, 16384], P('dp'), may hold values from 0 to 511
- counts: int32 [4, 128], P('dp'), may hold values from 1 to 128, 8192 in all within a row
- cotangent: bfloat16 [4, 16384, 1408], P('dp', 'ctx'), may hold values from -6 to 6
- w_out: bfloat16 [704, 1408], P('dp'), may hold values from -0.21875 to 0.21875
Outputs:
- attended: bfloat16 [4, 16384, 1408], P('dp', 'ctx')
- grad_queries: bfloat16 [4, 16384, 704], P('dp', 'ctx')
- grad_keys: bfloat16 [4, 16384, 704], P('dp', 'ctx')
- grad_values: bfloat16 [4, 16384, 704], P('dp', 'ctx')
- grad_w_out: float32 [704, 1408], P('dp')
The draws below stay inside these ranges and needn't reach their ends.
Inputs may be any that keep to these rules, and one draw needn't show every extreme that they name: patch_ids[r] is the kept patch's frame within its time shard times 256 plus its place in the frame; rows past a shard's count are padding. `counts`: each time shard's live rows come first in its 128 rows.
All inputs are finite; a program needn't handle non-finite values.
Results may differ from the reference program's by a relative error of at most 0.012.
The reference program's roundings to bfloat16 on the way count: a program that leaves them out, or rounds other values in their place, can miss the bound.
Values may be sent and summed in bfloat16 or wider, within the bound.
A program may use at most 64 MiB of HBM per device.

```python
import math
import jax
import jax.numpy as jnp
import numpy as np
from jax import lax

D = 1408
HEAD = 88
HEADS = 8
PATCHES = 256
FR = 2
CAP = 128
SPAN = 2
WIN = 4
HW = 704
CLIPS = 4
TOKENS = 16384
N_CTX = 128


def draw_queries(key, part):
    key = jax.random.fold_in(key, 3)
    drawn = jnp.clip(jax.random.normal(key, (CLIPS, TOKENS, HW), jnp.float32), -6.0, 6.0)
    return drawn.astype(jnp.bfloat16)


def draw_keys(key, part):
    key = jax.random.fold_in(key, 5)
    drawn = jnp.clip(jax.random.normal(key, (CLIPS, TOKENS, HW), jnp.float32), -6.0, 6.0)
    return drawn.astype(jnp.bfloat16)


def set_ends(values, rng, smallest, high):
    longest = values.shape.index(max(values.shape))
    spots = []
    for shift in (0, 1):
        where = [jax.random.randint(jax.random.fold_in(rng, axis), (), 0, length) for axis, length in enumerate(values.shape)]
        where[longest] = (where[longest] + shift) % values.shape[longest]
        spots.append(tuple(where))
    return values.at[spots[0]].set(smallest).at[spots[1]].set(high)


def shard_levels(rng, shape, cuts, low, high):
    gain = 1.0
    for axis_at, shards_of in cuts:
        heights = jax.random.uniform(jax.random.fold_in(jax.random.fold_in(rng, 6), axis_at), (shards_of,), jnp.float32, low / len(cuts), high / len(cuts))
        gain = gain * jnp.repeat(jnp.exp(heights), shape[axis_at] // shards_of).reshape((-1,) + (1,) * (len(shape) - 1 - axis_at))
    return gain


def length_profile(number_of, total, bound, skew):
    weights = [(1 << 20) // math.isqrt(standing ** skew) + 1 for standing in range(2, number_of + 1)]
    spare, given = total - bound - (number_of - 1), [1] * (number_of - 1)
    while spare > 0:
        free = [i for i in range(number_of - 1) if given[i] < bound]
        mass, left = sum([weights[i] for i in free]), spare
        for i in free:
            extra = min(bound - given[i], max(1, left * weights[i] // mass), spare)
            given[i] = given[i] + extra
            spare = spare - extra
    return np.array([bound] + given)


def uneven_parts(key, amount, total, bound, slope):
    if amount == 2:
        one = jax.random.randint(key, (), max(1, total - bound), min(bound, total - 1) + 1)
        return jnp.stack([one, total - one])
    sizes = jnp.asarray(length_profile(amount, total, bound, slope), jnp.int32)
    pairs = (amount - 1) // 2
    giver, sink = sizes[1:1 + 2 * pairs:2], sizes[2:2 + 2 * pairs:2]
    room = jnp.minimum(giver - 1, bound - sink)
    shifted = jax.random.randint(jax.random.fold_in(key, 1), (pairs,), 0, 1 << 20) % (room + 1)
    sizes = sizes.at[1:1 + 2 * pairs:2].set(giver - shifted).at[2:2 + 2 * pairs:2].set(sink + shifted)
    return sizes[jax.random.permutation(jax.random.fold_in(key, 2), amount)]


def gaussian(rng, shape, width, reach, shards=(), held_as=jnp.bfloat16):
    gain = shard_levels(rng, shape, shards, -0.22, 0.18) if shards else 1.0
    result = jax.random.normal(rng, shape, jnp.float32) * width * gain
    return jnp.minimum(jnp.maximum(result, -reach), reach).astype(held_as)


def setup_inputs(seed: int = 0) -> dict:
    seeds = jax.random.split(jax.random.key(seed), 8)
    queries = draw_queries(jax.random.fold_in(seeds[7], 71), 0)
    keys = draw_keys(jax.random.fold_in(seeds[7], 71), 0)
    values = gaussian(seeds[2], (CLIPS, TOKENS, HW), 4.0, 24.0, ((0, 4), (1, 128)))
    patch_ids = set_ends(jax.random.randint(seeds[3], (CLIPS, TOKENS), 0, FR * PATCHES), jax.random.fold_in(seeds[3], 1), 0, (FR * PATCHES) - 1).astype(jnp.int32)
    counts = jax.vmap(lambda own: uneven_parts(own, N_CTX, N_CTX * CAP // 2, CAP, 2))(jax.random.split(seeds[4], CLIPS)).reshape((CLIPS, N_CTX)).astype(jnp.int32)
    cotangent = gaussian(seeds[5], (CLIPS, TOKENS, D), 1.0, 6.0, ((0, 4), (1, 128)))
    w_out = gaussian(seeds[6], (HW, D), HW ** -0.5, 0.21875, ((0, 4),))
    return {"queries": queries, "keys": keys, "values": values, "patch_ids": patch_ids, "counts": counts, "cotangent": cotangent, "w_out": w_out}


masked_score = -1.0e30


def attend_block(query_block, key_block, value_block, query_frames, key_frames, key_live, query_live, cotangent_block, w_out):
    score_scale = HEAD ** -0.5
    query_heads = query_block.astype(jnp.float32).reshape(CAP, HEADS, HEAD)
    key_heads = key_block.astype(jnp.float32).reshape(-1, HEADS, HEAD)
    value_heads = value_block.astype(jnp.float32).reshape(-1, HEADS, HEAD)
    scores = jnp.einsum("qhd,khd->hqk", query_heads, key_heads) * score_scale
    allowed = (key_live[None, :] & (jnp.abs(query_frames[:, None] - key_frames[None, :]) <= WIN))[None]
    scores = jnp.where(allowed, scores, masked_score)
    row_max = jnp.max(scores, axis=2, keepdims=True)
    expon = jnp.where(allowed, jnp.exp(scores - row_max), 0.0)
    row_sum = jnp.sum(expon, axis=2, keepdims=True)
    attention = lax.optimization_barrier((expon / row_sum).astype(jnp.bfloat16))
    attention_wide = attention.astype(jnp.float32)
    context_heads = jnp.einsum("hqk,khd->qhd", attention_wide, value_heads).astype(jnp.bfloat16)
    context = context_heads.reshape(CAP, HW)
    grad_live = jnp.where(query_live[:, None], cotangent_block, jnp.zeros_like(cotangent_block))
    projected = jnp.dot(context, w_out, preferred_element_type=jnp.float32)
    attended = jnp.where(query_live[:, None], projected, 0.0).astype(jnp.bfloat16)
    grad_context = jnp.dot(grad_live, w_out.T, preferred_element_type=jnp.float32).astype(jnp.bfloat16)
    grad_heads = grad_context.astype(jnp.float32).reshape(CAP, HEADS, HEAD)
    row_delta = jnp.sum(grad_heads * context_heads.astype(jnp.float32), axis=2).T[:, :, None]
    grad_prob = jnp.einsum("qhd,khd->hqk", grad_heads, value_heads)
    grad_scores = lax.optimization_barrier((attention_wide * (grad_prob - row_delta)).astype(jnp.bfloat16))
    grad_scores = grad_scores.astype(jnp.float32)
    grad_query = (jnp.einsum("hqk,khd->qhd", grad_scores, key_heads) * score_scale).astype(jnp.bfloat16).reshape(CAP, HW)
    grad_key = (jnp.einsum("hqk,qhd->khd", grad_scores, query_heads) * score_scale).reshape(-1, HW)
    grad_value = jnp.einsum("hqk,qhd->khd", attention_wide, grad_heads).reshape(-1, HW)
    grad_weight = jnp.dot(context.T, grad_live, preferred_element_type=jnp.float32)
    return attended, grad_query, grad_key, grad_value, grad_weight


def one_clip(arrays, w_out):
    query_rows, key_rows, value_rows, patch_rows, count_row, cotangent_rows = arrays
    positions = jnp.arange(TOKENS, dtype=jnp.int32)
    shard = positions // CAP
    frames = shard * FR + patch_rows // PATCHES
    live = (positions % CAP) < count_row[shard]
    margin = SPAN * CAP
    extent = (2 * SPAN + 1) * CAP
    keys_padded = jnp.pad(key_rows, ((margin, margin), (0, 0)))
    values_padded = jnp.pad(value_rows, ((margin, margin), (0, 0)))
    frames_padded = jnp.pad(frames, (margin, margin))
    live_padded = jnp.pad(live, (margin, margin))

    def step(carry, shard_index):
        key_acc, value_acc, weight_acc = carry
        first = (shard_index * CAP).astype(jnp.int32)
        query_block = lax.dynamic_slice_in_dim(query_rows, first, CAP, 0)
        cotangent_block = lax.dynamic_slice_in_dim(cotangent_rows, first, CAP, 0)
        query_frames = lax.dynamic_slice_in_dim(frames, first, CAP, 0)
        query_live = lax.dynamic_slice_in_dim(live, first, CAP, 0)
        key_block = lax.dynamic_slice_in_dim(keys_padded, first, extent, 0)
        value_block = lax.dynamic_slice_in_dim(values_padded, first, extent, 0)
        key_frames = lax.dynamic_slice_in_dim(frames_padded, first, extent, 0)
        key_live = lax.dynamic_slice_in_dim(live_padded, first, extent, 0)
        attended, grad_query, grad_key, grad_value, grad_weight = attend_block(
            query_block, key_block, value_block, query_frames, key_frames, key_live, query_live, cotangent_block, w_out)
        key_acc = lax.dynamic_update_slice_in_dim(key_acc, lax.dynamic_slice_in_dim(key_acc, first, extent, 0) + grad_key, first, 0)
        value_acc = lax.dynamic_update_slice_in_dim(value_acc, lax.dynamic_slice_in_dim(value_acc, first, extent, 0) + grad_value, first, 0)
        return (key_acc, value_acc, weight_acc + grad_weight), (attended, grad_query)

    start = (jnp.zeros((TOKENS + 2 * margin, HW), jnp.float32), jnp.zeros((TOKENS + 2 * margin, HW), jnp.float32), jnp.zeros((HW, D), jnp.float32))
    carry, (attended, grad_query) = lax.scan(step, start, jnp.arange(N_CTX, dtype=jnp.int32))
    key_acc, value_acc, weight_acc = carry
    grad_keys = key_acc[margin:margin + TOKENS].astype(jnp.bfloat16)
    grad_values = value_acc[margin:margin + TOKENS].astype(jnp.bfloat16)
    return attended.reshape(TOKENS, D), grad_query.reshape(TOKENS, HW), grad_keys, grad_values, weight_acc


def reference(queries, keys, values, patch_ids, counts, cotangent, w_out):
    def per_clip(arrays):
        return one_clip(arrays, w_out)

    attended, grad_queries, grad_keys, grad_values, weights = lax.map(per_clip, (queries, keys, values, patch_ids, counts, cotangent))
    grad_w_out = jnp.sum(weights, axis=0)
    return attended, grad_queries, grad_keys, grad_values, grad_w_out
```

```python
import jax
import jax.numpy as jnp
from jax import lax
from jax.experimental import pallas as pl
from jax.experimental.pallas import tpu as pltpu
from jax.sharding import PartitionSpec as P

HEAD = 88
WIN = 4
ROWS = 128
HALF = 352
WIDE = 384
HW = 704
D = 1408
BLOCK = 176
SLOTS = 6
PLACES = 128
SCALE = HEAD ** -0.5
MASKED = -1e30
TILES = 121
MESH = pl.DeviceIdType.MESH
WINDOWS = ((0, 128), (0, 256), (128, 384), (256, 384))
BF = jnp.bfloat16
F32 = jnp.float32


def last_last(left, right):
    return lax.dot_general(left, right, (((1,), (1,)), ((), ())), preferred_element_type=F32)


def first_first(left, right):
    return lax.dot_general(left, right, (((0,), (0,)), ((), ())), preferred_element_type=F32)


def plain(left, right):
    return jnp.dot(left, right, preferred_element_type=F32)


def head_mask(head, rows):
    low, high = WINDOWS[head]
    lane = lax.broadcasted_iota(jnp.int32, (rows, high - low), 1) + low
    return jnp.where((lane >= HEAD * head) & (lane < HEAD * (head + 1)), 1.0, 0.0)


def kernel(q_ref, k_ref, v_ref, pid_ref, cnt_ref, cot_ref, w_ref,
           att_ref, gq_ref, gk_ref, gv_ref, gw_ref,
           kh, vh, qh, kw, vw, qw, gl, wf, bias, s_buf, probs, ds_buf,
           ctx_acc, cw, cf, ctb, ct, g_buf, dq_acc, dk_acc, dv_acc, dqw, dqf,
           dkb, dvb, rk, rv, dks, dvs, dkf, dvf,
           dw, ry, sx, rx, sz, rz, gf,
           k_rs, v_rs, q_rs, gl_rs, w_rs, c_rs, dq_rs, dk_rs, dv_rs, y_rs, x_rs, z_rs,
           ss, x_ss, z_ss):
    dp = lax.axis_index("dp")
    place = lax.axis_index("ctx")
    xh = lax.div(dp, 2)
    core = lax.rem(dp, 2)
    pair = lax.div(place, 2)
    xl = lax.rem(place, 2)
    y = lax.div(place, 32)
    z = lax.rem(pair, 16)
    spot = y * 2 + xl

    partner = (dp, place + 1 - 2 * xl)
    twin = (dp + 1 - 2 * core, place)
    other = lax.rem(dp + 2, 4)
    across = (other, place + 1 - 2 * xl)
    ahead = (dp, lax.rem(place + 2, PLACES))
    behind = (dp, lax.rem(place + PLACES - 2, PLACES))

    def around(j):
        where = lax.rem(spot + j, 8)
        return (dp, lax.div(where, 2) * 32 + z * 2 + lax.rem(where, 2))

    def along(j):
        return (dp, (y * 16 + lax.rem(z + j, 16)) * 2 + xl)

    barrier = pltpu.get_barrier_semaphore()
    for device in (twin, partner, across, (other, place), ahead, behind):
        pl.semaphore_signal(barrier, inc=1, device_id=device, device_id_type=MESH)

    def greet_around(j, carry):
        pl.semaphore_signal(barrier, inc=1, device_id=around(j), device_id_type=MESH)
        return carry

    def greet_along(j, carry):
        pl.semaphore_signal(barrier, inc=1, device_id=along(j), device_id_type=MESH)
        return carry

    lax.fori_loop(1, 8, greet_around, 0)
    lax.fori_loop(1, 16, greet_along, 0)

    pad = jnp.zeros((ROWS, 128), BF)
    for source, halves in ((k_ref, kh), (v_ref, vh), (q_ref, qh)):
        for half in range(2):
            halves[half, :, 256:384] = pad
            halves[half, :, 0:HALF] = source[:, half * HALF:(half + 1) * HALF]
    kw[2 + xl] = kh[xl]
    vw[2 + xl] = vh[xl]
    qw[xl] = qh[xl]

    own_live = lax.broadcasted_iota(jnp.int32, (ROWS, 128), 0) < cnt_ref[0, place]
    mine = core * 2 + xl
    for block in range(11):
        cols = slice(block * 128, (block + 1) * 128)
        gl[mine, :, cols] = jnp.where(own_live, cot_ref[:, cols].astype(F32), 0.0).astype(BF)

    pl.semaphore_wait(barrier, 28)

    sent = []

    def send(source, target, recv_sem, device):
        copy = pltpu.make_async_remote_copy(
            src_ref=source, dst_ref=target, send_sem=ss.at[len(sent)], recv_sem=recv_sem,
            device_id=device, device_id_type=MESH)
        copy.start()
        sent.append(copy)

    def arrived(ref, recv_sem):
        pltpu.make_async_remote_copy(
            src_ref=ref, dst_ref=ref, send_sem=ss.at[0], recv_sem=recv_sem,
            device_id=partner, device_id_type=MESH).wait_recv()

    far = 3 - xl
    send(kh.at[1 - xl], kw.at[2 + xl], k_rs.at[2 + xl], partner)
    send(kh.at[xl], kw.at[xl], k_rs.at[xl], ahead)
    send(kh.at[xl], kw.at[4 + xl], k_rs.at[4 + xl], behind)
    send(qh.at[1 - xl], qw.at[xl], q_rs, partner)
    send(vh.at[1 - xl], vw.at[2 + xl], v_rs.at[2 + xl], partner)
    send(w_ref, wf.at[dp], w_rs.at[dp], across)
    send(w_ref, wf.at[dp], w_rs.at[dp], twin)
    send(gl.at[mine], gl.at[mine], gl_rs.at[mine], twin)
    wf[dp] = w_ref[...]

    key_frames = []
    for slot in range(SLOTS):
        shard = lax.rem(2 * pair - 2 + slot + PLACES, PLACES)
        inside = (2 * pair - 2 + slot >= 0) & (2 * pair - 2 + slot < PLACES)
        count = jnp.where(inside, cnt_ref[0, shard], 0)
        frame = lax.shift_right_logical(pid_ref[pl.ds(shard, 1), :], 8) + 2 * (slot - 2)
        key_frames.append((frame, count))
    for slot, (frame, count) in enumerate(key_frames):
        column = jnp.transpose(jnp.broadcast_to(frame.astype(F32), (ROWS, 128)))
        alive = lax.broadcasted_iota(jnp.int32, (ROWS, 128), 0) < count
        for half in range(2):
            row = key_frames[2 + half][0].astype(F32)
            seen = alive & (jnp.abs(row - column) <= WIN)
            bias[slot, :, half * 128:(half + 1) * 128] = jnp.where(seen, 0.0, MASKED)

    arrived(kw.at[far], k_rs.at[far])
    send(kw.at[far], kw.at[1 - xl], k_rs.at[1 - xl], ahead)
    send(kw.at[far], kw.at[5 - xl], k_rs.at[5 - xl], behind)
    send(vh.at[xl], vw.at[xl], v_rs.at[xl], ahead)
    send(vh.at[xl], vw.at[4 + xl], v_rs.at[4 + xl], behind)
    arrived(qw.at[1 - xl], q_rs)
    arrived(vw.at[far], v_rs.at[far])
    send(vw.at[far], vw.at[1 - xl], v_rs.at[1 - xl], ahead)
    send(vw.at[far], vw.at[5 - xl], v_rs.at[5 - xl], behind)
    send(gl.at[mine], gl.at[mine], gl_rs.at[mine], partner)
    for slot in (0, 1, 4, 5):
        arrived(kw.at[slot], k_rs.at[slot])

    def add_to(ref, head, value, seen):
        low, high = WINDOWS[head]
        for start in range(low, high, 128):
            part = value[:, start - low:start - low + 128]
            if start in seen:
                ref[:, start:start + 128] += part
            else:
                ref[:, start:start + 128] = part
                seen.add(start)

    seen = set()
    for head in range(4):
        low, high = WINDOWS[head]
        q_head = qw[:, :, low:high].reshape(256, high - low) * head_mask(head, 256).astype(BF)
        top = None
        for slot in range(SLOTS):
            score = last_last(kw[slot, :, low:high], q_head) * SCALE + bias[slot]
            s_buf[slot] = score
            high_here = jnp.max(score, axis=0, keepdims=True)
            top = high_here if top is None else jnp.maximum(top, high_here)
        total = None
        for slot in range(SLOTS):
            expon = jnp.exp(s_buf[slot] - top)
            s_buf[slot] = expon
            here = jnp.sum(expon, axis=0, keepdims=True)
            total = here if total is None else total + here
        inverse = 1.0 / total
        for slot in range(SLOTS):
            probs[head, slot] = (s_buf[slot] * inverse).astype(BF)
        if head == 0:
            for slot in (0, 1, 4, 5):
                arrived(vw.at[slot], v_rs.at[slot])
        part = first_first(probs[head].reshape(768, 256), vw[:, :, low:high].reshape(768, high - low))
        add_to(ctx_acc, head, part * head_mask(head, 256), seen)
    context = ctx_acc[...].astype(BF)
    ctb[0] = context[:, 0:BLOCK]
    ctb[1] = context[:, BLOCK:HALF]
    send(ctb.at[1 - core], ct.at[core], c_rs.at[0], twin)
    cw[...] = context.reshape(2, ROWS, WIDE)
    send(cw.at[1 - xl], cf.at[xl], c_rs.at[1], partner)
    ct[core] = ctb[core]
    cf[xl] = cw[xl]

    arrived(wf.at[other], w_rs.at[other])
    send(wf.at[other], wf.at[other], w_rs.at[other], twin)
    theirs = core * 2 + 1 - xl
    arrived(gl.at[theirs], gl_rs.at[theirs])
    send(gl.at[theirs], gl.at[theirs], gl_rs.at[theirs], twin)
    arrived(wf.at[dp + 1 - 2 * core], w_rs.at[dp + 1 - 2 * core])
    arrived(wf.at[other + 1 - 2 * core], w_rs.at[other + 1 - 2 * core])
    grad_context = last_last(gl[pl.ds(core * 2, 2)].reshape(256, D), wf[pl.ds(xl * 2, 2)].reshape(HALF, D))
    g_buf[:, 256:384] = jnp.zeros((256, 128), BF)
    g_buf[:, 0:HALF] = grad_context.astype(BF)

    arrived(ct.at[1 - core], c_rs.at[0])
    for slot in range(2):
        there = (1 - core) * 2 + slot
        arrived(gl.at[there], gl_rs.at[there])
    turned = jnp.transpose(ct[...].reshape(512, BLOCK).astype(F32)).astype(BF)
    for start in range(0, D, 256):
        stop = min(start + 256, D)
        part = plain(turned, gl[:, :, start:stop].reshape(512, stop - start))
        for column in range(start, stop, 128):
            for row in range(11):
                tile = row * 11 + column // 128
                dw[tile // 32, tile % 32] = part[row * 16:row * 16 + 16, column - start:column - start + 128].astype(BF)
    for tile in range(TILES, 128):
        dw[tile // 32, tile % 32] = jnp.zeros((16, 128), BF)
    for step in (1, 3, 2):
        goal = lax.rem(y + step, 4)
        send(dw.at[goal], ry.at[step - 1], y_rs.at[step - 1], (dp, lax.rem(place + 32 * step, PLACES)))

    seen_q, seen_k, seen_v = set(), set(), set()
    for head in range(4):
        low, high = WINDOWS[head]
        mask = head_mask(head, 256)
        q_head = qw[:, :, low:high].reshape(256, high - low) * mask.astype(BF)
        g_head = g_buf[:, low:high] * mask.astype(BF)
        delta = None
        for slot in range(SLOTS):
            grad_prob = last_last(vw[slot, :, low:high], g_head)
            s_buf[slot] = grad_prob
            here = jnp.sum(probs[head, slot].astype(F32) * grad_prob, axis=0, keepdims=True)
            delta = here if delta is None else delta + here
        for slot in range(SLOTS):
            ds_buf[slot] = (probs[head, slot].astype(F32) * (s_buf[slot] - delta)).astype(BF)
        grad_scores = ds_buf[...].reshape(768, 256)
        part = first_first(grad_scores, kw[:, :, low:high].reshape(768, high - low))
        add_to(dq_acc, head, part * mask, seen_q)
        add_to(dk_acc, head, plain(grad_scores, q_head), seen_k)
        add_to(dv_acc, head, plain(probs[head].reshape(768, 256), g_head), seen_v)
    dkb[...] = (dk_acc[...] * SCALE).astype(BF).reshape(SLOTS, ROWS, WIDE)
    send(dkb.at[pl.ds(0, 2)], rk.at[1], dk_rs.at[1], behind)
    send(dkb.at[pl.ds(4, 2)], rk.at[0], dk_rs.at[0], ahead)
    dvb[...] = dv_acc[...].astype(BF).reshape(SLOTS, ROWS, WIDE)
    send(dvb.at[pl.ds(0, 2)], rv.at[1], dv_rs.at[1], behind)
    send(dvb.at[pl.ds(4, 2)], rv.at[0], dv_rs.at[0], ahead)
    dqw[...] = (dq_acc[...] * SCALE).astype(BF).reshape(2, ROWS, WIDE)
    send(dqw.at[1 - xl], dqf.at[xl], dq_rs, partner)
    dqf[xl] = dqw[xl]

    for step in range(3):
        arrived(ry.at[step], y_rs.at[step])
    total = dw[y].astype(F32) + ry[0].astype(F32) + ry[1].astype(F32) + ry[2].astype(F32)
    sx[...] = total.astype(BF).reshape(2, 16, 16, 128)

    def x_copy(half):
        return pltpu.make_async_remote_copy(
            src_ref=sx.at[half], dst_ref=rx.at[xh], send_sem=x_ss.at[half], recv_sem=x_rs.at[xh],
            device_id=(2 * xl + core, 2 * pair + half), device_id_type=MESH)

    for half in range(2):
        stays = (xh == xl) & (xl == half)

        @pl.when(stays)
        def _():
            rx[xh] = sx[half]

        @pl.when(jnp.logical_not(stays))
        def _():
            x_copy(half).start()

    arrived(cf.at[1 - xl], c_rs.at[1])
    projected = plain(cf[0][:, 0:HALF], wf[pl.ds(0, 2)].reshape(HALF, D))
    projected = projected + plain(cf[1][:, 0:HALF], wf[pl.ds(2, 2)].reshape(HALF, D))
    for block in range(11):
        cols = slice(block * 128, (block + 1) * 128)
        att_ref[:, cols] = jnp.where(own_live, projected[:, cols], 0.0).astype(BF)

    for source in range(2):
        @pl.when(jnp.logical_not((xh == xl) & (xh == source)))
        def _():
            arrived(rx.at[source], x_rs.at[source])

    sz[...] = (rx[0].astype(F32) + rx[1].astype(F32)).astype(BF)

    def scatter(j, carry):
        pltpu.make_async_remote_copy(
            src_ref=sz.at[lax.rem(z + j, 16)], dst_ref=rz.at[j - 1], send_sem=z_ss.at[0], recv_sem=z_rs.at[0],
            device_id=along(j), device_id_type=MESH).start()
        return carry

    lax.fori_loop(1, 16, scatter, 0)

    def gather_grad(terms, near, near_sems, summed, full, acc, scale, sem):
        arrived(near.at[0], near_sems.at[0])
        arrived(near.at[1], near_sems.at[1])
        value = acc[256:512, :].reshape(2, ROWS, WIDE) * scale + near[0].astype(F32) + near[1].astype(F32)
        summed[...] = value.astype(BF)
        send(summed.at[1 - xl], full.at[xl], sem, partner)
        full[xl] = summed[xl]

    def many(sem, ref, send_sem):
        return pltpu.make_async_remote_copy(
            src_ref=ref, dst_ref=ref, send_sem=send_sem, recv_sem=sem, device_id=partner, device_id_type=MESH)

    many(z_rs.at[0], rz, z_ss.at[0]).wait_recv()
    total = sz[z].astype(F32)
    for step in range(15):
        total = total + rz[step].astype(F32)
    gf[spot, z] = total.astype(BF)

    def spread(j, carry):
        pltpu.make_async_remote_copy(
            src_ref=gf.at[spot, z], dst_ref=gf.at[spot, z], send_sem=z_ss.at[1], recv_sem=z_rs.at[1],
            device_id=along(j), device_id_type=MESH).start()
        return carry

    lax.fori_loop(1, 16, spread, 0)

    gather_grad(dkb, rk, dk_rs, dks, dkf, dk_acc, SCALE, dk_rs.at[2])
    gather_grad(dvb, rv, dv_rs, dvs, dvf, dv_acc, 1.0, dv_rs.at[2])

    many(z_rs.at[1], rz, z_ss.at[1]).wait_recv()

    def share(j, carry):
        pltpu.make_async_remote_copy(
            src_ref=gf.at[spot], dst_ref=gf.at[spot], send_sem=z_ss.at[2], recv_sem=z_rs.at[2],
            device_id=around(j), device_id_type=MESH).start()
        return carry

    lax.fori_loop(1, 8, share, 0)

    for full, sem, out in ((dqf, dq_rs, gq_ref), (dkf, dk_rs.at[2], gk_ref), (dvf, dv_rs.at[2], gv_ref)):
        arrived(full.at[1 - xl], sem)
        for half in range(2):
            out[:, half * HALF:(half + 1) * HALF] = full[half, :, 0:HALF]

    many(z_rs.at[2], gf.at[pl.ds(0, 7)], z_ss.at[2]).wait_recv()
    for tile in range(TILES):
        row, column = tile // 11, tile % 11
        gw_ref[row * 16:row * 16 + 16, column * 128:(column + 1) * 128] = gf[tile // 16, tile % 16].astype(F32)

    for copy in sent:
        copy.wait_send()
    for half in range(2):
        @pl.when(jnp.logical_not((xh == xl) & (xl == half)))
        def _():
            x_copy(half).wait_send()
    many(z_rs.at[0], rz, z_ss.at[0]).wait_send()
    many(z_rs.at[1], rz, z_ss.at[1]).wait_send()
    many(z_rs.at[2], gf.at[pl.ds(0, 7)], z_ss.at[2]).wait_send()


def per_device(queries, keys, values, patch_ids, counts, cotangent, w_out):
    vmem = pl.BlockSpec(memory_space=pltpu.VMEM)
    smem = pl.BlockSpec(memory_space=pltpu.SMEM)
    pair_rows = (2, ROWS, WIDE)
    window = (SLOTS, ROWS, WIDE)
    dma = pltpu.SemaphoreType.DMA
    scratch = [
        pltpu.VMEM(pair_rows, BF), pltpu.VMEM(pair_rows, BF), pltpu.VMEM(pair_rows, BF),
        pltpu.VMEM(window, BF), pltpu.VMEM(window, BF), pltpu.VMEM(pair_rows, BF),
        pltpu.VMEM((4, ROWS, D), BF), pltpu.VMEM((4, BLOCK, D), BF),
        pltpu.VMEM((SLOTS, ROWS, 256), F32), pltpu.VMEM((SLOTS, ROWS, 256), F32),
        pltpu.VMEM((4, SLOTS, ROWS, 256), BF), pltpu.VMEM((SLOTS, ROWS, 256), BF),
        pltpu.VMEM((256, WIDE), F32), pltpu.VMEM(pair_rows, BF), pltpu.VMEM(pair_rows, BF),
        pltpu.VMEM((2, 256, BLOCK), BF), pltpu.VMEM((2, 256, BLOCK), BF), pltpu.VMEM((256, WIDE), BF),
        pltpu.VMEM((256, WIDE), F32), pltpu.VMEM((768, WIDE), F32), pltpu.VMEM((768, WIDE), F32),
        pltpu.VMEM(pair_rows, BF), pltpu.VMEM(pair_rows, BF),
        pltpu.VMEM(window, BF), pltpu.VMEM(window, BF),
        pltpu.VMEM((2,) + pair_rows, BF), pltpu.VMEM((2,) + pair_rows, BF),
        pltpu.VMEM(pair_rows, BF), pltpu.VMEM(pair_rows, BF), pltpu.VMEM(pair_rows, BF), pltpu.VMEM(pair_rows, BF),
        pltpu.VMEM((4, 32, 16, 128), BF), pltpu.VMEM((3, 32, 16, 128), BF),
        pltpu.VMEM((2, 16, 16, 128), BF), pltpu.VMEM((2, 16, 16, 128), BF),
        pltpu.VMEM((16, 16, 128), BF), pltpu.VMEM((15, 16, 128), BF), pltpu.VMEM((8, 16, 16, 128), BF),
        dma((6,)), dma((6,)), dma, dma((4,)), dma((4,)), dma((2,)), dma, dma((3,)), dma((3,)), dma((3,)),
        dma((2,)), dma((3,)),
        dma((32,)), dma((2,)), dma((3,)),
    ]
    outs = pl.pallas_call(
        kernel,
        out_shape=(
            jax.ShapeDtypeStruct((ROWS, D), BF),
            jax.ShapeDtypeStruct((ROWS, HW), BF),
            jax.ShapeDtypeStruct((ROWS, HW), BF),
            jax.ShapeDtypeStruct((ROWS, HW), BF),
            jax.ShapeDtypeStruct((BLOCK, D), F32),
        ),
        in_specs=[vmem, vmem, vmem, vmem, smem, vmem, vmem],
        out_specs=(vmem,) * 5,
        scratch_shapes=scratch,
        compiler_params=pltpu.CompilerParams(
            collective_id=0, has_side_effects=True, vmem_limit_bytes=48 * 1024 * 1024),
        cost_estimate=pl.CostEstimate(flops=1500000000, bytes_accessed=4000000, transcendentals=800000),
    )(queries[0], keys[0], values[0], patch_ids.reshape(PLACES, ROWS), counts, cotangent[0], w_out)
    attended, grad_queries, grad_keys, grad_values, grad_weight = outs
    return attended[None], grad_queries[None], grad_keys[None], grad_values[None], grad_weight


def solution(mesh):
    placed = (
        P("dp", "ctx", None),
        P("dp", "ctx", None),
        P("dp", "ctx", None),
        P("dp", None),
        P("dp", None),
        P("dp", "ctx", None),
        P("dp", None),
    )
    return jax.shard_map(
        per_device,
        mesh=mesh,
        in_specs=placed,
        out_specs=(
            P("dp", "ctx", None),
            P("dp", "ctx", None),
            P("dp", "ctx", None),
            P("dp", "ctx", None),
            P("dp", None),
        ),
        check_vma=False,
    )
```

```python
import jax
import jax.numpy as jnp
from jax import lax
from jax.experimental import pallas as pl
from jax.experimental.pallas import tpu as pltpu
from jax.sharding import PartitionSpec as P

HEAD = 88
WIN = 4
ROWS = 128
HALF = 352
HW = 704
D = 1408
BLOCK = 176
SLOTS = 6
PLACES = 128
SCALE = HEAD ** -0.5
MASKED = -1e30
TILES = 121
MESH = pl.DeviceIdType.MESH
WINDOWS = ((0, 128), (0, 256), (128, 352), (256, 352))
STRIPES = ((0, 96), (80, 176), (176, 272), (256, 352))
BF = jnp.bfloat16
F32 = jnp.float32


def last_last(left, right):
    return lax.dot_general(left, right, (((1,), (1,)), ((), ())), preferred_element_type=F32)


def first_first(left, right):
    return lax.dot_general(left, right, (((0,), (0,)), ((), ())), preferred_element_type=F32)


def plain(left, right):
    return jnp.dot(left, right, preferred_element_type=F32)


def head_mask(head, rows):
    low, high = WINDOWS[head]
    lane = lax.broadcasted_iota(jnp.int32, (rows, high - low), 1) + low
    return jnp.where((lane >= HEAD * head) & (lane < HEAD * (head + 1)), 1.0, 0.0)


def stripe(head, value):
    skip = HEAD * head - STRIPES[head][0]
    return value[skip:skip + HEAD]


def kernel(q_ref, k_ref, v_ref, pid_ref, cnt_ref, cot_ref, w_ref,
           att_ref, gq_ref, gk_ref, gv_ref, gw_ref,
           kw, vw, qw, qn, gl, wf, bias, s_buf, probs, ds_buf,
           ctx_acc, cb, cw, cf, ct, g_buf, gt_buf, dq_acc, dk_acc, dv_acc, dqw, dqf,
           kvb, rkv, kvs, kvf,
           dw, ry, sx, rx, fr, gf,
           k_rs, v_rs, q_rs, gl_rs, w_rs, c_rs, dq_rs, kv_rs, kvf_rs, y_rs, x_rs, f_rs, z_rs,
           ss, x_ss, z_ss):
    dp = lax.axis_index("dp")
    place = lax.axis_index("ctx")
    xh = lax.div(dp, 2)
    core = lax.rem(dp, 2)
    pair = lax.div(place, 2)
    xl = lax.rem(place, 2)
    y = lax.div(place, 32)
    z = lax.rem(pair, 16)
    group = lax.div(z, 4)
    inner = lax.rem(z, 4)
    spot = y * 2 + xl

    partner = (dp, place + 1 - 2 * xl)
    twin = (dp + 1 - 2 * core, place)
    other = lax.rem(dp + 2, 4)
    across = (other, place + 1 - 2 * xl)
    ahead = (dp, lax.rem(place + 2, PLACES))
    behind = (dp, lax.rem(place + PLACES - 2, PLACES))

    def around(j):
        where = lax.rem(spot + j, 8)
        return (dp, lax.div(where, 2) * 32 + z * 2 + lax.rem(where, 2))

    def quad(x, b):
        return (lax.div(x, 2) * 2 + core, (y * 16 + group * 4 + b) * 2 + lax.rem(x, 2))

    def far(j):
        return (dp, (y * 16 + lax.rem(z + 4 * j, 16)) * 2 + xl)

    barrier = pltpu.get_barrier_semaphore()

    def greet(device):
        pl.semaphore_signal(barrier, inc=1, device_id=device, device_id_type=MESH)

    def greet_quad(j, carry):
        at = lax.rem((xh * 2 + xl) * 4 + inner + j, 16)
        greet(quad(lax.div(at, 4), lax.rem(at, 4)))
        return carry

    def greet_around(j, carry):
        greet(around(j))
        return carry

    def greet_far(j, carry):
        greet(far(j))
        return carry

    for device in (ahead, behind, twin):
        greet(device)
    lax.fori_loop(1, 4, greet_far, 0)
    lax.fori_loop(1, 16, greet_quad, 0)
    lax.fori_loop(1, 8, greet_around, 0)

    own_live = lax.broadcasted_iota(jnp.int32, (ROWS, 128), 0) < cnt_ref[0, place]
    mine = core * 2 + xl
    for block in range(11):
        cols = slice(block * 128, (block + 1) * 128)
        gl[mine, :, cols] = jnp.where(own_live, cot_ref[:, cols].astype(F32), 0.0).astype(BF)

    pl.semaphore_wait(barrier, 28)

    sent = []

    def send(source, target, recv_sem, device):
        copy = pltpu.make_async_remote_copy(
            src_ref=source, dst_ref=target, send_sem=ss.at[len(sent)], recv_sem=recv_sem,
            device_id=device, device_id_type=MESH)
        copy.start()
        sent.append(copy)

    def incoming(ref, recv_sem, send_sem):
        return pltpu.make_async_remote_copy(
            src_ref=ref, dst_ref=ref, send_sem=send_sem, recv_sem=recv_sem,
            device_id=partner, device_id_type=MESH)

    def arrived(ref, recv_sem):
        incoming(ref, recv_sem, ss.at[0]).wait_recv()

    away = 3 - xl
    near_rows = pl.ds(pl.multiple_of(xl * HALF, 16), HALF)
    away_rows = pl.ds(pl.multiple_of((1 - xl) * HALF, 16), HALF)
    send(k_ref.at[away_rows], kw.at[2 + xl], k_rs.at[2 + xl], partner)
    send(k_ref.at[near_rows], kw.at[xl], k_rs.at[xl], ahead)
    send(k_ref.at[near_rows], kw.at[4 + xl], k_rs.at[4 + xl], behind)
    send(v_ref.at[away_rows], vw.at[2 + xl], v_rs.at[2 + xl], partner)
    send(q_ref.at[away_rows], qw.at[xl], q_rs, partner)
    send(gl.at[mine], gl.at[mine], gl_rs.at[mine], partner)
    send(w_ref, wf.at[dp], w_rs.at[dp], across)
    send(w_ref, wf.at[dp], w_rs.at[dp], twin)
    send(gl.at[mine], gl.at[mine], gl_rs.at[mine], twin)
    kw[2 + xl] = k_ref[near_rows, :]
    vw[2 + xl] = v_ref[near_rows, :]
    qw[xl] = q_ref[near_rows, :]

    arrived(kw.at[away], k_rs.at[away])
    send(kw.at[away], kw.at[1 - xl], k_rs.at[1 - xl], ahead)
    send(kw.at[away], kw.at[5 - xl], k_rs.at[5 - xl], behind)
    send(v_ref.at[near_rows], vw.at[xl], v_rs.at[xl], ahead)
    send(v_ref.at[near_rows], vw.at[4 + xl], v_rs.at[4 + xl], behind)
    arrived(vw.at[away], v_rs.at[away])
    send(vw.at[away], vw.at[1 - xl], v_rs.at[1 - xl], ahead)
    send(vw.at[away], vw.at[5 - xl], v_rs.at[5 - xl], behind)

    frames, live = [], []
    for slot in range(SLOTS):
        shard = lax.rem(2 * pair - 2 + slot + PLACES, PLACES)
        inside = (2 * pair - 2 + slot >= 0) & (2 * pair - 2 + slot < PLACES)
        count = jnp.where(inside, cnt_ref[0, shard], 0)
        frame = lax.shift_right_logical(pid_ref[pl.ds(shard, 1), :], 8) + 2 * (slot - 2)
        frames.append(frame.astype(F32))
        live.append(lax.broadcasted_iota(jnp.int32, (ROWS, 128), 1) < count)
    for half in range(2):
        column = jnp.transpose(jnp.broadcast_to(frames[2 + half], (ROWS, 128)))
        for slot in range(SLOTS):
            seen = live[slot] & (jnp.abs(frames[slot] - column) <= WIN)
            bias[half * 128:(half + 1) * 128, slot * 128:(slot + 1) * 128] = jnp.where(seen, 0.0, MASKED)
    wf[dp] = w_ref[...]

    arrived(qw.at[1 - xl], q_rs)
    for half in range(2):
        qn[half * 128:(half + 1) * 128, :] = jnp.transpose(qw[half].astype(F32)).astype(BF)
    for slot in (0, 1, 4, 5):
        arrived(kw.at[slot], k_rs.at[slot])

    def lanes(ref, low, high, first, slots):
        return jnp.concatenate([ref[first + i, low:high, :] for i in range(slots)], axis=1)

    def folded(op, value, old):
        here = op(value[:, :128], value[:, 128:])
        return here if old is None else op(old, here)

    for head in range(4):
        low, high = WINDOWS[head]
        q_head = qn[:, low:high] * head_mask(head, 256).astype(BF)
        top = None
        for part in range(3):
            cols = slice(part * 256, part * 256 + 256)
            score = plain(q_head, lanes(kw, low, high, part * 2, 2)) * SCALE + bias[:, cols]
            s_buf[:, cols] = score
            top = folded(jnp.maximum, score, top)
        top = jnp.max(top, axis=1, keepdims=True)
        total = None
        for part in range(3):
            cols = slice(part * 256, part * 256 + 256)
            expon = jnp.exp(s_buf[:, cols] - top)
            s_buf[:, cols] = expon
            total = folded(jnp.add, expon, total)
        inverse = 1.0 / jnp.sum(total, axis=1, keepdims=True)
        for part in range(3):
            cols = slice(part * 256, part * 256 + 256)
            probs[head, :, cols] = (s_buf[:, cols] * inverse).astype(BF)
        if head == 0:
            for slot in (0, 1, 4, 5):
                arrived(vw.at[slot], v_rs.at[slot])
        ctx_acc[head * HEAD:(head + 1) * HEAD, :] = stripe(
            head, last_last(lanes(vw, *STRIPES[head], 0, SLOTS), probs[head]))
    cb[...] = ctx_acc[...].astype(BF)
    core_rows = pl.ds(pl.multiple_of(core * BLOCK, 16), BLOCK)
    send(cb.at[pl.ds(pl.multiple_of((1 - core) * BLOCK, 16), BLOCK)], ct.at[core], c_rs.at[0], twin)
    cw[0] = cb[:, 0:128]
    cw[1] = cb[:, 128:256]
    send(cw.at[1 - xl], cf.at[near_rows], c_rs.at[1], partner)
    ct[core] = cb[core_rows, :]
    cf[near_rows, :] = cw[xl]

    theirs = core * 2 + 1 - xl
    arrived(gl.at[theirs], gl_rs.at[theirs])
    send(gl.at[theirs], gl.at[theirs], gl_rs.at[theirs], twin)
    arrived(wf.at[other], w_rs.at[other])
    send(wf.at[other], wf.at[other], w_rs.at[other], twin)
    arrived(wf.at[dp + 1 - 2 * core], w_rs.at[dp + 1 - 2 * core])
    arrived(wf.at[other + 1 - 2 * core], w_rs.at[other + 1 - 2 * core])
    grad_context = last_last(gl[pl.ds(core * 2, 2)].reshape(256, D), wf[pl.ds(xl * 2, 2)].reshape(HALF, D))
    g_buf[...] = grad_context.astype(BF)
    gt_buf[...] = jnp.transpose(grad_context).astype(BF)

    arrived(ct.at[1 - core], c_rs.at[0])
    for slot in range(2):
        there = (1 - core) * 2 + slot
        arrived(gl.at[there], gl_rs.at[there])
    context = jnp.concatenate([ct[0], ct[1]], axis=1)
    for start in range(0, D, 256):
        stop = min(start + 256, D)
        part = plain(context, gl[:, :, start:stop].reshape(512, stop - start))
        for column in range(start, stop, 128):
            for row in range(11):
                tile = row * 11 + column // 128
                dw[tile // 32, tile % 32] = part[row * 16:row * 16 + 16, column - start:column - start + 128].astype(BF)
    for tile in range(TILES, 128):
        dw[tile // 32, tile % 32] = jnp.zeros((16, 128), BF)
    for step in (1, 3, 2):
        goal = lax.rem(y + step, 4)
        send(dw.at[goal], ry.at[step - 1], y_rs.at[step - 1], (dp, lax.rem(place + 32 * step, PLACES)))

    for head in range(4):
        low, high = WINDOWS[head]
        g_head = g_buf[:, low:high] * head_mask(head, 256).astype(BF)
        delta = None
        for part in range(3):
            cols = slice(part * 256, part * 256 + 256)
            grad_prob = plain(g_head, lanes(vw, low, high, part * 2, 2))
            s_buf[:, cols] = grad_prob
            delta = folded(jnp.add, probs[head, :, cols].astype(F32) * grad_prob, delta)
        delta = jnp.sum(delta, axis=1, keepdims=True)
        for part in range(3):
            cols = slice(part * 256, part * 256 + 256)
            ds_buf[:, cols] = (probs[head, :, cols].astype(F32) * (s_buf[:, cols] - delta)).astype(BF)
        rows = slice(head * HEAD, (head + 1) * HEAD)
        first, stop = STRIPES[head]
        dk_acc[rows, :] = stripe(head, plain(lanes(qw, first, stop, 0, 2), ds_buf[...])) * SCALE
        dv_acc[rows, :] = stripe(head, plain(gt_buf[first:stop, :], probs[head]))
        dq_acc[rows, :] = stripe(head, last_last(lanes(kw, first, stop, 0, SLOTS), ds_buf[...])) * SCALE
        if head % 2 == 1:
            piece = head // 2
            block = slice(piece * BLOCK, (piece + 1) * BLOCK)
            for side in range(2):
                cols = slice(side * 512, side * 512 + 256)
                kvb[side, piece, 0] = dk_acc[block, cols].astype(BF)
                kvb[side, piece, 1] = dv_acc[block, cols].astype(BF)
                send(kvb.at[side, piece], rkv.at[1 - side, piece], kv_rs.at[1 - side, piece], (behind, ahead)[side])
    dqw[0] = dq_acc[:, 0:128].astype(BF)
    dqw[1] = dq_acc[:, 128:256].astype(BF)
    send(dqw.at[1 - xl], dqf, dq_rs, partner)
    gq_ref[near_rows, :] = dqw[xl]

    for step in range(3):
        arrived(ry.at[step], y_rs.at[step])
    total = dw[y].astype(F32) + ry[0].astype(F32) + ry[1].astype(F32) + ry[2].astype(F32)
    sx[...] = total.astype(BF).reshape(8, 4, 16, 128)

    def stays(half, b):
        return (xh == xl) & (xl == half) & (inner == b)

    def quad_copy(n):
        half, b = lax.div(n, 4), lax.rem(n, 4)
        return pltpu.make_async_remote_copy(
            src_ref=sx.at[n], dst_ref=rx.at[xh * 4 + inner], send_sem=x_ss.at[n], recv_sem=x_rs.at[xh * 4 + inner],
            device_id=quad(xl * 2 + half, b), device_id_type=MESH)

    def quad_start(n, carry):
        @pl.when(jnp.logical_not(stays(lax.div(n, 4), lax.rem(n, 4))))
        def _():
            quad_copy(n).start()

        return carry

    def quad_sent(n, carry):
        @pl.when(jnp.logical_not(stays(lax.div(n, 4), lax.rem(n, 4))))
        def _():
            quad_copy(n).wait_send()

        return carry

    def quad_here(n, carry):
        @pl.when(jnp.logical_not((xh == xl) & (n == xh * 4 + inner)))
        def _():
            arrived(rx.at[n], x_rs.at[n])

        return carry

    lax.fori_loop(0, 8, quad_start, 0)

    @pl.when(xh == xl)
    def _():
        rx[xh * 4 + inner] = sx[xl * 4 + inner]

    arrived(cf.at[away_rows], c_rs.at[1])
    projected = first_first(cf[...], wf[...].reshape(HW, D))
    for block in range(11):
        cols = slice(block * 128, (block + 1) * 128)
        att_ref[:, cols] = jnp.where(own_live, projected[:, cols], 0.0).astype(BF)

    lax.fori_loop(0, 8, quad_here, 0)
    total = rx[0].astype(F32)
    for source in range(1, 8):
        total = total + rx[source].astype(F32)
    fr[group] = total.astype(BF)
    for step in (2, 1, 3):
        send(fr.at[group], fr.at[group], f_rs.at[group], far(step))

    for piece in range(2):
        block = slice(piece * BLOCK, (piece + 1) * BLOCK)
        for side in range(2):
            arrived(rkv.at[side, piece], kv_rs.at[side, piece])
        for which, acc in ((0, dk_acc), (1, dv_acc)):
            value = acc[block, 256:512] + rkv[0, piece, which].astype(F32) + rkv[1, piece, which].astype(F32)
            kvs[0, which, block, :] = value[:, 0:128].astype(BF)
            kvs[1, which, block, :] = value[:, 128:256].astype(BF)
    send(kvs.at[1 - xl], kvf, kvf_rs, partner)
    gk_ref[near_rows, :] = kvs[xl, 0]
    gv_ref[near_rows, :] = kvs[xl, 1]
    arrived(dqf, dq_rs)
    gq_ref[away_rows, :] = dqf[...]

    for step in range(1, 4):
        source = lax.rem(group + step, 4)
        arrived(fr.at[source], f_rs.at[source])
    total = fr[0].astype(F32) + fr[1].astype(F32) + fr[2].astype(F32) + fr[3].astype(F32)
    gf[spot, inner] = total.astype(BF)

    def spread(j, carry):
        pltpu.make_async_remote_copy(
            src_ref=gf.at[spot, inner], dst_ref=gf.at[spot, inner], send_sem=z_ss.at[0], recv_sem=z_rs.at[0],
            device_id=quad(xh * 2 + xl, lax.rem(inner + j, 4)), device_id_type=MESH).start()
        return carry

    def share(j, carry):
        pltpu.make_async_remote_copy(
            src_ref=gf.at[spot], dst_ref=gf.at[spot], send_sem=z_ss.at[1], recv_sem=z_rs.at[1],
            device_id=around(j), device_id_type=MESH).start()
        return carry

    three = incoming(gf.at[0, pl.ds(0, 3)], z_rs.at[0], z_ss.at[0])
    seven = incoming(gf.at[pl.ds(0, 7)], z_rs.at[1], z_ss.at[1])
    lax.fori_loop(1, 4, spread, 0)
    three.wait_recv()
    lax.fori_loop(1, 8, share, 0)

    arrived(kvf, kvf_rs)
    gk_ref[away_rows, :] = kvf[0]
    gv_ref[away_rows, :] = kvf[1]

    seven.wait_recv()
    for tile in range(TILES):
        row, column = tile // 11, tile % 11
        gw_ref[row * 16:row * 16 + 16, column * 128:(column + 1) * 128] = gf[
            tile // 16, tile // 4 % 4, tile % 4].astype(F32)

    for copy in sent:
        copy.wait_send()
    lax.fori_loop(0, 8, quad_sent, 0)
    three.wait_send()
    seven.wait_send()


def hand_over(*refs):
    count = len(refs) // 2
    sems = refs[-1]
    copies = [pltpu.make_async_copy(refs[i], refs[count + i], sems.at[i]) for i in range(count)]
    for copy in copies:
        copy.start()
    for copy in copies:
        copy.wait()


def per_device(queries, keys, values, patch_ids, counts, cotangent, w_out):
    vmem = pl.BlockSpec(memory_space=pltpu.VMEM)
    smem = pl.BlockSpec(memory_space=pltpu.SMEM)
    whole = pl.BlockSpec(memory_space=pl.ANY)
    halves = (2, HALF, ROWS)
    window = (SLOTS, HALF, ROWS)
    dma = pltpu.SemaphoreType.DMA
    scratch = [
        pltpu.VMEM(window, BF), pltpu.VMEM(window, BF), pltpu.VMEM(halves, BF), pltpu.VMEM((256, HALF), BF),
        pltpu.VMEM((4, ROWS, D), BF), pltpu.VMEM((4, BLOCK, D), BF),
        pltpu.VMEM((256, 768), F32), pltpu.VMEM((256, 768), F32),
        pltpu.VMEM((4, 256, 768), BF), pltpu.VMEM((256, 768), BF),
        pltpu.VMEM((HALF, 256), F32), pltpu.VMEM((HALF, 256), BF), pltpu.VMEM(halves, BF), pltpu.VMEM((HW, ROWS), BF),
        pltpu.VMEM((2, BLOCK, 256), BF), pltpu.VMEM((256, HALF), BF), pltpu.VMEM((HALF, 256), BF),
        pltpu.VMEM((HALF, 256), F32), pltpu.VMEM((HALF, 768), F32), pltpu.VMEM((HALF, 768), F32),
        pltpu.VMEM(halves, BF), pltpu.VMEM((HALF, ROWS), BF),
        pltpu.VMEM((2, 2, 2, BLOCK, 256), BF), pltpu.VMEM((2, 2, 2, BLOCK, 256), BF),
        pltpu.VMEM((2, 2, HALF, ROWS), BF), pltpu.VMEM((2, HALF, ROWS), BF),
        pltpu.VMEM((4, 32, 16, 128), BF), pltpu.VMEM((3, 32, 16, 128), BF),
        pltpu.VMEM((8, 4, 16, 128), BF), pltpu.VMEM((8, 4, 16, 128), BF),
        pltpu.VMEM((4, 4, 16, 128), BF), pltpu.VMEM((8, 4, 4, 16, 128), BF),
        dma((6,)), dma((6,)), dma, dma((4,)), dma((4,)), dma((2,)), dma, dma((2, 2)), dma, dma((3,)), dma((8,)),
        dma((4,)), dma((2,)),
        dma((40,)), dma((8,)), dma((2,)),
    ]
    shapes = (
        jax.ShapeDtypeStruct((ROWS, D), BF),
        jax.ShapeDtypeStruct((HW, ROWS), BF),
        jax.ShapeDtypeStruct((HW, ROWS), BF),
        jax.ShapeDtypeStruct((HW, ROWS), BF),
        jax.ShapeDtypeStruct((BLOCK, D), F32),
    )
    outs = pl.pallas_call(
        kernel,
        out_shape=shapes,
        in_specs=[vmem, vmem, vmem, vmem, smem, vmem, vmem],
        out_specs=(vmem,) * 5,
        scratch_shapes=scratch,
        compiler_params=pltpu.CompilerParams(
            collective_id=0, has_side_effects=True, vmem_limit_bytes=48 * 1024 * 1024),
        cost_estimate=pl.CostEstimate(flops=1500000000, bytes_accessed=4000000, transcendentals=800000),
    )(queries[0].T, keys[0].T, values[0].T, patch_ids.reshape(PLACES, ROWS), counts, cotangent[0], w_out)
    outs = pl.pallas_call(
        hand_over,
        out_shape=shapes,
        in_specs=[whole] * 5,
        out_specs=(whole,) * 5,
        scratch_shapes=[dma((5,))],
    )(*outs)
    attended, grad_queries, grad_keys, grad_values, grad_weight = outs
    return attended[None], grad_queries.T[None], grad_keys.T[None], grad_values.T[None], grad_weight


def solution(mesh):
    placed = (
        P("dp", "ctx", None),
        P("dp", "ctx", None),
        P("dp", "ctx", None),
        P("dp", None),
        P("dp", None),
        P("dp", "ctx", None),
        P("dp", None),
    )
    return jax.shard_map(
        per_device,
        mesh=mesh,
        in_specs=placed,
        out_specs=(
            P("dp", "ctx", None),
            P("dp", "ctx", None),
            P("dp", "ctx", None),
            P("dp", "ctx", None),
            P("dp", None),
        ),
        check_vma=False,
    )
```

```python
import jax
import jax.numpy as jnp
from jax import lax
from jax.experimental import pallas as pl
from jax.experimental.pallas import tpu as pltpu
from jax.sharding import PartitionSpec as P

HEAD = 88
WIN = 4
ROWS = 128
HALF = 352
HW = 704
D = 1408
BLOCK = 176
SLOTS = 6
PLACES = 128
SCALE = HEAD ** -0.5
MASKED = -1e30
TILES = 121
VMEM_LIMIT = 61 * 1024 * 1024
MESH = pl.DeviceIdType.MESH
WINDOWS = ((0, 128), (0, 256), (128, 352), (256, 352))
STRIPES = ((0, 96), (80, 176), (176, 272), (256, 352))
BF = jnp.bfloat16
F32 = jnp.float32


def last_last(left, right):
    return lax.dot_general(left, right, (((1,), (1,)), ((), ())), preferred_element_type=F32)


def first_first(left, right):
    return lax.dot_general(left, right, (((0,), (0,)), ((), ())), preferred_element_type=F32)


def plain(left, right):
    return jnp.dot(left, right, preferred_element_type=F32)


def head_mask(head, rows):
    low, high = WINDOWS[head]
    lane = lax.broadcasted_iota(jnp.int32, (rows, high - low), 1) + low
    return jnp.where((lane >= HEAD * head) & (lane < HEAD * (head + 1)), 1.0, 0.0)


def stripe(head, value):
    skip = HEAD * head - STRIPES[head][0]
    return value[skip:skip + HEAD]


def kernel(q_ref, k_ref, v_ref, pid_hbm, cnt_hbm, cot_hbm, w_ref,
           att_hbm, gq_hbm, gk_hbm, gv_hbm, gw_hbm,
           pid_ref, cnt_ref, cot_ref, att_ref,
           kw, vw, qw, qn, gl, wf, bias, s_buf, probs, ds_buf,
           ctx_acc, cb, cw, cf, ct, g_buf, gt_buf, dq_acc, dk_acc, dv_acc, dqw, dqf,
           kvb, rkv, kvs, kvf,
           dw, ry, sx, rx, fr, gf,
           k_rs, v_rs, q_rs, gl_rs, w_rs, c_rs, dq_rs, kv_rs, kvf_rs, y_rs, x_rs, f_rs, z_rs,
           ss, x_ss, z_ss, in_sems, out_sems):
    dp = lax.axis_index("dp")
    place = lax.axis_index("ctx")
    xh = lax.div(dp, 2)
    core = lax.rem(dp, 2)
    pair = lax.div(place, 2)
    xl = lax.rem(place, 2)
    y = lax.div(place, 32)
    z = lax.rem(pair, 16)
    group = lax.div(z, 4)
    inner = lax.rem(z, 4)
    spot = y * 2 + xl

    partner = (dp, place + 1 - 2 * xl)
    twin = (dp + 1 - 2 * core, place)
    other = lax.rem(dp + 2, 4)
    across = (other, place + 1 - 2 * xl)
    ahead = (dp, lax.rem(place + 2, PLACES))
    behind = (dp, lax.rem(place + PLACES - 2, PLACES))

    def around(j):
        where = lax.rem(spot + j, 8)
        return (dp, lax.div(where, 2) * 32 + z * 2 + lax.rem(where, 2))

    def quad(x, b):
        return (lax.div(x, 2) * 2 + core, (y * 16 + group * 4 + b) * 2 + lax.rem(x, 2))

    def far(j):
        return (dp, (y * 16 + lax.rem(z + 4 * j, 16)) * 2 + xl)

    near_rows = pl.ds(pl.multiple_of(xl * HALF, 16), HALF)
    away_rows = pl.ds(pl.multiple_of((1 - xl) * HALF, 16), HALF)
    fetches = []
    for source, target in (
            (cot_hbm, cot_ref), (cnt_hbm, cnt_ref), (pid_hbm, pid_ref), (k_ref.at[near_rows], kw.at[2 + xl]),
            (q_ref.at[near_rows], qw.at[xl]), (v_ref.at[near_rows], vw.at[2 + xl]), (w_ref, wf.at[dp])):
        fetches.append(pltpu.make_async_copy(source, target, in_sems.at[len(fetches)]))
        fetches[-1].start()

    written = []

    def write(source, target):
        written.append(pltpu.make_async_copy(source, target, out_sems.at[len(written)]))
        written[-1].start()

    barrier = pltpu.get_barrier_semaphore()

    def greet(device):
        pl.semaphore_signal(barrier, inc=1, device_id=device, device_id_type=MESH)

    def greet_quad(j, carry):
        at = lax.rem((xh * 2 + xl) * 4 + inner + j, 16)
        greet(quad(lax.div(at, 4), lax.rem(at, 4)))
        return carry

    def greet_around(j, carry):
        greet(around(j))
        return carry

    def greet_far(j, carry):
        greet(far(j))
        return carry

    for device in (ahead, behind, twin):
        greet(device)
    lax.fori_loop(1, 4, greet_far, 0)
    lax.fori_loop(1, 16, greet_quad, 0)
    lax.fori_loop(1, 8, greet_around, 0)

    fetches[0].wait()
    fetches[1].wait()
    own_live = lax.broadcasted_iota(jnp.int32, (ROWS, 128), 0) < cnt_ref[0, place]
    mine = core * 2 + xl
    for block in range(11):
        cols = slice(block * 128, (block + 1) * 128)
        gl[mine, :, cols] = jnp.where(own_live, cot_ref[:, cols].astype(F32), 0.0).astype(BF)

    pl.semaphore_wait(barrier, 28)

    sent = []

    def send(source, target, recv_sem, device):
        copy = pltpu.make_async_remote_copy(
            src_ref=source, dst_ref=target, send_sem=ss.at[len(sent)], recv_sem=recv_sem,
            device_id=device, device_id_type=MESH)
        copy.start()
        sent.append(copy)

    def incoming(ref, recv_sem, send_sem):
        return pltpu.make_async_remote_copy(
            src_ref=ref, dst_ref=ref, send_sem=send_sem, recv_sem=recv_sem,
            device_id=partner, device_id_type=MESH)

    def arrived(ref, recv_sem):
        incoming(ref, recv_sem, ss.at[0]).wait_recv()

    away = 3 - xl
    send(k_ref.at[away_rows], kw.at[2 + xl], k_rs.at[2 + xl], partner)
    send(k_ref.at[near_rows], kw.at[xl], k_rs.at[xl], ahead)
    send(k_ref.at[near_rows], kw.at[4 + xl], k_rs.at[4 + xl], behind)
    send(v_ref.at[away_rows], vw.at[2 + xl], v_rs.at[2 + xl], partner)
    send(q_ref.at[away_rows], qw.at[xl], q_rs, partner)
    send(gl.at[mine], gl.at[mine], gl_rs.at[mine], partner)
    send(w_ref, wf.at[dp], w_rs.at[dp], across)
    send(w_ref, wf.at[dp], w_rs.at[dp], twin)
    send(gl.at[mine], gl.at[mine], gl_rs.at[mine], twin)
    for fetch in fetches[2:]:
        fetch.wait()

    arrived(kw.at[away], k_rs.at[away])
    send(kw.at[away], kw.at[1 - xl], k_rs.at[1 - xl], ahead)
    send(kw.at[away], kw.at[5 - xl], k_rs.at[5 - xl], behind)
    send(v_ref.at[near_rows], vw.at[xl], v_rs.at[xl], ahead)
    send(v_ref.at[near_rows], vw.at[4 + xl], v_rs.at[4 + xl], behind)
    arrived(vw.at[away], v_rs.at[away])
    send(vw.at[away], vw.at[1 - xl], v_rs.at[1 - xl], ahead)
    send(vw.at[away], vw.at[5 - xl], v_rs.at[5 - xl], behind)

    frames, live = [], []
    for slot in range(SLOTS):
        shard = lax.rem(2 * pair - 2 + slot + PLACES, PLACES)
        inside = (2 * pair - 2 + slot >= 0) & (2 * pair - 2 + slot < PLACES)
        count = jnp.where(inside, cnt_ref[0, shard], 0)
        frame = lax.shift_right_logical(pid_ref[pl.ds(shard, 1), :], 8) + 2 * (slot - 2)
        frames.append(frame.astype(F32))
        live.append(lax.broadcasted_iota(jnp.int32, (ROWS, 128), 1) < count)
    for half in range(2):
        column = jnp.transpose(jnp.broadcast_to(frames[2 + half], (ROWS, 128)))
        for slot in range(SLOTS):
            seen = live[slot] & (jnp.abs(frames[slot] - column) <= WIN)
            bias[half * 128:(half + 1) * 128, slot * 128:(slot + 1) * 128] = jnp.where(seen, 0.0, MASKED)

    arrived(qw.at[1 - xl], q_rs)
    for half in range(2):
        qn[half * 128:(half + 1) * 128, :] = jnp.transpose(qw[half].astype(F32)).astype(BF)
    for slot in (0, 1, 4, 5):
        arrived(kw.at[slot], k_rs.at[slot])

    def lanes(ref, low, high, first, slots):
        return jnp.concatenate([ref[first + i, low:high, :] for i in range(slots)], axis=1)

    def folded(op, value, old):
        here = op(value[:, :128], value[:, 128:])
        return here if old is None else op(old, here)

    for head in range(4):
        low, high = WINDOWS[head]
        q_head = qn[:, low:high] * head_mask(head, 256).astype(BF)
        top = None
        for part in range(3):
            cols = slice(part * 256, part * 256 + 256)
            score = plain(q_head, lanes(kw, low, high, part * 2, 2)) * SCALE + bias[:, cols]
            s_buf[:, cols] = score
            top = folded(jnp.maximum, score, top)
        top = jnp.max(top, axis=1, keepdims=True)
        total = None
        for part in range(3):
            cols = slice(part * 256, part * 256 + 256)
            expon = jnp.exp(s_buf[:, cols] - top)
            s_buf[:, cols] = expon
            total = folded(jnp.add, expon, total)
        inverse = 1.0 / jnp.sum(total, axis=1, keepdims=True)
        for part in range(3):
            cols = slice(part * 256, part * 256 + 256)
            probs[head, :, cols] = (s_buf[:, cols] * inverse).astype(BF)
        if head == 0:
            for slot in (0, 1, 4, 5):
                arrived(vw.at[slot], v_rs.at[slot])
        ctx_acc[head * HEAD:(head + 1) * HEAD, :] = stripe(
            head, last_last(lanes(vw, *STRIPES[head], 0, SLOTS), probs[head]))
    cb[...] = ctx_acc[...].astype(BF)
    core_rows = pl.ds(pl.multiple_of(core * BLOCK, 16), BLOCK)
    send(cb.at[pl.ds(pl.multiple_of((1 - core) * BLOCK, 16), BLOCK)], ct.at[core], c_rs.at[0], twin)
    cw[0] = cb[:, 0:128]
    cw[1] = cb[:, 128:256]
    send(cw.at[1 - xl], cf.at[near_rows], c_rs.at[1], partner)
    ct[core] = cb[core_rows, :]
    cf[near_rows, :] = cw[xl]

    theirs = core * 2 + 1 - xl
    arrived(gl.at[theirs], gl_rs.at[theirs])
    send(gl.at[theirs], gl.at[theirs], gl_rs.at[theirs], twin)
    arrived(wf.at[other], w_rs.at[other])
    send(wf.at[other], wf.at[other], w_rs.at[other], twin)
    arrived(wf.at[dp + 1 - 2 * core], w_rs.at[dp + 1 - 2 * core])
    arrived(wf.at[other + 1 - 2 * core], w_rs.at[other + 1 - 2 * core])
    grad_context = last_last(gl[pl.ds(core * 2, 2)].reshape(256, D), wf[pl.ds(xl * 2, 2)].reshape(HALF, D))
    g_buf[...] = grad_context.astype(BF)
    gt_buf[...] = jnp.transpose(grad_context).astype(BF)

    arrived(ct.at[1 - core], c_rs.at[0])
    for slot in range(2):
        there = (1 - core) * 2 + slot
        arrived(gl.at[there], gl_rs.at[there])
    context = jnp.concatenate([ct[0], ct[1]], axis=1)
    for start in range(0, D, 256):
        stop = min(start + 256, D)
        part = plain(context, gl[:, :, start:stop].reshape(512, stop - start))
        for column in range(start, stop, 128):
            for row in range(11):
                tile = row * 11 + column // 128
                dw[tile // 32, tile % 32] = part[row * 16:row * 16 + 16, column - start:column - start + 128].astype(BF)
    for tile in range(TILES, 128):
        dw[tile // 32, tile % 32] = jnp.zeros((16, 128), BF)
    for step in (1, 3, 2):
        goal = lax.rem(y + step, 4)
        send(dw.at[goal], ry.at[step - 1], y_rs.at[step - 1], (dp, lax.rem(place + 32 * step, PLACES)))

    for head in range(4):
        low, high = WINDOWS[head]
        g_head = g_buf[:, low:high] * head_mask(head, 256).astype(BF)
        delta = None
        for part in range(3):
            cols = slice(part * 256, part * 256 + 256)
            grad_prob = plain(g_head, lanes(vw, low, high, part * 2, 2))
            s_buf[:, cols] = grad_prob
            delta = folded(jnp.add, probs[head, :, cols].astype(F32) * grad_prob, delta)
        delta = jnp.sum(delta, axis=1, keepdims=True)
        for part in range(3):
            cols = slice(part * 256, part * 256 + 256)
            ds_buf[:, cols] = (probs[head, :, cols].astype(F32) * (s_buf[:, cols] - delta)).astype(BF)
        rows = slice(head * HEAD, (head + 1) * HEAD)
        first, stop = STRIPES[head]
        dk_acc[rows, :] = stripe(head, plain(lanes(qw, first, stop, 0, 2), ds_buf[...])) * SCALE
        dv_acc[rows, :] = stripe(head, plain(gt_buf[first:stop, :], probs[head]))
        dq_acc[rows, :] = stripe(head, last_last(lanes(kw, first, stop, 0, SLOTS), ds_buf[...])) * SCALE
        if head % 2 == 1:
            piece = head // 2
            block = slice(piece * BLOCK, (piece + 1) * BLOCK)
            for side in range(2):
                cols = slice(side * 512, side * 512 + 256)
                kvb[side, piece, 0] = dk_acc[block, cols].astype(BF)
                kvb[side, piece, 1] = dv_acc[block, cols].astype(BF)
                send(kvb.at[side, piece], rkv.at[1 - side, piece], kv_rs.at[1 - side, piece], (behind, ahead)[side])
    dqw[0] = dq_acc[:, 0:128].astype(BF)
    dqw[1] = dq_acc[:, 128:256].astype(BF)
    send(dqw.at[1 - xl], dqf, dq_rs, partner)
    write(dqw.at[xl], gq_hbm.at[near_rows])

    for step in range(3):
        arrived(ry.at[step], y_rs.at[step])
    total = dw[y].astype(F32) + ry[0].astype(F32) + ry[1].astype(F32) + ry[2].astype(F32)
    sx[...] = total.astype(BF).reshape(8, 4, 16, 128)

    def stays(half, b):
        return (xh == xl) & (xl == half) & (inner == b)

    def quad_copy(n):
        half, b = lax.div(n, 4), lax.rem(n, 4)
        return pltpu.make_async_remote_copy(
            src_ref=sx.at[n], dst_ref=rx.at[xh * 4 + inner], send_sem=x_ss.at[n], recv_sem=x_rs.at[xh * 4 + inner],
            device_id=quad(xl * 2 + half, b), device_id_type=MESH)

    def quad_start(n, carry):
        @pl.when(jnp.logical_not(stays(lax.div(n, 4), lax.rem(n, 4))))
        def _():
            quad_copy(n).start()

        return carry

    def quad_sent(n, carry):
        @pl.when(jnp.logical_not(stays(lax.div(n, 4), lax.rem(n, 4))))
        def _():
            quad_copy(n).wait_send()

        return carry

    def quad_here(n, carry):
        @pl.when(jnp.logical_not((xh == xl) & (n == xh * 4 + inner)))
        def _():
            arrived(rx.at[n], x_rs.at[n])

        return carry

    lax.fori_loop(0, 8, quad_start, 0)

    @pl.when(xh == xl)
    def _():
        rx[xh * 4 + inner] = sx[xl * 4 + inner]

    arrived(cf.at[away_rows], c_rs.at[1])
    projected = first_first(cf[...], wf[...].reshape(HW, D))
    for block in range(11):
        cols = slice(block * 128, (block + 1) * 128)
        att_ref[:, cols] = jnp.where(own_live, projected[:, cols], 0.0).astype(BF)
    write(att_ref, att_hbm)

    lax.fori_loop(0, 8, quad_here, 0)
    total = rx[0].astype(F32)
    for source in range(1, 8):
        total = total + rx[source].astype(F32)
    fr[group] = total.astype(BF)
    for step in (2, 1, 3):
        send(fr.at[group], fr.at[group], f_rs.at[group], far(step))

    for piece in range(2):
        block = slice(piece * BLOCK, (piece + 1) * BLOCK)
        for side in range(2):
            arrived(rkv.at[side, piece], kv_rs.at[side, piece])
        for which, acc in ((0, dk_acc), (1, dv_acc)):
            value = acc[block, 256:512] + rkv[0, piece, which].astype(F32) + rkv[1, piece, which].astype(F32)
            kvs[0, which, block, :] = value[:, 0:128].astype(BF)
            kvs[1, which, block, :] = value[:, 128:256].astype(BF)
    send(kvs.at[1 - xl], kvf, kvf_rs, partner)
    write(kvs.at[xl, 0], gk_hbm.at[near_rows])
    write(kvs.at[xl, 1], gv_hbm.at[near_rows])
    arrived(dqf, dq_rs)
    write(dqf, gq_hbm.at[away_rows])

    for step in range(1, 4):
        source = lax.rem(group + step, 4)
        arrived(fr.at[source], f_rs.at[source])
    total = fr[0].astype(F32) + fr[1].astype(F32) + fr[2].astype(F32) + fr[3].astype(F32)
    gf[spot, inner] = total.astype(BF)

    def spread(j, carry):
        pltpu.make_async_remote_copy(
            src_ref=gf.at[spot, inner], dst_ref=gf.at[spot, inner], send_sem=z_ss.at[0], recv_sem=z_rs.at[0],
            device_id=quad(xh * 2 + xl, lax.rem(inner + j, 4)), device_id_type=MESH).start()
        return carry

    def share(j, carry):
        pltpu.make_async_remote_copy(
            src_ref=gf.at[spot], dst_ref=gf.at[spot], send_sem=z_ss.at[1], recv_sem=z_rs.at[1],
            device_id=around(j), device_id_type=MESH).start()
        return carry

    three = incoming(gf.at[0, pl.ds(0, 3)], z_rs.at[0], z_ss.at[0])
    seven = incoming(gf.at[pl.ds(0, 7)], z_rs.at[1], z_ss.at[1])
    lax.fori_loop(1, 4, spread, 0)
    three.wait_recv()
    lax.fori_loop(1, 8, share, 0)

    arrived(kvf, kvf_rs)
    write(kvf.at[0], gk_hbm.at[away_rows])
    write(kvf.at[1], gv_hbm.at[away_rows])

    seven.wait_recv()
    write(gf, gw_hbm)
    for copy in sent:
        copy.wait_send()
    lax.fori_loop(0, 8, quad_sent, 0)
    three.wait_send()
    seven.wait_send()
    for copy in written:
        copy.wait()


def hand_over(att_in, gq_in, gk_in, gv_in, gw_in, att_out, gq_out, gk_out, gv_out, gw_out,
              att, gq, gk, gv, tiles, gw, in_sems, out_sems):
    held = (tiles, att, gq, gk, gv)
    outs = (gw_out, att_out, gq_out, gk_out, gv_out)
    reads = [pltpu.make_async_copy(source, target, in_sems.at[i])
             for i, (source, target) in enumerate(zip((gw_in, att_in, gq_in, gk_in, gv_in), held))]
    writes = [pltpu.make_async_copy(source, target, out_sems.at[i])
              for i, (source, target) in enumerate(zip((gw,) + held[1:], outs))]
    for read in reads:
        read.start()
    for read, copy in list(zip(reads, writes))[1:]:
        read.wait()
        copy.start()
    reads[0].wait()
    for tile in range(TILES):
        row, column = tile // 11, tile % 11
        gw[row * 16:row * 16 + 16, column * 128:(column + 1) * 128] = tiles[
            tile // 16, tile // 4 % 4, tile % 4].astype(F32)
    writes[0].start()
    for copy in writes:
        copy.wait()


def per_device(queries, keys, values, patch_ids, counts, cotangent, w_out):
    hbm = pl.BlockSpec(memory_space=pltpu.HBM)
    tiles = (8, 4, 4, 16, 128)
    halves = (2, HALF, ROWS)
    window = (SLOTS, HALF, ROWS)
    dma = pltpu.SemaphoreType.DMA
    scratch = [
        pltpu.VMEM((PLACES, ROWS), jnp.int32), pltpu.SMEM((1, PLACES), jnp.int32), pltpu.VMEM((ROWS, D), BF),
        pltpu.VMEM((ROWS, D), BF),
        pltpu.VMEM(window, BF), pltpu.VMEM(window, BF), pltpu.VMEM(halves, BF), pltpu.VMEM((256, HALF), BF),
        pltpu.VMEM((4, ROWS, D), BF), pltpu.VMEM((4, BLOCK, D), BF),
        pltpu.VMEM((256, 768), F32), pltpu.VMEM((256, 768), F32),
        pltpu.VMEM((4, 256, 768), BF), pltpu.VMEM((256, 768), BF),
        pltpu.VMEM((HALF, 256), F32), pltpu.VMEM((HALF, 256), BF), pltpu.VMEM(halves, BF), pltpu.VMEM((HW, ROWS), BF),
        pltpu.VMEM((2, BLOCK, 256), BF), pltpu.VMEM((256, HALF), BF), pltpu.VMEM((HALF, 256), BF),
        pltpu.VMEM((HALF, 256), F32), pltpu.VMEM((HALF, 768), F32), pltpu.VMEM((HALF, 768), F32),
        pltpu.VMEM(halves, BF), pltpu.VMEM((HALF, ROWS), BF),
        pltpu.VMEM((2, 2, 2, BLOCK, 256), BF), pltpu.VMEM((2, 2, 2, BLOCK, 256), BF),
        pltpu.VMEM((2, 2, HALF, ROWS), BF), pltpu.VMEM((2, HALF, ROWS), BF),
        pltpu.VMEM((4, 32, 16, 128), BF), pltpu.VMEM((3, 32, 16, 128), BF),
        pltpu.VMEM((8, 4, 16, 128), BF), pltpu.VMEM((8, 4, 16, 128), BF),
        pltpu.VMEM((4, 4, 16, 128), BF), pltpu.VMEM(tiles, BF),
        dma((6,)), dma((6,)), dma, dma((4,)), dma((4,)), dma((2,)), dma, dma((2, 2)), dma, dma((3,)), dma((8,)),
        dma((4,)), dma((2,)),
        dma((40,)), dma((8,)), dma((2,)), dma((7,)), dma((8,)),
    ]
    shapes = (
        jax.ShapeDtypeStruct((ROWS, D), BF),
        jax.ShapeDtypeStruct((HW, ROWS), BF),
        jax.ShapeDtypeStruct((HW, ROWS), BF),
        jax.ShapeDtypeStruct((HW, ROWS), BF),
    )
    outs = pl.pallas_call(
        kernel,
        out_shape=shapes + (jax.ShapeDtypeStruct(tiles, BF),),
        in_specs=[hbm] * 7,
        out_specs=(hbm,) * 5,
        scratch_shapes=scratch,
        compiler_params=pltpu.CompilerParams(
            collective_id=0, has_side_effects=True, vmem_limit_bytes=VMEM_LIMIT),
        cost_estimate=pl.CostEstimate(flops=1500000000, bytes_accessed=4000000, transcendentals=800000),
    )(queries[0].T, keys[0].T, values[0].T, patch_ids.reshape(PLACES, ROWS), counts, cotangent[0], w_out)
    outs = pl.pallas_call(
        hand_over,
        out_shape=shapes + (jax.ShapeDtypeStruct((BLOCK, D), F32),),
        in_specs=[hbm] * 5,
        out_specs=(hbm,) * 5,
        scratch_shapes=[
            pltpu.VMEM((ROWS, D), BF), pltpu.VMEM((HW, ROWS), BF), pltpu.VMEM((HW, ROWS), BF), pltpu.VMEM((HW, ROWS), BF),
            pltpu.VMEM(tiles, BF), pltpu.VMEM((BLOCK, D), F32), dma((5,)), dma((5,))],
        compiler_params=pltpu.CompilerParams(vmem_limit_bytes=VMEM_LIMIT),
    )(*outs)
    attended, grad_queries, grad_keys, grad_values, grad_weight = outs
    return attended[None], grad_queries.T[None], grad_keys.T[None], grad_values.T[None], grad_weight


def solution(mesh):
    placed = (
        P("dp", "ctx", None),
        P("dp", "ctx", None),
        P("dp", "ctx", None),
        P("dp", None),
        P("dp", None),
        P("dp", "ctx", None),
        P("dp", None),
    )
    return jax.shard_map(
        per_device,
        mesh=mesh,
        in_specs=placed,
        out_specs=(
            P("dp", "ctx", None),
            P("dp", "ctx", None),
            P("dp", "ctx", None),
            P("dp", "ctx", None),
            P("dp", None),
        ),
        check_vma=False,
    )
```

```python
import jax
import jax.numpy as jnp
from jax import lax
from jax.experimental import pallas as pl
from jax.experimental.pallas import tpu as pltpu
from jax.sharding import PartitionSpec as P

HEAD = 88
WIN = 4
ROWS = 128
HALF = 352
HW = 704
D = 1408
BLOCK = 176
SLOTS = 6
PLACES = 128
SCALE = HEAD ** -0.5
MASKED = -1e30
TILES = 121
PIECE = 384
ORDER = (1, 3, 2, 0)
VMEM_LIMIT = 61 * 1024 * 1024
MESH = pl.DeviceIdType.MESH
WINDOWS = ((0, 128), (0, 256), (128, 352), (256, 352))
STRIPES = ((0, 96), (80, 176), (176, 272), (256, 352))
BF = jnp.bfloat16
F32 = jnp.float32


def last_last(left, right):
    return lax.dot_general(left, right, (((1,), (1,)), ((), ())), preferred_element_type=F32)


def first_first(left, right):
    return lax.dot_general(left, right, (((0,), (0,)), ((), ())), preferred_element_type=F32)


def plain(left, right):
    return jnp.dot(left, right, preferred_element_type=F32)


def head_mask(head, rows):
    low, high = WINDOWS[head]
    lane = lax.broadcasted_iota(jnp.int32, (rows, high - low), 1) + low
    return jnp.where((lane >= HEAD * head) & (lane < HEAD * (head + 1)), 1.0, 0.0)


def stripe(head, value):
    skip = HEAD * head - STRIPES[head][0]
    return value[skip:skip + HEAD]


def kernel(q_ref, k_ref, v_ref, pid_hbm, cnt_hbm, cot_hbm, w_ref,
           att_hbm, gq_hbm, gk_hbm, gv_hbm, gw_hbm,
           pid_ref, cnt_ref, cot_ref, att_ref,
           kw, vw, qw, qn, gl, wf, bias, s_buf, probs, ds_buf,
           ctx_acc, cb, cw, cf, ct, g_buf, gt_buf, dq_acc, dk_acc, dv_acc, dqw, dqf,
           kvb, rkv, kvs, kvf,
           dw, dwx, ry, ryx, sx, rx, fr, gf,
           k_rs, v_rs, q_rs, gl_rs, w_rs, c_rs, dq_rs, kv_rs, kvf_rs, y_rs, yx_rs, x_rs, f_rs, z_rs,
           ss, y_ss, x_ss, z_ss, in_sems, out_sems):
    dp = lax.axis_index("dp")
    place = lax.axis_index("ctx")
    xh = lax.div(dp, 2)
    core = lax.rem(dp, 2)
    pair = lax.div(place, 2)
    xl = lax.rem(place, 2)
    y = lax.div(place, 32)
    z = lax.rem(pair, 16)
    group = lax.div(z, 4)
    inner = lax.rem(z, 4)
    spot = y * 2 + xl

    partner = (dp, place + 1 - 2 * xl)
    twin = (dp + 1 - 2 * core, place)
    other = lax.rem(dp + 2, 4)
    across = (other, place + 1 - 2 * xl)
    ahead = (dp, lax.rem(place + 2, PLACES))
    behind = (dp, lax.rem(place + PLACES - 2, PLACES))

    def around(j):
        where = lax.rem(spot + j, 8)
        return (dp, lax.div(where, 2) * 32 + z * 2 + lax.rem(where, 2))

    def quad(x, b):
        return (lax.div(x, 2) * 2 + core, (y * 16 + group * 4 + b) * 2 + lax.rem(x, 2))

    def far(j):
        return (dp, (y * 16 + lax.rem(z + 4 * j, 16)) * 2 + xl)

    near_rows = pl.ds(pl.multiple_of(xl * HALF, 16), HALF)
    away_rows = pl.ds(pl.multiple_of((1 - xl) * HALF, 16), HALF)
    fetches = []
    for source, target in (
            (cot_hbm, cot_ref), (cnt_hbm, cnt_ref), (pid_hbm, pid_ref), (k_ref.at[near_rows], kw.at[2 + xl]),
            (q_ref.at[near_rows], qw.at[xl]), (v_ref.at[near_rows], vw.at[2 + xl]), (w_ref, wf.at[dp])):
        fetches.append(pltpu.make_async_copy(source, target, in_sems.at[len(fetches)]))
        fetches[-1].start()

    written = []

    def write(source, target):
        written.append(pltpu.make_async_copy(source, target, out_sems.at[len(written)]))
        written[-1].start()

    barrier = pltpu.get_barrier_semaphore()

    def greet(device):
        pl.semaphore_signal(barrier, inc=1, device_id=device, device_id_type=MESH)

    def greet_quad(j, carry):
        at = lax.rem((xh * 2 + xl) * 4 + inner + j, 16)
        greet(quad(lax.div(at, 4), lax.rem(at, 4)))
        return carry

    def greet_around(j, carry):
        greet(around(j))
        return carry

    def greet_far(j, carry):
        greet(far(j))
        return carry

    for device in (ahead, behind, twin):
        greet(device)
    lax.fori_loop(1, 4, greet_far, 0)
    lax.fori_loop(1, 16, greet_quad, 0)
    lax.fori_loop(1, 8, greet_around, 0)

    fetches[0].wait()
    fetches[1].wait()
    own_live = lax.broadcasted_iota(jnp.int32, (ROWS, 128), 0) < cnt_ref[0, place]
    mine = core * 2 + xl
    for block in range(11):
        cols = slice(block * 128, (block + 1) * 128)
        inside = slice(block % 3 * 128, (block % 3 + 1) * 128)
        gl[block // 3, mine, :, inside] = jnp.where(own_live, cot_ref[:, cols].astype(F32), 0.0).astype(BF)
    gl[3, mine, :, 256:384] = jnp.zeros((ROWS, 128), BF)

    def piece_at(step):
        return lax.rem(y + step, 4)

    pl.semaphore_wait(barrier, 28)

    sent = []

    def send(source, target, recv_sem, device):
        copy = pltpu.make_async_remote_copy(
            src_ref=source, dst_ref=target, send_sem=ss.at[len(sent)], recv_sem=recv_sem,
            device_id=device, device_id_type=MESH)
        copy.start()
        sent.append(copy)

    def incoming(ref, recv_sem, send_sem):
        return pltpu.make_async_remote_copy(
            src_ref=ref, dst_ref=ref, send_sem=send_sem, recv_sem=recv_sem,
            device_id=partner, device_id_type=MESH)

    def arrived(ref, recv_sem):
        incoming(ref, recv_sem, ss.at[0]).wait_recv()

    away = 3 - xl
    send(k_ref.at[away_rows], kw.at[2 + xl], k_rs.at[2 + xl], partner)
    send(k_ref.at[near_rows], kw.at[xl], k_rs.at[xl], ahead)
    send(k_ref.at[near_rows], kw.at[4 + xl], k_rs.at[4 + xl], behind)
    send(v_ref.at[away_rows], vw.at[2 + xl], v_rs.at[2 + xl], partner)
    send(v_ref.at[near_rows], vw.at[xl], v_rs.at[xl], ahead)
    send(v_ref.at[near_rows], vw.at[4 + xl], v_rs.at[4 + xl], behind)
    send(q_ref.at[away_rows], qw.at[xl], q_rs, partner)
    for step in ORDER:
        here = gl.at[piece_at(step), mine]
        send(here, here, gl_rs.at[mine, step], partner)
    send(w_ref, wf.at[dp], w_rs.at[dp], across)
    send(w_ref, wf.at[dp], w_rs.at[dp], twin)
    send(gl.at[:, mine], gl.at[:, mine], gl_rs.at[mine, 0], twin)
    for fetch in fetches[2:]:
        fetch.wait()

    arrived(kw.at[away], k_rs.at[away])
    send(kw.at[away], kw.at[1 - xl], k_rs.at[1 - xl], ahead)
    send(kw.at[away], kw.at[5 - xl], k_rs.at[5 - xl], behind)
    arrived(vw.at[away], v_rs.at[away])
    send(vw.at[away], vw.at[1 - xl], v_rs.at[1 - xl], ahead)
    send(vw.at[away], vw.at[5 - xl], v_rs.at[5 - xl], behind)

    frames, live = [], []
    for slot in range(SLOTS):
        shard = lax.rem(2 * pair - 2 + slot + PLACES, PLACES)
        inside = (2 * pair - 2 + slot >= 0) & (2 * pair - 2 + slot < PLACES)
        count = jnp.where(inside, cnt_ref[0, shard], 0)
        frame = lax.shift_right_logical(pid_ref[pl.ds(shard, 1), :], 8) + 2 * (slot - 2)
        frames.append(frame.astype(F32))
        live.append(lax.broadcasted_iota(jnp.int32, (ROWS, 128), 1) < count)
    for half in range(2):
        column = jnp.transpose(jnp.broadcast_to(frames[2 + half], (ROWS, 128)))
        for slot in range(SLOTS):
            seen = live[slot] & (jnp.abs(frames[slot] - column) <= WIN)
            bias[half * 128:(half + 1) * 128, slot * 128:(slot + 1) * 128] = jnp.where(seen, 0.0, MASKED)

    arrived(qw.at[1 - xl], q_rs)
    for half in range(2):
        qn[half * 128:(half + 1) * 128, :] = jnp.transpose(qw[half].astype(F32)).astype(BF)
    for slot in (0, 1, 4, 5):
        arrived(kw.at[slot], k_rs.at[slot])

    def lanes(ref, low, high, first, slots):
        return jnp.concatenate([ref[first + i, low:high, :] for i in range(slots)], axis=1)

    def folded(op, value, old):
        here = op(value[:, :128], value[:, 128:])
        return here if old is None else op(old, here)

    theirs = core * 2 + 1 - xl

    def relay_cotangent(step):
        here = gl.at[piece_at(step), theirs]
        arrived(here, gl_rs.at[theirs, step])
        send(here, here, gl_rs.at[theirs, step], twin)

    for head in range(4):
        low, high = WINDOWS[head]
        q_head = qn[:, low:high] * head_mask(head, 256).astype(BF)
        top = None
        for part in range(3):
            cols = slice(part * 256, part * 256 + 256)
            score = plain(q_head, lanes(kw, low, high, part * 2, 2)) * SCALE + bias[:, cols]
            s_buf[:, cols] = score
            top = folded(jnp.maximum, score, top)
        top = jnp.max(top, axis=1, keepdims=True)
        total = None
        for part in range(3):
            cols = slice(part * 256, part * 256 + 256)
            expon = jnp.exp(s_buf[:, cols] - top)
            s_buf[:, cols] = expon
            total = folded(jnp.add, expon, total)
        inverse = 1.0 / jnp.sum(total, axis=1, keepdims=True)
        for part in range(3):
            cols = slice(part * 256, part * 256 + 256)
            probs[head, :, cols] = (s_buf[:, cols] * inverse).astype(BF)
    relay_cotangent(ORDER[0])
    for slot in (0, 1, 4, 5):
        arrived(vw.at[slot], v_rs.at[slot])
    for head in range(4):
        ctx_acc[head * HEAD:(head + 1) * HEAD, :] = stripe(
            head, last_last(lanes(vw, *STRIPES[head], 0, SLOTS), probs[head]))
    cb[...] = ctx_acc[...].astype(BF)
    core_rows = pl.ds(pl.multiple_of(core * BLOCK, 16), BLOCK)
    send(cb.at[pl.ds(pl.multiple_of((1 - core) * BLOCK, 16), BLOCK)], ct.at[core], c_rs.at[0], twin)
    cw[0] = cb[:, 0:128]
    cw[1] = cb[:, 128:256]
    send(cw.at[1 - xl], cf.at[near_rows], c_rs.at[1], partner)
    ct[core] = cb[core_rows, :]
    cf[near_rows, :] = cw[xl]

    def weight_piece(step):
        piece = piece_at(step)
        there = (1 - core) * 2 + 1 - xl
        arrived(gl.at[piece, there], gl_rs.at[there, step])
        part = plain(context, gl[piece].reshape(512, PIECE))
        for tile in range(33):
            row, column = tile % 11 * 16, tile // 11 * 128
            value = part[row:row + 16, column:column + 128].astype(BF)
            if tile < 32:
                dw[piece, tile] = value
            else:
                dwx[piece] = value
        if step:
            send(dw.at[piece], ry.at[step - 1], y_rs.at[step - 1], (dp, piece * 32 + z * 2 + xl))

    def extra_copy():
        return pltpu.make_async_remote_copy(
            src_ref=dwx.at[pl.ds(0, 3)], dst_ref=ryx.at[y], send_sem=y_ss, recv_sem=yx_rs.at[y],
            device_id=(dp, 96 + z * 2 + xl), device_id_type=MESH)

    relay_cotangent(ORDER[1])
    arrived(gl.at[:, (1 - core) * 2 + xl], gl_rs.at[(1 - core) * 2 + xl, 0])
    arrived(ct.at[1 - core], c_rs.at[0])
    context = jnp.concatenate([ct[0], ct[1]], axis=1)
    weight_piece(ORDER[0])
    weight_piece(ORDER[1])
    arrived(wf.at[other], w_rs.at[other])
    send(wf.at[other], wf.at[other], w_rs.at[other], twin)
    relay_cotangent(ORDER[2])
    weight_piece(ORDER[2])

    arrived(cf.at[away_rows], c_rs.at[1])
    arrived(wf.at[dp + 1 - 2 * core], w_rs.at[dp + 1 - 2 * core])
    arrived(wf.at[other + 1 - 2 * core], w_rs.at[other + 1 - 2 * core])
    projected = first_first(cf[...], wf[...].reshape(HW, D))
    for block in range(11):
        cols = slice(block * 128, (block + 1) * 128)
        att_ref[:, cols] = jnp.where(own_live, projected[:, cols], 0.0).astype(BF)
    write(att_ref, att_hbm)

    relay_cotangent(ORDER[3])
    weight_piece(ORDER[3])

    @pl.when(y != 3)
    def _():
        extra_copy().start()

    grad_context = None
    for piece in range(4):
        width = min(PIECE, D - piece * PIECE)
        part = last_last(
            gl[piece, pl.ds(core * 2, 2), :, 0:width].reshape(256, width),
            wf[pl.ds(xl * 2, 2), :, piece * PIECE:piece * PIECE + width].reshape(HALF, width))
        grad_context = part if grad_context is None else grad_context + part
    g_buf[...] = grad_context.astype(BF)
    gt_buf[...] = jnp.transpose(grad_context).astype(BF)

    for step in range(3):
        arrived(ry.at[step], y_rs.at[step])
    total = dw[y].astype(F32) + ry[0].astype(F32) + ry[1].astype(F32) + ry[2].astype(F32)
    sx[...] = total.astype(BF).reshape(8, 4, 16, 128)

    @pl.when(y == 3)
    def _():
        for source in range(3):
            arrived(ryx.at[source], yx_rs.at[source])
        for tile in range(22, 25):
            own = tile - 22
            total = dwx[own].astype(F32)
            for source in range(3):
                total = total + ryx[source, own].astype(F32)
            sx[tile // 4, tile % 4] = total.astype(BF)

    def stays(half, b):
        return (xh == xl) & (xl == half) & (inner == b)

    def quad_copy(n):
        half, b = lax.div(n, 4), lax.rem(n, 4)
        return pltpu.make_async_remote_copy(
            src_ref=sx.at[n], dst_ref=rx.at[xh * 4 + inner], send_sem=x_ss.at[n], recv_sem=x_rs.at[xh * 4 + inner],
            device_id=quad(xl * 2 + half, b), device_id_type=MESH)

    def quad_start(n, carry):
        @pl.when(jnp.logical_not(stays(lax.div(n, 4), lax.rem(n, 4))))
        def _():
            quad_copy(n).start()

        return carry

    def quad_sent(n, carry):
        @pl.when(jnp.logical_not(stays(lax.div(n, 4), lax.rem(n, 4))))
        def _():
            quad_copy(n).wait_send()

        return carry

    def quad_here(n, carry):
        @pl.when(jnp.logical_not((xh == xl) & (n == xh * 4 + inner)))
        def _():
            arrived(rx.at[n], x_rs.at[n])

        return carry

    lax.fori_loop(0, 8, quad_start, 0)

    @pl.when(xh == xl)
    def _():
        rx[xh * 4 + inner] = sx[xl * 4 + inner]

    def backward(head):
        low, high = WINDOWS[head]
        g_head = g_buf[:, low:high] * head_mask(head, 256).astype(BF)
        delta = None
        for part in range(3):
            cols = slice(part * 256, part * 256 + 256)
            grad_prob = plain(g_head, lanes(vw, low, high, part * 2, 2))
            s_buf[:, cols] = grad_prob
            delta = folded(jnp.add, probs[head, :, cols].astype(F32) * grad_prob, delta)
        delta = jnp.sum(delta, axis=1, keepdims=True)
        for part in range(3):
            cols = slice(part * 256, part * 256 + 256)
            ds_buf[:, cols] = (probs[head, :, cols].astype(F32) * (s_buf[:, cols] - delta)).astype(BF)
        rows = slice(head * HEAD, (head + 1) * HEAD)
        first, stop = STRIPES[head]
        dk_acc[rows, :] = stripe(head, plain(lanes(qw, first, stop, 0, 2), ds_buf[...])) * SCALE
        dv_acc[rows, :] = stripe(head, plain(gt_buf[first:stop, :], probs[head]))
        dq_acc[rows, :] = stripe(head, last_last(lanes(kw, first, stop, 0, SLOTS), ds_buf[...])) * SCALE

    def send_terms(piece):
        block = slice(piece * BLOCK, (piece + 1) * BLOCK)
        for side in range(2):
            cols = slice(side * 512, side * 512 + 256)
            kvb[side, piece, 0] = dk_acc[block, cols].astype(BF)
            kvb[side, piece, 1] = dv_acc[block, cols].astype(BF)
            send(kvb.at[side, piece], rkv.at[1 - side, piece], kv_rs.at[1 - side, piece], (behind, ahead)[side])

    backward(0)
    backward(1)
    send_terms(0)
    backward(2)
    backward(3)
    dqw[0] = dq_acc[:, 0:128].astype(BF)
    dqw[1] = dq_acc[:, 128:256].astype(BF)
    send(dqw.at[1 - xl], dqf, dq_rs, partner)
    write(dqw.at[xl], gq_hbm.at[near_rows])

    lax.fori_loop(0, 8, quad_here, 0)
    total = rx[0].astype(F32)
    for source in range(1, 8):
        total = total + rx[source].astype(F32)
    fr[group] = total.astype(BF)
    for step in (2, 1, 3):
        send(fr.at[group], fr.at[group], f_rs.at[group], far(step))

    def sum_terms(piece):
        block = slice(piece * BLOCK, (piece + 1) * BLOCK)
        for side in range(2):
            arrived(rkv.at[side, piece], kv_rs.at[side, piece])
        for which, acc in ((0, dk_acc), (1, dv_acc)):
            value = acc[block, 256:512] + rkv[0, piece, which].astype(F32) + rkv[1, piece, which].astype(F32)
            kvs[0, piece, which] = value[:, 0:128].astype(BF)
            kvs[1, piece, which] = value[:, 128:256].astype(BF)
        send(kvs.at[1 - xl, piece], kvf.at[piece], kvf_rs.at[piece], partner)
        write_terms(kvs.at[xl, piece], xl, piece)

    def write_terms(source, half, piece):
        rows = pl.ds(pl.multiple_of(half * HALF + piece * BLOCK, 16), BLOCK)
        write(source.at[0], gk_hbm.at[rows])
        write(source.at[1], gv_hbm.at[rows])

    sum_terms(0)
    arrived(dqf, dq_rs)
    write(dqf, gq_hbm.at[away_rows])

    for step in range(1, 4):
        source = lax.rem(group + step, 4)
        arrived(fr.at[source], f_rs.at[source])
    total = fr[0].astype(F32) + fr[1].astype(F32) + fr[2].astype(F32) + fr[3].astype(F32)
    gf[spot, inner] = total.astype(BF)

    def spread(j, carry):
        pltpu.make_async_remote_copy(
            src_ref=gf.at[spot, inner], dst_ref=gf.at[spot, inner], send_sem=z_ss.at[0], recv_sem=z_rs.at[0],
            device_id=quad(xh * 2 + xl, lax.rem(inner + j, 4)), device_id_type=MESH).start()
        return carry

    def share(j, carry):
        pltpu.make_async_remote_copy(
            src_ref=gf.at[spot], dst_ref=gf.at[spot], send_sem=z_ss.at[1], recv_sem=z_rs.at[1],
            device_id=around(j), device_id_type=MESH).start()
        return carry

    three = incoming(gf.at[0, pl.ds(0, 3)], z_rs.at[0], z_ss.at[0])
    seven = incoming(gf.at[pl.ds(0, 7)], z_rs.at[1], z_ss.at[1])
    lax.fori_loop(1, 4, spread, 0)
    send_terms(1)
    three.wait_recv()
    lax.fori_loop(1, 8, share, 0)

    sum_terms(1)
    for piece in range(2):
        arrived(kvf.at[piece], kvf_rs.at[piece])
        write_terms(kvf.at[piece], 1 - xl, piece)

    seven.wait_recv()
    write(gf, gw_hbm)
    for copy in sent:
        copy.wait_send()
    @pl.when(y != 3)
    def _():
        extra_copy().wait_send()

    lax.fori_loop(0, 8, quad_sent, 0)
    three.wait_send()
    seven.wait_send()
    for copy in written:
        copy.wait()


def hand_over(att_in, gq_in, gk_in, gv_in, gw_in, att_out, gq_out, gk_out, gv_out, gw_out,
              att, gq, gk, gv, tiles, gw, in_sems, out_sems):
    held = (tiles, att, gq, gk, gv)
    outs = (gw_out, att_out, gq_out, gk_out, gv_out)
    reads = [pltpu.make_async_copy(source, target, in_sems.at[i])
             for i, (source, target) in enumerate(zip((gw_in, att_in, gq_in, gk_in, gv_in), held))]
    writes = [pltpu.make_async_copy(source, target, out_sems.at[i])
              for i, (source, target) in enumerate(zip((gw,) + held[1:], outs))]
    for read in reads:
        read.start()
    for read, copy in list(zip(reads, writes))[1:]:
        read.wait()
        copy.start()
    reads[0].wait()
    for tile in range(TILES):
        row, column = tile % 32 % 11, tile // 32 * 3 + tile % 32 // 11
        if tile >= 96 + 22:
            row, column = 10, (tile - 118) * 3 + 2
        gw[row * 16:row * 16 + 16, column * 128:(column + 1) * 128] = tiles[
            tile // 16, tile // 4 % 4, tile % 4].astype(F32)
    writes[0].start()
    for copy in writes:
        copy.wait()


def per_device(queries, keys, values, patch_ids, counts, cotangent, w_out):
    hbm = pl.BlockSpec(memory_space=pltpu.HBM)
    tiles = (8, 4, 4, 16, 128)
    halves = (2, HALF, ROWS)
    window = (SLOTS, HALF, ROWS)
    dma = pltpu.SemaphoreType.DMA
    scratch = [
        pltpu.VMEM((PLACES, ROWS), jnp.int32), pltpu.SMEM((1, PLACES), jnp.int32), pltpu.VMEM((ROWS, D), BF),
        pltpu.VMEM((ROWS, D), BF),
        pltpu.VMEM(window, BF), pltpu.VMEM(window, BF), pltpu.VMEM(halves, BF), pltpu.VMEM((256, HALF), BF),
        pltpu.VMEM((4, 4, ROWS, PIECE), BF), pltpu.VMEM((4, BLOCK, D), BF),
        pltpu.VMEM((256, 768), F32), pltpu.VMEM((256, 768), F32),
        pltpu.VMEM((4, 256, 768), BF), pltpu.VMEM((256, 768), BF),
        pltpu.VMEM((HALF, 256), F32), pltpu.VMEM((HALF, 256), BF), pltpu.VMEM(halves, BF), pltpu.VMEM((HW, ROWS), BF),
        pltpu.VMEM((2, BLOCK, 256), BF), pltpu.VMEM((256, HALF), BF), pltpu.VMEM((HALF, 256), BF),
        pltpu.VMEM((HALF, 256), F32), pltpu.VMEM((HALF, 768), F32), pltpu.VMEM((HALF, 768), F32),
        pltpu.VMEM(halves, BF), pltpu.VMEM((HALF, ROWS), BF),
        pltpu.VMEM((2, 2, 2, BLOCK, 256), BF), pltpu.VMEM((2, 2, 2, BLOCK, 256), BF),
        pltpu.VMEM((2, 2, 2, BLOCK, ROWS), BF), pltpu.VMEM((2, 2, BLOCK, ROWS), BF),
        pltpu.VMEM((4, 32, 16, 128), BF), pltpu.VMEM((4, 16, 128), BF),
        pltpu.VMEM((3, 32, 16, 128), BF), pltpu.VMEM((3, 3, 16, 128), BF),
        pltpu.VMEM((8, 4, 16, 128), BF), pltpu.VMEM((8, 4, 16, 128), BF),
        pltpu.VMEM((4, 4, 16, 128), BF), pltpu.VMEM(tiles, BF),
        dma((6,)), dma((6,)), dma, dma((4, 4)), dma((4,)), dma((2,)), dma, dma((2, 2)), dma((2,)), dma((3,)), dma((3,)), dma((8,)),
        dma((4,)), dma((2,)),
        dma((40,)), dma, dma((8,)), dma((2,)), dma((7,)), dma((12,)),
    ]
    shapes = (
        jax.ShapeDtypeStruct((ROWS, D), BF),
        jax.ShapeDtypeStruct((HW, ROWS), BF),
        jax.ShapeDtypeStruct((HW, ROWS), BF),
        jax.ShapeDtypeStruct((HW, ROWS), BF),
    )
    outs = pl.pallas_call(
        kernel,
        out_shape=shapes + (jax.ShapeDtypeStruct(tiles, BF),),
        in_specs=[hbm] * 7,
        out_specs=(hbm,) * 5,
        scratch_shapes=scratch,
        compiler_params=pltpu.CompilerParams(
            collective_id=0, has_side_effects=True, vmem_limit_bytes=VMEM_LIMIT),
        cost_estimate=pl.CostEstimate(flops=1500000000, bytes_accessed=4000000, transcendentals=800000),
    )(queries[0].T, keys[0].T, values[0].T, patch_ids.reshape(PLACES, ROWS), counts, cotangent[0], w_out)
    outs = pl.pallas_call(
        hand_over,
        out_shape=shapes + (jax.ShapeDtypeStruct((BLOCK, D), F32),),
        in_specs=[hbm] * 5,
        out_specs=(hbm,) * 5,
        scratch_shapes=[
            pltpu.VMEM((ROWS, D), BF), pltpu.VMEM((HW, ROWS), BF), pltpu.VMEM((HW, ROWS), BF), pltpu.VMEM((HW, ROWS), BF),
            pltpu.VMEM(tiles, BF), pltpu.VMEM((BLOCK, D), F32), dma((5,)), dma((5,))],
        compiler_params=pltpu.CompilerParams(vmem_limit_bytes=VMEM_LIMIT),
    )(*outs)
    attended, grad_queries, grad_keys, grad_values, grad_weight = outs
    return attended[None], grad_queries.T[None], grad_keys.T[None], grad_values.T[None], grad_weight


def solution(mesh):
    placed = (
        P("dp", "ctx", None),
        P("dp", "ctx", None),
        P("dp", "ctx", None),
        P("dp", None),
        P("dp", None),
        P("dp", "ctx", None),
        P("dp", None),
    )
    return jax.shard_map(
        per_device,
        mesh=mesh,
        in_specs=placed,
        out_specs=(
            P("dp", "ctx", None),
            P("dp", "ctx", None),
            P("dp", "ctx", None),
            P("dp", "ctx", None),
            P("dp", None),
        ),
        check_vma=False,
    )
```

```python
import jax
import jax.numpy as jnp
from jax import lax
from jax.experimental import pallas as pl
from jax.experimental.pallas import tpu as pltpu
from jax.sharding import PartitionSpec as P

HEAD = 88
WIN = 4
ROWS = 128
HALF = 352
HW = 704
D = 1408
BLOCK = 176
SLOTS = 6
PLACES = 128
SCALE = HEAD ** -0.5
MASKED = -1e30
TILES = 121
PIECE = 384
ORDER = (1, 3, 2, 0)
VMEM_LIMIT = 61 * 1024 * 1024
MESH = pl.DeviceIdType.MESH
WINDOWS = ((0, 128), (0, 256), (128, 352), (256, 352))
STRIPES = ((0, 96), (80, 176), (176, 272), (256, 352))
BF = jnp.bfloat16
F32 = jnp.float32


def last_last(left, right):
    return lax.dot_general(left, right, (((1,), (1,)), ((), ())), preferred_element_type=F32)


def first_first(left, right):
    return lax.dot_general(left, right, (((0,), (0,)), ((), ())), preferred_element_type=F32)


def plain(left, right):
    return jnp.dot(left, right, preferred_element_type=F32)


def head_mask(head, rows):
    low, high = WINDOWS[head]
    lane = lax.broadcasted_iota(jnp.int32, (rows, high - low), 1) + low
    return jnp.where((lane >= HEAD * head) & (lane < HEAD * (head + 1)), 1.0, 0.0)


def stripe(head, value):
    skip = HEAD * head - STRIPES[head][0]
    return value[skip:skip + HEAD]


def kernel(q_ref, k_ref, v_ref, pid_hbm, cnt_hbm, cot_hbm, w_ref,
           att_hbm, gq_hbm, gk_hbm, gv_hbm, gw_hbm,
           pid_ref, cnt_ref, cot_ref, att_ref,
           kw, vw, qw, qn, gl, wf, bias, s_buf, probs, ds_buf,
           ctx_acc, cb, cw, cf, ct, g_buf, gt_buf, dq_acc, dk_acc, dv_acc, dqw, dqf,
           kvb, rkv, kvs, kvf,
           dw, dwx, ry, ryx, sx, rx, fr, gf,
           k_rs, v_rs, q_rs, gl_rs, w_rs, c_rs, dq_rs, kv_rs, kvf_rs, y_rs, yx_rs, x_rs, f_rs, z_rs,
           ss, y_ss, x_ss, z_ss, in_sems, out_sems):
    dp = lax.axis_index("dp")
    place = lax.axis_index("ctx")
    xh = lax.div(dp, 2)
    core = lax.rem(dp, 2)
    pair = lax.div(place, 2)
    xl = lax.rem(place, 2)
    y = lax.div(place, 32)
    z = lax.rem(pair, 16)
    group = lax.div(z, 4)
    inner = lax.rem(z, 4)
    spot = y * 2 + xl

    partner = (dp, place + 1 - 2 * xl)
    twin = (dp + 1 - 2 * core, place)
    other = lax.rem(dp + 2, 4)
    across = (other, place + 1 - 2 * xl)
    ahead = (dp, lax.rem(place + 2, PLACES))
    behind = (dp, lax.rem(place + PLACES - 2, PLACES))

    def around(j):
        where = lax.rem(spot + j, 8)
        return (dp, lax.div(where, 2) * 32 + z * 2 + lax.rem(where, 2))

    def quad(x, b):
        return (lax.div(x, 2) * 2 + core, (y * 16 + group * 4 + b) * 2 + lax.rem(x, 2))

    def far(j):
        return (dp, (y * 16 + lax.rem(z + 4 * j, 16)) * 2 + xl)

    near_rows = pl.ds(pl.multiple_of(xl * HALF, 16), HALF)
    away_rows = pl.ds(pl.multiple_of((1 - xl) * HALF, 16), HALF)
    written = []

    def write(source, target):
        written.append(pltpu.make_async_copy(source, target, out_sems.at[len(written)]))
        written[-1].start()

    barrier = pltpu.get_barrier_semaphore()

    def greet(device):
        pl.semaphore_signal(barrier, inc=1, device_id=device, device_id_type=MESH)

    def greet_quad(j, carry):
        at = lax.rem((xh * 2 + xl) * 4 + inner + j, 16)
        greet(quad(lax.div(at, 4), lax.rem(at, 4)))
        return carry

    def greet_around(j, carry):
        greet(around(j))
        return carry

    def greet_far(j, carry):
        greet(far(j))
        return carry

    for device in (ahead, behind, twin):
        greet(device)
    lax.fori_loop(1, 4, greet_far, 0)
    lax.fori_loop(1, 16, greet_quad, 0)
    lax.fori_loop(1, 8, greet_around, 0)

    def piece_at(step):
        return lax.rem(y + step, 4)

    fetches = []
    for source, target in (
            (cot_hbm, cot_ref), (cnt_hbm, cnt_ref), (pid_hbm, pid_ref), (k_ref.at[near_rows], kw.at[2 + xl]),
            (q_ref.at[near_rows], qw.at[xl]), (v_ref.at[near_rows], vw.at[2 + xl]), (w_ref, wf.at[dp])):
        fetches.append(pltpu.make_async_copy(source, target, in_sems.at[len(fetches)]))
        fetches[-1].start()

    pl.semaphore_wait(barrier, 28)

    sent = []

    def send(source, target, recv_sem, device):
        copy = pltpu.make_async_remote_copy(
            src_ref=source, dst_ref=target, send_sem=ss.at[len(sent)], recv_sem=recv_sem,
            device_id=device, device_id_type=MESH)
        copy.start()
        sent.append(copy)

    def incoming(ref, recv_sem, send_sem):
        return pltpu.make_async_remote_copy(
            src_ref=ref, dst_ref=ref, send_sem=send_sem, recv_sem=recv_sem,
            device_id=partner, device_id_type=MESH)

    def arrived(ref, recv_sem):
        incoming(ref, recv_sem, ss.at[0]).wait_recv()

    away = 3 - xl
    send(k_ref.at[away_rows], kw.at[2 + xl], k_rs.at[2 + xl], partner)
    send(k_ref.at[near_rows], kw.at[xl], k_rs.at[xl], ahead)
    send(k_ref.at[near_rows], kw.at[4 + xl], k_rs.at[4 + xl], behind)
    send(v_ref.at[away_rows], vw.at[2 + xl], v_rs.at[2 + xl], partner)
    send(v_ref.at[near_rows], vw.at[xl], v_rs.at[xl], ahead)
    send(v_ref.at[near_rows], vw.at[4 + xl], v_rs.at[4 + xl], behind)
    send(q_ref.at[away_rows], qw.at[xl], q_rs, partner)
    fetches[0].wait()
    fetches[1].wait()
    own_live = lax.broadcasted_iota(jnp.int32, (ROWS, 128), 0) < cnt_ref[0, place]
    mine = core * 2 + xl
    for block in range(11):
        cols = slice(block * 128, (block + 1) * 128)
        inside = slice(block % 3 * 128, (block % 3 + 1) * 128)
        gl[block // 3, mine, :, inside] = jnp.where(own_live, cot_ref[:, cols].astype(F32), 0.0).astype(BF)
    gl[3, mine, :, 256:384] = jnp.zeros((ROWS, 128), BF)

    for step in ORDER:
        here = gl.at[piece_at(step), mine]
        send(here, here, gl_rs.at[mine, step], partner)
    send(w_ref, wf.at[dp], w_rs.at[dp], across)
    send(w_ref, wf.at[dp], w_rs.at[dp], twin)
    send(gl.at[:, mine], gl.at[:, mine], gl_rs.at[mine, 0], twin)
    for fetch in fetches[2:]:
        fetch.wait()

    arrived(kw.at[away], k_rs.at[away])
    send(kw.at[away], kw.at[1 - xl], k_rs.at[1 - xl], ahead)
    send(kw.at[away], kw.at[5 - xl], k_rs.at[5 - xl], behind)
    arrived(vw.at[away], v_rs.at[away])
    send(vw.at[away], vw.at[1 - xl], v_rs.at[1 - xl], ahead)
    send(vw.at[away], vw.at[5 - xl], v_rs.at[5 - xl], behind)

    frames, live = [], []
    for slot in range(SLOTS):
        shard = lax.rem(2 * pair - 2 + slot + PLACES, PLACES)
        inside = (2 * pair - 2 + slot >= 0) & (2 * pair - 2 + slot < PLACES)
        count = jnp.where(inside, cnt_ref[0, shard], 0)
        frame = lax.shift_right_logical(pid_ref[pl.ds(shard, 1), :], 8) + 2 * (slot - 2)
        frames.append(frame.astype(F32))
        live.append(lax.broadcasted_iota(jnp.int32, (ROWS, 128), 1) < count)
    for half in range(2):
        column = jnp.transpose(jnp.broadcast_to(frames[2 + half], (ROWS, 128)))
        for slot in range(SLOTS):
            seen = live[slot] & (jnp.abs(frames[slot] - column) <= WIN)
            bias[half * 128:(half + 1) * 128, slot * 128:(slot + 1) * 128] = jnp.where(seen, 0.0, MASKED)

    arrived(qw.at[1 - xl], q_rs)
    for half in range(2):
        qn[half * 128:(half + 1) * 128, :] = jnp.transpose(qw[half].astype(F32)).astype(BF)
    for slot in (0, 1, 4, 5):
        arrived(kw.at[slot], k_rs.at[slot])

    def lanes(ref, low, high, first, slots):
        return jnp.concatenate([ref[first + i, low:high, :] for i in range(slots)], axis=1)

    def folded(op, value, old):
        here = op(value[:, :128], value[:, 128:])
        return here if old is None else op(old, here)

    theirs = core * 2 + 1 - xl

    def relay_cotangent(step):
        here = gl.at[piece_at(step), theirs]
        arrived(here, gl_rs.at[theirs, step])
        send(here, here, gl_rs.at[theirs, step], twin)

    for head in range(4):
        low, high = WINDOWS[head]
        q_head = qn[:, low:high] * head_mask(head, 256).astype(BF)
        top = None
        for part in range(3):
            cols = slice(part * 256, part * 256 + 256)
            score = plain(q_head, lanes(kw, low, high, part * 2, 2)) * SCALE + bias[:, cols]
            s_buf[:, cols] = score
            top = folded(jnp.maximum, score, top)
        top = jnp.max(top, axis=1, keepdims=True)
        total = None
        for part in range(3):
            cols = slice(part * 256, part * 256 + 256)
            expon = jnp.exp(s_buf[:, cols] - top)
            s_buf[:, cols] = expon
            total = folded(jnp.add, expon, total)
        inverse = 1.0 / jnp.sum(total, axis=1, keepdims=True)
        for part in range(3):
            cols = slice(part * 256, part * 256 + 256)
            probs[head, :, cols] = (s_buf[:, cols] * inverse).astype(BF)
    relay_cotangent(ORDER[0])
    for slot in (0, 1, 4, 5):
        arrived(vw.at[slot], v_rs.at[slot])
    for head in range(4):
        ctx_acc[head * HEAD:(head + 1) * HEAD, :] = stripe(
            head, last_last(lanes(vw, *STRIPES[head], 0, SLOTS), probs[head]))
    cb[...] = ctx_acc[...].astype(BF)
    core_rows = pl.ds(pl.multiple_of(core * BLOCK, 16), BLOCK)
    send(cb.at[pl.ds(pl.multiple_of((1 - core) * BLOCK, 16), BLOCK)], ct.at[core], c_rs.at[0], twin)
    cw[0] = cb[:, 0:128]
    cw[1] = cb[:, 128:256]
    ct[core] = cb[core_rows, :]
    cf[near_rows, :] = cw[xl]

    def weight_piece(step):
        piece = piece_at(step)
        there = (1 - core) * 2 + 1 - xl
        arrived(gl.at[piece, there], gl_rs.at[there, step])
        part = plain(context, gl[piece].reshape(512, PIECE))
        for tile in range(33):
            row, column = tile % 11 * 16, tile // 11 * 128
            value = part[row:row + 16, column:column + 128].astype(BF)
            if tile < 32:
                dw[piece, tile] = value
            else:
                dwx[piece] = value
        if step:
            send(dw.at[piece], ry.at[step - 1], y_rs.at[step - 1], (dp, piece * 32 + z * 2 + xl))

    def extra_copy():
        return pltpu.make_async_remote_copy(
            src_ref=dwx.at[pl.ds(0, 3)], dst_ref=ryx.at[y], send_sem=y_ss, recv_sem=yx_rs.at[y],
            device_id=(dp, 96 + z * 2 + xl), device_id_type=MESH)

    relay_cotangent(ORDER[1])
    arrived(gl.at[:, (1 - core) * 2 + xl], gl_rs.at[(1 - core) * 2 + xl, 0])
    arrived(ct.at[1 - core], c_rs.at[0])
    context = jnp.concatenate([ct[0], ct[1]], axis=1)
    weight_piece(ORDER[0])
    weight_piece(ORDER[1])
    arrived(wf.at[other], w_rs.at[other])
    send(wf.at[other], wf.at[other], w_rs.at[other], twin)
    relay_cotangent(ORDER[2])
    weight_piece(ORDER[2])

    relay_cotangent(ORDER[3])
    send(cw.at[1 - xl], cf.at[near_rows], c_rs.at[1], partner)
    weight_piece(ORDER[3])

    @pl.when(y != 3)
    def _():
        extra_copy().start()

    arrived(wf.at[dp + 1 - 2 * core], w_rs.at[dp + 1 - 2 * core])
    arrived(wf.at[other + 1 - 2 * core], w_rs.at[other + 1 - 2 * core])
    grad_context = None
    for piece in range(4):
        width = min(PIECE, D - piece * PIECE)
        part = last_last(
            gl[piece, pl.ds(core * 2, 2), :, 0:width].reshape(256, width),
            wf[pl.ds(xl * 2, 2), :, piece * PIECE:piece * PIECE + width].reshape(HALF, width))
        grad_context = part if grad_context is None else grad_context + part
    g_buf[...] = grad_context.astype(BF)
    gt_buf[...] = jnp.transpose(grad_context).astype(BF)

    for step in range(3):
        arrived(ry.at[step], y_rs.at[step])
    total = dw[y].astype(F32) + ry[0].astype(F32) + ry[1].astype(F32) + ry[2].astype(F32)
    sx[...] = total.astype(BF).reshape(8, 4, 16, 128)

    @pl.when(y == 3)
    def _():
        for source in range(3):
            arrived(ryx.at[source], yx_rs.at[source])
        for tile in range(22, 25):
            own = tile - 22
            total = dwx[own].astype(F32)
            for source in range(3):
                total = total + ryx[source, own].astype(F32)
            sx[tile // 4, tile % 4] = total.astype(BF)

    def stays(half, b):
        return (xh == xl) & (xl == half) & (inner == b)

    def quad_copy(n):
        half, b = lax.div(n, 4), lax.rem(n, 4)
        return pltpu.make_async_remote_copy(
            src_ref=sx.at[n], dst_ref=rx.at[xh * 4 + inner], send_sem=x_ss.at[n], recv_sem=x_rs.at[xh * 4 + inner],
            device_id=quad(xl * 2 + half, b), device_id_type=MESH)

    def quad_start(n, carry):
        @pl.when(jnp.logical_not(stays(lax.div(n, 4), lax.rem(n, 4))))
        def _():
            quad_copy(n).start()

        return carry

    def quad_sent(n, carry):
        @pl.when(jnp.logical_not(stays(lax.div(n, 4), lax.rem(n, 4))))
        def _():
            quad_copy(n).wait_send()

        return carry

    def quad_here(n, carry):
        @pl.when(jnp.logical_not((xh == xl) & (n == xh * 4 + inner)))
        def _():
            arrived(rx.at[n], x_rs.at[n])

        return carry

    lax.fori_loop(0, 8, quad_start, 0)

    @pl.when(xh == xl)
    def _():
        rx[xh * 4 + inner] = sx[xl * 4 + inner]

    def backward(head):
        low, high = WINDOWS[head]
        g_head = g_buf[:, low:high] * head_mask(head, 256).astype(BF)
        delta = None
        for part in range(3):
            cols = slice(part * 256, part * 256 + 256)
            grad_prob = plain(g_head, lanes(vw, low, high, part * 2, 2))
            s_buf[:, cols] = grad_prob
            delta = folded(jnp.add, probs[head, :, cols].astype(F32) * grad_prob, delta)
        delta = jnp.sum(delta, axis=1, keepdims=True)
        for part in range(3):
            cols = slice(part * 256, part * 256 + 256)
            ds_buf[:, cols] = (probs[head, :, cols].astype(F32) * (s_buf[:, cols] - delta)).astype(BF)
        rows = slice(head * HEAD, (head + 1) * HEAD)
        first, stop = STRIPES[head]
        dk_acc[rows, :] = stripe(head, plain(lanes(qw, first, stop, 0, 2), ds_buf[...])) * SCALE
        dv_acc[rows, :] = stripe(head, plain(gt_buf[first:stop, :], probs[head]))
        dq_acc[rows, :] = stripe(head, last_last(lanes(kw, first, stop, 0, SLOTS), ds_buf[...])) * SCALE

    def send_terms(piece):
        block = slice(piece * BLOCK, (piece + 1) * BLOCK)
        for side in range(2):
            cols = slice(side * 512, side * 512 + 256)
            kvb[side, piece, 0] = dk_acc[block, cols].astype(BF)
            kvb[side, piece, 1] = dv_acc[block, cols].astype(BF)
            send(kvb.at[side, piece], rkv.at[1 - side, piece], kv_rs.at[1 - side, piece], (behind, ahead)[side])

    backward(0)
    backward(1)
    send_terms(0)
    backward(2)
    backward(3)
    dqw[0] = dq_acc[:, 0:128].astype(BF)
    dqw[1] = dq_acc[:, 128:256].astype(BF)
    send(dqw.at[1 - xl], dqf, dq_rs, partner)
    write(dqw.at[xl], gq_hbm.at[near_rows])

    arrived(cf.at[away_rows], c_rs.at[1])
    projected = first_first(cf[...], wf[...].reshape(HW, D))
    for block in range(11):
        cols = slice(block * 128, (block + 1) * 128)
        att_ref[:, cols] = jnp.where(own_live, projected[:, cols], 0.0).astype(BF)
    write(att_ref, att_hbm)

    lax.fori_loop(0, 8, quad_here, 0)
    total = rx[0].astype(F32)
    for source in range(1, 8):
        total = total + rx[source].astype(F32)
    fr[group] = total.astype(BF)
    for step in (2, 1, 3):
        send(fr.at[group], fr.at[group], f_rs.at[group], far(step))
    send_terms(1)

    def sum_terms(piece):
        block = slice(piece * BLOCK, (piece + 1) * BLOCK)
        for side in range(2):
            arrived(rkv.at[side, piece], kv_rs.at[side, piece])
        for which, acc in ((0, dk_acc), (1, dv_acc)):
            value = acc[block, 256:512] + rkv[0, piece, which].astype(F32) + rkv[1, piece, which].astype(F32)
            kvs[0, piece, which] = value[:, 0:128].astype(BF)
            kvs[1, piece, which] = value[:, 128:256].astype(BF)
        send(kvs.at[1 - xl, piece], kvf.at[piece], kvf_rs.at[piece], partner)
        write_terms(kvs.at[xl, piece], xl, piece)

    def write_terms(source, half, piece):
        rows = pl.ds(pl.multiple_of(half * HALF + piece * BLOCK, 16), BLOCK)
        write(source.at[0], gk_hbm.at[rows])
        write(source.at[1], gv_hbm.at[rows])

    sum_terms(0)
    arrived(dqf, dq_rs)
    write(dqf, gq_hbm.at[away_rows])

    for step in range(1, 4):
        source = lax.rem(group + step, 4)
        arrived(fr.at[source], f_rs.at[source])
    total = fr[0].astype(F32) + fr[1].astype(F32) + fr[2].astype(F32) + fr[3].astype(F32)
    gf[spot, inner] = total.astype(BF)

    def spread(j, carry):
        pltpu.make_async_remote_copy(
            src_ref=gf.at[spot, inner], dst_ref=gf.at[spot, inner], send_sem=z_ss.at[0], recv_sem=z_rs.at[0],
            device_id=quad(xh * 2 + xl, lax.rem(inner + j, 4)), device_id_type=MESH).start()
        return carry

    def share(j, carry):
        pltpu.make_async_remote_copy(
            src_ref=gf.at[spot], dst_ref=gf.at[spot], send_sem=z_ss.at[1], recv_sem=z_rs.at[1],
            device_id=around(j), device_id_type=MESH).start()
        return carry

    three = incoming(gf.at[0, pl.ds(0, 3)], z_rs.at[0], z_ss.at[0])
    seven = incoming(gf.at[pl.ds(0, 7)], z_rs.at[1], z_ss.at[1])
    lax.fori_loop(1, 4, spread, 0)
    three.wait_recv()
    lax.fori_loop(1, 8, share, 0)

    sum_terms(1)
    for piece in range(2):
        arrived(kvf.at[piece], kvf_rs.at[piece])
        write_terms(kvf.at[piece], 1 - xl, piece)

    seven.wait_recv()
    write(gf, gw_hbm)
    for copy in sent:
        copy.wait_send()
    @pl.when(y != 3)
    def _():
        extra_copy().wait_send()

    lax.fori_loop(0, 8, quad_sent, 0)
    three.wait_send()
    seven.wait_send()
    for copy in written:
        copy.wait()


def hand_over(att_in, gq_in, gk_in, gv_in, gw_in, att_out, gq_out, gk_out, gv_out, gw_out,
              att, gq, gk, gv, tiles, gw, in_sems, out_sems):
    held = (tiles, att, gq, gk, gv)
    outs = (gw_out, att_out, gq_out, gk_out, gv_out)
    reads = [pltpu.make_async_copy(source, target, in_sems.at[i])
             for i, (source, target) in enumerate(zip((gw_in, att_in, gq_in, gk_in, gv_in), held))]
    writes = [pltpu.make_async_copy(source, target, out_sems.at[i])
              for i, (source, target) in enumerate(zip((gw,) + held[1:], outs))]
    for read in reads:
        read.start()
    for read, copy in list(zip(reads, writes))[1:]:
        read.wait()
        copy.start()
    reads[0].wait()
    for tile in range(TILES):
        row, column = tile % 32 % 11, tile // 32 * 3 + tile % 32 // 11
        if tile >= 96 + 22:
            row, column = 10, (tile - 118) * 3 + 2
        gw[row * 16:row * 16 + 16, column * 128:(column + 1) * 128] = tiles[
            tile // 16, tile // 4 % 4, tile % 4].astype(F32)
    writes[0].start()
    for copy in writes:
        copy.wait()


def per_device(queries, keys, values, patch_ids, counts, cotangent, w_out):
    hbm = pl.BlockSpec(memory_space=pltpu.HBM)
    tiles = (8, 4, 4, 16, 128)
    halves = (2, HALF, ROWS)
    window = (SLOTS, HALF, ROWS)
    dma = pltpu.SemaphoreType.DMA
    scratch = [
        pltpu.VMEM((PLACES, ROWS), jnp.int32), pltpu.SMEM((1, PLACES), jnp.int32), pltpu.VMEM((ROWS, D), BF),
        pltpu.VMEM((ROWS, D), BF),
        pltpu.VMEM(window, BF), pltpu.VMEM(window, BF), pltpu.VMEM(halves, BF), pltpu.VMEM((256, HALF), BF),
        pltpu.VMEM((4, 4, ROWS, PIECE), BF), pltpu.VMEM((4, BLOCK, D), BF),
        pltpu.VMEM((256, 768), F32), pltpu.VMEM((256, 768), F32),
        pltpu.VMEM((4, 256, 768), BF), pltpu.VMEM((256, 768), BF),
        pltpu.VMEM((HALF, 256), F32), pltpu.VMEM((HALF, 256), BF), pltpu.VMEM(halves, BF), pltpu.VMEM((HW, ROWS), BF),
        pltpu.VMEM((2, BLOCK, 256), BF), pltpu.VMEM((256, HALF), BF), pltpu.VMEM((HALF, 256), BF),
        pltpu.VMEM((HALF, 256), F32), pltpu.VMEM((HALF, 768), F32), pltpu.VMEM((HALF, 768), F32),
        pltpu.VMEM(halves, BF), pltpu.VMEM((HALF, ROWS), BF),
        pltpu.VMEM((2, 2, 2, BLOCK, 256), BF), pltpu.VMEM((2, 2, 2, BLOCK, 256), BF),
        pltpu.VMEM((2, 2, 2, BLOCK, ROWS), BF), pltpu.VMEM((2, 2, BLOCK, ROWS), BF),
        pltpu.VMEM((4, 32, 16, 128), BF), pltpu.VMEM((4, 16, 128), BF),
        pltpu.VMEM((3, 32, 16, 128), BF), pltpu.VMEM((3, 3, 16, 128), BF),
        pltpu.VMEM((8, 4, 16, 128), BF), pltpu.VMEM((8, 4, 16, 128), BF),
        pltpu.VMEM((4, 4, 16, 128), BF), pltpu.VMEM(tiles, BF),
        dma((6,)), dma((6,)), dma, dma((4, 4)), dma((4,)), dma((2,)), dma, dma((2, 2)), dma((2,)), dma((3,)), dma((3,)), dma((8,)),
        dma((4,)), dma((2,)),
        dma((40,)), dma, dma((8,)), dma((2,)), dma((7,)), dma((12,)),
    ]
    shapes = (
        jax.ShapeDtypeStruct((ROWS, D), BF),
        jax.ShapeDtypeStruct((HW, ROWS), BF),
        jax.ShapeDtypeStruct((HW, ROWS), BF),
        jax.ShapeDtypeStruct((HW, ROWS), BF),
    )
    outs = pl.pallas_call(
        kernel,
        out_shape=shapes + (jax.ShapeDtypeStruct(tiles, BF),),
        in_specs=[hbm] * 7,
        out_specs=(hbm,) * 5,
        scratch_shapes=scratch,
        compiler_params=pltpu.CompilerParams(
            collective_id=0, has_side_effects=True, vmem_limit_bytes=VMEM_LIMIT),
        cost_estimate=pl.CostEstimate(flops=1500000000, bytes_accessed=4000000, transcendentals=800000),
    )(queries[0].T, keys[0].T, values[0].T, patch_ids.reshape(PLACES, ROWS), counts, cotangent[0], w_out)
    outs = pl.pallas_call(
        hand_over,
        out_shape=shapes + (jax.ShapeDtypeStruct((BLOCK, D), F32),),
        in_specs=[hbm] * 5,
        out_specs=(hbm,) * 5,
        scratch_shapes=[
            pltpu.VMEM((ROWS, D), BF), pltpu.VMEM((HW, ROWS), BF), pltpu.VMEM((HW, ROWS), BF), pltpu.VMEM((HW, ROWS), BF),
            pltpu.VMEM(tiles, BF), pltpu.VMEM((BLOCK, D), F32), dma((5,)), dma((5,))],
        compiler_params=pltpu.CompilerParams(vmem_limit_bytes=VMEM_LIMIT),
    )(*outs)
    attended, grad_queries, grad_keys, grad_values, grad_weight = outs
    return attended[None], grad_queries.T[None], grad_keys.T[None], grad_values.T[None], grad_weight


def solution(mesh):
    placed = (
        P("dp", "ctx", None),
        P("dp", "ctx", None),
        P("dp", "ctx", None),
        P("dp", None),
        P("dp", None),
        P("dp", "ctx", None),
        P("dp", None),
    )
    return jax.shard_map(
        per_device,
        mesh=mesh,
        in_specs=placed,
        out_specs=(
            P("dp", "ctx", None),
            P("dp", "ctx", None),
            P("dp", "ctx", None),
            P("dp", "ctx", None),
            P("dp", None),
        ),
        check_vma=False,
    )
```

```python
import jax
import jax.numpy as jnp
from jax import lax
from jax.experimental import pallas as pl
from jax.experimental.pallas import tpu as pltpu
from jax.sharding import PartitionSpec as P

HEAD = 88
WIN = 4
ROWS = 128
HALF = 352
HW = 704
D = 1408
BLOCK = 176
SLOTS = 6
PLACES = 128
SCALE = HEAD ** -0.5
MASKED = -1e30
TILES = 121
PIECE = 384
ORDER = (1, 3, 2, 0)
VMEM_LIMIT = 61 * 1024 * 1024
MESH = pl.DeviceIdType.MESH
WINDOWS = ((0, 128), (0, 256), (128, 352), (256, 352))
STRIPES = ((0, 96), (80, 176), (176, 272), (256, 352))
BF = jnp.bfloat16
F32 = jnp.float32


def last_last(left, right):
    return lax.dot_general(left, right, (((1,), (1,)), ((), ())), preferred_element_type=F32)


def first_first(left, right):
    return lax.dot_general(left, right, (((0,), (0,)), ((), ())), preferred_element_type=F32)


def plain(left, right):
    return jnp.dot(left, right, preferred_element_type=F32)


def head_mask(head, rows):
    low, high = WINDOWS[head]
    lane = lax.broadcasted_iota(jnp.int32, (rows, high - low), 1) + low
    return jnp.where((lane >= HEAD * head) & (lane < HEAD * (head + 1)), 1.0, 0.0)


def stripe(head, value):
    skip = HEAD * head - STRIPES[head][0]
    return value[skip:skip + HEAD]


def kernel(q_ref, k_ref, v_ref, pid_hbm, cnt_hbm, cot_hbm, w_ref,
           att_hbm, gq_hbm, gk_hbm, gv_hbm, gw_hbm,
           pid_ref, cnt_ref, cot_ref, att_ref,
           kw, vw, qw, qn, gl, wf, bias, s_buf, probs, ds_buf,
           ctx_acc, cb, cw, cf, ct, g_buf, gt_buf, dq_acc, dk_acc, dv_acc, dqw, dqf,
           kb, vb, rk, rv, ks, vs, kf, vf,
           dw, dwx, ry, ryx, sx, rx, fr, gf,
           k_rs, v_rs, q_rs, gl_rs, w_rs, c_rs, dq_rs, kt_rs, vt_rs, kf_rs, vf_rs, y_rs, yx_rs, x_rs, f_rs, z_rs,
           ss, y_ss, x_ss, z_ss, in_sems, out_sems):
    dp = lax.axis_index("dp")
    place = lax.axis_index("ctx")
    xh = lax.div(dp, 2)
    core = lax.rem(dp, 2)
    pair = lax.div(place, 2)
    xl = lax.rem(place, 2)
    y = lax.div(place, 32)
    z = lax.rem(pair, 16)
    group = lax.div(z, 4)
    inner = lax.rem(z, 4)
    spot = y * 2 + xl

    partner = (dp, place + 1 - 2 * xl)
    twin = (dp + 1 - 2 * core, place)
    other = lax.rem(dp + 2, 4)
    across = (other, place + 1 - 2 * xl)
    ahead = (dp, lax.rem(place + 2, PLACES))
    behind = (dp, lax.rem(place + PLACES - 2, PLACES))

    def around(j):
        where = lax.rem(spot + j, 8)
        return (dp, lax.div(where, 2) * 32 + z * 2 + lax.rem(where, 2))

    def quad(x, b):
        return (lax.div(x, 2) * 2 + core, (y * 16 + group * 4 + b) * 2 + lax.rem(x, 2))

    def far(j):
        return (dp, (y * 16 + lax.rem(z + 4 * j, 16)) * 2 + xl)

    near_rows = pl.ds(pl.multiple_of(xl * HALF, 16), HALF)
    away_rows = pl.ds(pl.multiple_of((1 - xl) * HALF, 16), HALF)
    written = []

    def write(source, target):
        written.append(pltpu.make_async_copy(source, target, out_sems.at[len(written)]))
        written[-1].start()

    barrier = pltpu.get_barrier_semaphore()

    def greet(device):
        pl.semaphore_signal(barrier, inc=1, device_id=device, device_id_type=MESH)

    def greet_quad(j, carry):
        at = lax.rem((xh * 2 + xl) * 4 + inner + j, 16)
        greet(quad(lax.div(at, 4), lax.rem(at, 4)))
        return carry

    def greet_around(j, carry):
        greet(around(j))
        return carry

    def greet_far(j, carry):
        greet(far(j))
        return carry

    for device in (ahead, behind, twin):
        greet(device)
    lax.fori_loop(1, 4, greet_far, 0)
    lax.fori_loop(1, 16, greet_quad, 0)
    lax.fori_loop(1, 8, greet_around, 0)

    def piece_at(step):
        return lax.rem(y + step, 4)

    fetches = []
    for source, target in (
            (cot_hbm, cot_ref), (cnt_hbm, cnt_ref), (pid_hbm, pid_ref), (k_ref.at[near_rows], kw.at[2 + xl]),
            (q_ref.at[near_rows], qw.at[xl]), (v_ref.at[near_rows], vw.at[2 + xl]), (w_ref, wf.at[dp])):
        fetches.append(pltpu.make_async_copy(source, target, in_sems.at[len(fetches)]))
        fetches[-1].start()

    pl.semaphore_wait(barrier, 28)

    sent = []

    def send(source, target, recv_sem, device):
        copy = pltpu.make_async_remote_copy(
            src_ref=source, dst_ref=target, send_sem=ss.at[len(sent)], recv_sem=recv_sem,
            device_id=device, device_id_type=MESH)
        copy.start()
        sent.append(copy)

    def incoming(ref, recv_sem, send_sem):
        return pltpu.make_async_remote_copy(
            src_ref=ref, dst_ref=ref, send_sem=send_sem, recv_sem=recv_sem,
            device_id=partner, device_id_type=MESH)

    def arrived(ref, recv_sem):
        incoming(ref, recv_sem, ss.at[0]).wait_recv()

    away = 3 - xl
    send(k_ref.at[away_rows], kw.at[2 + xl], k_rs.at[2 + xl], partner)
    send(k_ref.at[near_rows], kw.at[xl], k_rs.at[xl], ahead)
    send(k_ref.at[near_rows], kw.at[4 + xl], k_rs.at[4 + xl], behind)
    send(v_ref.at[away_rows], vw.at[2 + xl], v_rs.at[2 + xl], partner)
    send(v_ref.at[near_rows], vw.at[xl], v_rs.at[xl], ahead)
    send(v_ref.at[near_rows], vw.at[4 + xl], v_rs.at[4 + xl], behind)
    send(q_ref.at[away_rows], qw.at[xl], q_rs, partner)
    fetches[0].wait()
    fetches[1].wait()
    own_live = lax.broadcasted_iota(jnp.int32, (ROWS, 128), 0) < cnt_ref[0, place]
    mine = core * 2 + xl
    for block in range(11):
        cols = slice(block * 128, (block + 1) * 128)
        inside = slice(block % 3 * 128, (block % 3 + 1) * 128)
        gl[block // 3, mine, :, inside] = jnp.where(own_live, cot_ref[:, cols].astype(F32), 0.0).astype(BF)
    gl[3, mine, :, 256:384] = jnp.zeros((ROWS, 128), BF)

    for step in ORDER:
        here = gl.at[piece_at(step), mine]
        send(here, here, gl_rs.at[mine, step], partner)
    send(w_ref, wf.at[dp], w_rs.at[dp], across)
    send(w_ref, wf.at[dp], w_rs.at[dp], twin)
    send(gl.at[:, mine], gl.at[:, mine], gl_rs.at[mine, 0], twin)
    for fetch in fetches[2:]:
        fetch.wait()

    arrived(kw.at[away], k_rs.at[away])
    send(kw.at[away], kw.at[1 - xl], k_rs.at[1 - xl], ahead)
    send(kw.at[away], kw.at[5 - xl], k_rs.at[5 - xl], behind)
    arrived(vw.at[away], v_rs.at[away])
    send(vw.at[away], vw.at[1 - xl], v_rs.at[1 - xl], ahead)
    send(vw.at[away], vw.at[5 - xl], v_rs.at[5 - xl], behind)

    frames, live = [], []
    for slot in range(SLOTS):
        shard = lax.rem(2 * pair - 2 + slot + PLACES, PLACES)
        inside = (2 * pair - 2 + slot >= 0) & (2 * pair - 2 + slot < PLACES)
        count = jnp.where(inside, cnt_ref[0, shard], 0)
        frame = lax.shift_right_logical(pid_ref[pl.ds(shard, 1), :], 8) + 2 * (slot - 2)
        frames.append(frame.astype(F32))
        live.append(lax.broadcasted_iota(jnp.int32, (ROWS, 128), 1) < count)
    for half in range(2):
        column = jnp.transpose(jnp.broadcast_to(frames[2 + half], (ROWS, 128)))
        for slot in range(SLOTS):
            seen = live[slot] & (jnp.abs(frames[slot] - column) <= WIN)
            bias[half * 128:(half + 1) * 128, slot * 128:(slot + 1) * 128] = jnp.where(seen, 0.0, MASKED)

    arrived(qw.at[1 - xl], q_rs)
    for half in range(2):
        qn[half * 128:(half + 1) * 128, :] = jnp.transpose(qw[half].astype(F32)).astype(BF)
    for slot in (0, 1, 4, 5):
        arrived(kw.at[slot], k_rs.at[slot])

    def lanes(ref, low, high, first, slots):
        return jnp.concatenate([ref[first + i, low:high, :] for i in range(slots)], axis=1)

    def folded(op, value, old):
        here = op(value[:, :128], value[:, 128:])
        return here if old is None else op(old, here)

    theirs = core * 2 + 1 - xl

    def relay_cotangent(step):
        here = gl.at[piece_at(step), theirs]
        arrived(here, gl_rs.at[theirs, step])
        send(here, here, gl_rs.at[theirs, step], twin)

    for head in range(4):
        low, high = WINDOWS[head]
        q_head = qn[:, low:high] * head_mask(head, 256).astype(BF)
        top = None
        for part in range(3):
            cols = slice(part * 256, part * 256 + 256)
            score = plain(q_head, lanes(kw, low, high, part * 2, 2)) * SCALE + bias[:, cols]
            s_buf[:, cols] = score
            top = folded(jnp.maximum, score, top)
        top = jnp.max(top, axis=1, keepdims=True)
        total = None
        for part in range(3):
            cols = slice(part * 256, part * 256 + 256)
            expon = jnp.exp(s_buf[:, cols] - top)
            s_buf[:, cols] = expon
            total = folded(jnp.add, expon, total)
        inverse = 1.0 / jnp.sum(total, axis=1, keepdims=True)
        for part in range(3):
            cols = slice(part * 256, part * 256 + 256)
            probs[head, :, cols] = (s_buf[:, cols] * inverse).astype(BF)
    relay_cotangent(ORDER[0])
    for slot in (0, 1, 4, 5):
        arrived(vw.at[slot], v_rs.at[slot])
    for head in range(4):
        ctx_acc[head * HEAD:(head + 1) * HEAD, :] = stripe(
            head, last_last(lanes(vw, *STRIPES[head], 0, SLOTS), probs[head]))
    cb[...] = ctx_acc[...].astype(BF)
    core_rows = pl.ds(pl.multiple_of(core * BLOCK, 16), BLOCK)
    send(cb.at[pl.ds(pl.multiple_of((1 - core) * BLOCK, 16), BLOCK)], ct.at[core], c_rs.at[0], twin)
    cw[0] = cb[:, 0:128]
    cw[1] = cb[:, 128:256]
    ct[core] = cb[core_rows, :]
    cf[near_rows, :] = cw[xl]

    def weight_piece(step):
        piece = piece_at(step)
        there = (1 - core) * 2 + 1 - xl
        arrived(gl.at[piece, there], gl_rs.at[there, step])
        part = plain(context, gl[piece].reshape(512, PIECE))
        for tile in range(33):
            row, column = tile % 11 * 16, tile // 11 * 128
            value = part[row:row + 16, column:column + 128].astype(BF)
            if tile < 32:
                dw[piece, tile] = value
            else:
                dwx[piece] = value
        if step:
            send(dw.at[piece], ry.at[step - 1], y_rs.at[step - 1], (dp, piece * 32 + z * 2 + xl))

    def extra_copy():
        return pltpu.make_async_remote_copy(
            src_ref=dwx.at[pl.ds(0, 3)], dst_ref=ryx.at[y], send_sem=y_ss, recv_sem=yx_rs.at[y],
            device_id=(dp, 96 + z * 2 + xl), device_id_type=MESH)

    relay_cotangent(ORDER[1])
    arrived(gl.at[:, (1 - core) * 2 + xl], gl_rs.at[(1 - core) * 2 + xl, 0])
    arrived(ct.at[1 - core], c_rs.at[0])
    context = jnp.concatenate([ct[0], ct[1]], axis=1)
    weight_piece(ORDER[0])
    weight_piece(ORDER[1])
    arrived(wf.at[other], w_rs.at[other])
    send(wf.at[other], wf.at[other], w_rs.at[other], twin)
    relay_cotangent(ORDER[2])
    weight_piece(ORDER[2])

    relay_cotangent(ORDER[3])
    send(cw.at[1 - xl], cf.at[near_rows], c_rs.at[1], partner)
    weight_piece(ORDER[3])

    @pl.when(y != 3)
    def _():
        extra_copy().start()

    arrived(wf.at[dp + 1 - 2 * core], w_rs.at[dp + 1 - 2 * core])
    arrived(wf.at[other + 1 - 2 * core], w_rs.at[other + 1 - 2 * core])
    grad_context = None
    for piece in range(4):
        width = min(PIECE, D - piece * PIECE)
        part = last_last(
            gl[piece, pl.ds(core * 2, 2), :, 0:width].reshape(256, width),
            wf[pl.ds(xl * 2, 2), :, piece * PIECE:piece * PIECE + width].reshape(HALF, width))
        grad_context = part if grad_context is None else grad_context + part
    g_buf[...] = grad_context.astype(BF)
    gt_buf[...] = jnp.transpose(grad_context).astype(BF)

    for head in range(4):
        first, stop = STRIPES[head]
        dv_acc[head * HEAD:(head + 1) * HEAD, :] = stripe(head, plain(gt_buf[first:stop, :], probs[head]))
    for side in range(2):
        vb[side] = dv_acc[:, side * 512:side * 512 + 256].astype(BF)
        send(vb.at[side], rv.at[1 - side], vt_rs.at[1 - side], (behind, ahead)[side])

    for step in range(3):
        arrived(ry.at[step], y_rs.at[step])
    total = dw[y].astype(F32) + ry[0].astype(F32) + ry[1].astype(F32) + ry[2].astype(F32)
    sx[...] = total.astype(BF).reshape(8, 4, 16, 128)

    @pl.when(y == 3)
    def _():
        for source in range(3):
            arrived(ryx.at[source], yx_rs.at[source])
        for tile in range(22, 25):
            own = tile - 22
            total = dwx[own].astype(F32)
            for source in range(3):
                total = total + ryx[source, own].astype(F32)
            sx[tile // 4, tile % 4] = total.astype(BF)

    def stays(half, b):
        return (xh == xl) & (xl == half) & (inner == b)

    def quad_copy(n):
        half, b = lax.div(n, 4), lax.rem(n, 4)
        return pltpu.make_async_remote_copy(
            src_ref=sx.at[n], dst_ref=rx.at[xh * 4 + inner], send_sem=x_ss.at[n], recv_sem=x_rs.at[xh * 4 + inner],
            device_id=quad(xl * 2 + half, b), device_id_type=MESH)

    def quad_start(n, carry):
        @pl.when(jnp.logical_not(stays(lax.div(n, 4), lax.rem(n, 4))))
        def _():
            quad_copy(n).start()

        return carry

    def quad_sent(n, carry):
        @pl.when(jnp.logical_not(stays(lax.div(n, 4), lax.rem(n, 4))))
        def _():
            quad_copy(n).wait_send()

        return carry

    def quad_here(n, carry):
        @pl.when(jnp.logical_not((xh == xl) & (n == xh * 4 + inner)))
        def _():
            arrived(rx.at[n], x_rs.at[n])

        return carry

    lax.fori_loop(0, 8, quad_start, 0)

    @pl.when(xh == xl)
    def _():
        rx[xh * 4 + inner] = sx[xl * 4 + inner]

    def backward(head):
        low, high = WINDOWS[head]
        g_head = g_buf[:, low:high] * head_mask(head, 256).astype(BF)
        delta = None
        for part in range(3):
            cols = slice(part * 256, part * 256 + 256)
            grad_prob = plain(g_head, lanes(vw, low, high, part * 2, 2))
            s_buf[:, cols] = grad_prob
            delta = folded(jnp.add, probs[head, :, cols].astype(F32) * grad_prob, delta)
        delta = jnp.sum(delta, axis=1, keepdims=True)
        for part in range(3):
            cols = slice(part * 256, part * 256 + 256)
            ds_buf[:, cols] = (probs[head, :, cols].astype(F32) * (s_buf[:, cols] - delta)).astype(BF)
        rows = slice(head * HEAD, (head + 1) * HEAD)
        first, stop = STRIPES[head]
        dk_acc[rows, :] = stripe(head, plain(lanes(qw, first, stop, 0, 2), ds_buf[...])) * SCALE
        dq_acc[rows, :] = stripe(head, last_last(lanes(kw, first, stop, 0, SLOTS), ds_buf[...])) * SCALE

    def send_terms(piece):
        block = slice(piece * BLOCK, (piece + 1) * BLOCK)
        for side in range(2):
            cols = slice(side * 512, side * 512 + 256)
            kb[side, piece] = dk_acc[block, cols].astype(BF)
            send(kb.at[side, piece], rk.at[1 - side, piece], kt_rs.at[1 - side, piece], (behind, ahead)[side])

    backward(0)
    backward(1)
    send_terms(0)
    backward(2)
    backward(3)
    dqw[0] = dq_acc[:, 0:128].astype(BF)
    dqw[1] = dq_acc[:, 128:256].astype(BF)
    send(dqw.at[1 - xl], dqf, dq_rs, partner)
    write(dqw.at[xl], gq_hbm.at[near_rows])

    arrived(cf.at[away_rows], c_rs.at[1])
    projected = first_first(cf[...], wf[...].reshape(HW, D))
    for block in range(11):
        cols = slice(block * 128, (block + 1) * 128)
        att_ref[:, cols] = jnp.where(own_live, projected[:, cols], 0.0).astype(BF)
    write(att_ref, att_hbm)

    lax.fori_loop(0, 8, quad_here, 0)
    total = rx[0].astype(F32)
    for source in range(1, 8):
        total = total + rx[source].astype(F32)
    fr[group] = total.astype(BF)
    for step in (2, 1, 3):
        send(fr.at[group], fr.at[group], f_rs.at[group], far(step))
    send_terms(1)

    def sum_values():
        for side in range(2):
            arrived(rv.at[side], vt_rs.at[side])
        value = dv_acc[:, 256:512] + rv[0].astype(F32) + rv[1].astype(F32)
        vs[0] = value[:, 0:128].astype(BF)
        vs[1] = value[:, 128:256].astype(BF)
        send(vs.at[1 - xl], vf, vf_rs, partner)
        write(vs.at[xl], gv_hbm.at[near_rows])

    def key_rows(half, piece):
        return gk_hbm.at[pl.ds(pl.multiple_of(half * HALF + piece * BLOCK, 16), BLOCK)]

    def sum_keys(piece):
        block = slice(piece * BLOCK, (piece + 1) * BLOCK)
        for side in range(2):
            arrived(rk.at[side, piece], kt_rs.at[side, piece])
        value = dk_acc[block, 256:512] + rk[0, piece].astype(F32) + rk[1, piece].astype(F32)
        ks[0, piece] = value[:, 0:128].astype(BF)
        ks[1, piece] = value[:, 128:256].astype(BF)
        send(ks.at[1 - xl, piece], kf.at[piece], kf_rs.at[piece], partner)
        write(ks.at[xl, piece], key_rows(xl, piece))

    sum_values()
    sum_keys(0)
    arrived(dqf, dq_rs)
    write(dqf, gq_hbm.at[away_rows])

    for step in range(1, 4):
        source = lax.rem(group + step, 4)
        arrived(fr.at[source], f_rs.at[source])
    total = fr[0].astype(F32) + fr[1].astype(F32) + fr[2].astype(F32) + fr[3].astype(F32)
    gf[spot, inner] = total.astype(BF)

    def spread(j, carry):
        pltpu.make_async_remote_copy(
            src_ref=gf.at[spot, inner], dst_ref=gf.at[spot, inner], send_sem=z_ss.at[0], recv_sem=z_rs.at[0],
            device_id=quad(xh * 2 + xl, lax.rem(inner + j, 4)), device_id_type=MESH).start()
        return carry

    def share(j, carry):
        pltpu.make_async_remote_copy(
            src_ref=gf.at[spot], dst_ref=gf.at[spot], send_sem=z_ss.at[1], recv_sem=z_rs.at[1],
            device_id=around(j), device_id_type=MESH).start()
        return carry

    three = incoming(gf.at[0, pl.ds(0, 3)], z_rs.at[0], z_ss.at[0])
    seven = incoming(gf.at[pl.ds(0, 7)], z_rs.at[1], z_ss.at[1])
    lax.fori_loop(1, 4, spread, 0)
    sum_keys(1)
    three.wait_recv()
    lax.fori_loop(1, 8, share, 0)

    arrived(vf, vf_rs)
    write(vf, gv_hbm.at[away_rows])
    for piece in range(2):
        arrived(kf.at[piece], kf_rs.at[piece])
        write(kf.at[piece], key_rows(1 - xl, piece))

    seven.wait_recv()
    write(gf, gw_hbm)
    for copy in sent:
        copy.wait_send()
    @pl.when(y != 3)
    def _():
        extra_copy().wait_send()

    lax.fori_loop(0, 8, quad_sent, 0)
    three.wait_send()
    seven.wait_send()
    for copy in written:
        copy.wait()


def hand_over(att_in, gq_in, gk_in, gv_in, gw_in, att_out, gq_out, gk_out, gv_out, gw_out,
              att, gq, gk, gv, tiles, gw, in_sems, out_sems):
    held = (tiles, att, gq, gk, gv)
    outs = (gw_out, att_out, gq_out, gk_out, gv_out)
    reads = [pltpu.make_async_copy(source, target, in_sems.at[i])
             for i, (source, target) in enumerate(zip((gw_in, att_in, gq_in, gk_in, gv_in), held))]
    writes = [pltpu.make_async_copy(source, target, out_sems.at[i])
              for i, (source, target) in enumerate(zip((gw,) + held[1:], outs))]
    for read in reads:
        read.start()
    for read, copy in list(zip(reads, writes))[1:]:
        read.wait()
        copy.start()
    reads[0].wait()
    for tile in range(TILES):
        row, column = tile % 32 % 11, tile // 32 * 3 + tile % 32 // 11
        if tile >= 96 + 22:
            row, column = 10, (tile - 118) * 3 + 2
        gw[row * 16:row * 16 + 16, column * 128:(column + 1) * 128] = tiles[
            tile // 16, tile // 4 % 4, tile % 4].astype(F32)
    writes[0].start()
    for copy in writes:
        copy.wait()


def per_device(queries, keys, values, patch_ids, counts, cotangent, w_out):
    hbm = pl.BlockSpec(memory_space=pltpu.HBM)
    tiles = (8, 4, 4, 16, 128)
    halves = (2, HALF, ROWS)
    window = (SLOTS, HALF, ROWS)
    dma = pltpu.SemaphoreType.DMA
    scratch = [
        pltpu.VMEM((PLACES, ROWS), jnp.int32), pltpu.SMEM((1, PLACES), jnp.int32), pltpu.VMEM((ROWS, D), BF),
        pltpu.VMEM((ROWS, D), BF),
        pltpu.VMEM(window, BF), pltpu.VMEM(window, BF), pltpu.VMEM(halves, BF), pltpu.VMEM((256, HALF), BF),
        pltpu.VMEM((4, 4, ROWS, PIECE), BF), pltpu.VMEM((4, BLOCK, D), BF),
        pltpu.VMEM((256, 768), F32), pltpu.VMEM((256, 768), F32),
        pltpu.VMEM((4, 256, 768), BF), pltpu.VMEM((256, 768), BF),
        pltpu.VMEM((HALF, 256), F32), pltpu.VMEM((HALF, 256), BF), pltpu.VMEM(halves, BF), pltpu.VMEM((HW, ROWS), BF),
        pltpu.VMEM((2, BLOCK, 256), BF), pltpu.VMEM((256, HALF), BF), pltpu.VMEM((HALF, 256), BF),
        pltpu.VMEM((HALF, 256), F32), pltpu.VMEM((HALF, 768), F32), pltpu.VMEM((HALF, 768), F32),
        pltpu.VMEM(halves, BF), pltpu.VMEM((HALF, ROWS), BF),
        pltpu.VMEM((2, 2, BLOCK, 256), BF), pltpu.VMEM((2, HALF, 256), BF),
        pltpu.VMEM((2, 2, BLOCK, 256), BF), pltpu.VMEM((2, HALF, 256), BF),
        pltpu.VMEM((2, 2, BLOCK, ROWS), BF), pltpu.VMEM(halves, BF),
        pltpu.VMEM((2, BLOCK, ROWS), BF), pltpu.VMEM((HALF, ROWS), BF),
        pltpu.VMEM((4, 32, 16, 128), BF), pltpu.VMEM((4, 16, 128), BF),
        pltpu.VMEM((3, 32, 16, 128), BF), pltpu.VMEM((3, 3, 16, 128), BF),
        pltpu.VMEM((8, 4, 16, 128), BF), pltpu.VMEM((8, 4, 16, 128), BF),
        pltpu.VMEM((4, 4, 16, 128), BF), pltpu.VMEM(tiles, BF),
        dma((6,)), dma((6,)), dma, dma((4, 4)), dma((4,)), dma((2,)), dma, dma((2, 2)), dma((2,)), dma((2,)), dma,
        dma((3,)), dma((3,)), dma((8,)),
        dma((4,)), dma((2,)),
        dma((48,)), dma, dma((8,)), dma((2,)), dma((7,)), dma((12,)),
    ]
    shapes = (
        jax.ShapeDtypeStruct((ROWS, D), BF),
        jax.ShapeDtypeStruct((HW, ROWS), BF),
        jax.ShapeDtypeStruct((HW, ROWS), BF),
        jax.ShapeDtypeStruct((HW, ROWS), BF),
    )
    outs = pl.pallas_call(
        kernel,
        out_shape=shapes + (jax.ShapeDtypeStruct(tiles, BF),),
        in_specs=[hbm] * 7,
        out_specs=(hbm,) * 5,
        scratch_shapes=scratch,
        compiler_params=pltpu.CompilerParams(
            collective_id=0, has_side_effects=True, vmem_limit_bytes=VMEM_LIMIT),
        cost_estimate=pl.CostEstimate(flops=1500000000, bytes_accessed=4000000, transcendentals=800000),
    )(queries[0].T, keys[0].T, values[0].T, patch_ids.reshape(PLACES, ROWS), counts, cotangent[0], w_out)
    outs = pl.pallas_call(
        hand_over,
        out_shape=shapes + (jax.ShapeDtypeStruct((BLOCK, D), F32),),
        in_specs=[hbm] * 5,
        out_specs=(hbm,) * 5,
        scratch_shapes=[
            pltpu.VMEM((ROWS, D), BF), pltpu.VMEM((HW, ROWS), BF), pltpu.VMEM((HW, ROWS), BF), pltpu.VMEM((HW, ROWS), BF),
            pltpu.VMEM(tiles, BF), pltpu.VMEM((BLOCK, D), F32), dma((5,)), dma((5,))],
        compiler_params=pltpu.CompilerParams(vmem_limit_bytes=VMEM_LIMIT),
    )(*outs)
    attended, grad_queries, grad_keys, grad_values, grad_weight = outs
    return attended[None], grad_queries.T[None], grad_keys.T[None], grad_values.T[None], grad_weight


def solution(mesh):
    placed = (
        P("dp", "ctx", None),
        P("dp", "ctx", None),
        P("dp", "ctx", None),
        P("dp", None),
        P("dp", None),
        P("dp", "ctx", None),
        P("dp", None),
    )
    return jax.shard_map(
        per_device,
        mesh=mesh,
        in_specs=placed,
        out_specs=(
            P("dp", "ctx", None),
            P("dp", "ctx", None),
            P("dp", "ctx", None),
            P("dp", "ctx", None),
            P("dp", None),
        ),
        check_vma=False,
    )
```

```python
import jax
import jax.numpy as jnp
from jax import lax
from jax.experimental import pallas as pl
from jax.experimental.pallas import tpu as pltpu
from jax.sharding import PartitionSpec as P

HEAD = 88
WIN = 4
ROWS = 128
HALF = 352
HW = 704
D = 1408
BLOCK = 176
SLOTS = 6
PLACES = 128
SCALE = HEAD ** -0.5
MASKED = -1e30
TILES = 121
PIECE = 384
ORDER = (1, 3, 2, 0)
VMEM_LIMIT = 61 * 1024 * 1024
MESH = pl.DeviceIdType.MESH
WINDOWS = ((0, 128), (0, 256), (128, 352), (256, 352))
STRIPES = ((0, 96), (80, 176), (176, 272), (256, 352))
BF = jnp.bfloat16
F32 = jnp.float32


def last_last(left, right):
    return lax.dot_general(left, right, (((1,), (1,)), ((), ())), preferred_element_type=F32)


def first_first(left, right):
    return lax.dot_general(left, right, (((0,), (0,)), ((), ())), preferred_element_type=F32)


def plain(left, right):
    return jnp.dot(left, right, preferred_element_type=F32)


def head_mask(head, rows):
    low, high = WINDOWS[head]
    lane = lax.broadcasted_iota(jnp.int32, (rows, high - low), 1) + low
    return jnp.where((lane >= HEAD * head) & (lane < HEAD * (head + 1)), 1.0, 0.0)


def stripe(head, value):
    skip = HEAD * head - STRIPES[head][0]
    return value[skip:skip + HEAD]


def kernel(q_ref, k_ref, v_ref, pid_hbm, cnt_hbm, cot_hbm, w_ref,
           att_hbm, gq_hbm, gk_hbm, gv_hbm, gw_hbm,
           pid_ref, cnt_ref, cot_ref, att_ref,
           kw, vw, qw, qn, gl, wf, bias, s_buf, probs, ds_buf,
           ctx_acc, cb, cw, cf, ct, g_buf, gt_buf, dq_acc, dk_acc, dv_acc, dqw, dqf,
           kb, vb, rk, rv, ks, vs, kf, vf,
           dw, dwx, ry, ryx, sx, rx, fr, gf,
           k_rs, v_rs, q_rs, gl_rs, w_rs, c_rs, dq_rs, kt_rs, vt_rs, kf_rs, vf_rs, y_rs, yx_rs, x_rs, f_rs, z_rs,
           ss, y_ss, x_ss, z_ss, in_sems, out_sems):
    dp = lax.axis_index("dp")
    place = lax.axis_index("ctx")
    xh = lax.div(dp, 2)
    core = lax.rem(dp, 2)
    pair = lax.div(place, 2)
    xl = lax.rem(place, 2)
    y = lax.div(place, 32)
    z = lax.rem(pair, 16)
    group = lax.div(z, 4)
    inner = lax.rem(z, 4)
    spot = y * 2 + xl

    partner = (dp, place + 1 - 2 * xl)
    twin = (dp + 1 - 2 * core, place)
    other = lax.rem(dp + 2, 4)
    across = (other, place + 1 - 2 * xl)
    ahead = (dp, lax.rem(place + 2, PLACES))
    behind = (dp, lax.rem(place + PLACES - 2, PLACES))

    def around(j):
        where = lax.rem(spot + j, 8)
        return (dp, lax.div(where, 2) * 32 + z * 2 + lax.rem(where, 2))

    def quad(x, b):
        return (lax.div(x, 2) * 2 + core, (y * 16 + group * 4 + b) * 2 + lax.rem(x, 2))

    def far(j):
        return (dp, (y * 16 + lax.rem(z + 4 * j, 16)) * 2 + xl)

    near_rows = pl.ds(pl.multiple_of(xl * HALF, 16), HALF)
    away_rows = pl.ds(pl.multiple_of((1 - xl) * HALF, 16), HALF)
    written = []

    def write(source, target):
        written.append(pltpu.make_async_copy(source, target, out_sems.at[len(written)]))
        written[-1].start()

    barrier = pltpu.get_barrier_semaphore()

    def greet(device):
        pl.semaphore_signal(barrier, inc=1, device_id=device, device_id_type=MESH)

    def greet_quad(j, carry):
        at = lax.rem((xh * 2 + xl) * 4 + inner + j, 16)
        greet(quad(lax.div(at, 4), lax.rem(at, 4)))
        return carry

    def greet_around(j, carry):
        greet(around(j))
        return carry

    def greet_far(j, carry):
        greet(far(j))
        return carry

    for device in (ahead, behind, twin):
        greet(device)
    lax.fori_loop(1, 4, greet_far, 0)
    lax.fori_loop(1, 16, greet_quad, 0)
    lax.fori_loop(1, 8, greet_around, 0)

    def piece_at(step):
        return lax.rem(y + step, 4)

    fetches = []
    for source, target in (
            (cot_hbm, cot_ref), (cnt_hbm, cnt_ref), (pid_hbm, pid_ref), (k_ref.at[near_rows], kw.at[2 + xl]),
            (q_ref.at[near_rows], qw.at[xl]), (v_ref.at[near_rows], vw.at[2 + xl]), (w_ref, wf.at[dp])):
        fetches.append(pltpu.make_async_copy(source, target, in_sems.at[len(fetches)]))
        fetches[-1].start()

    pl.semaphore_wait(barrier, 28)

    sent = []

    def send(source, target, recv_sem, device):
        copy = pltpu.make_async_remote_copy(
            src_ref=source, dst_ref=target, send_sem=ss.at[len(sent)], recv_sem=recv_sem,
            device_id=device, device_id_type=MESH)
        copy.start()
        sent.append(copy)

    def incoming(ref, recv_sem, send_sem):
        return pltpu.make_async_remote_copy(
            src_ref=ref, dst_ref=ref, send_sem=send_sem, recv_sem=recv_sem,
            device_id=partner, device_id_type=MESH)

    def arrived(ref, recv_sem):
        incoming(ref, recv_sem, ss.at[0]).wait_recv()

    away = 3 - xl
    send(k_ref.at[away_rows], kw.at[2 + xl], k_rs.at[2 + xl], partner)
    send(k_ref.at[near_rows], kw.at[xl], k_rs.at[xl], ahead)
    send(k_ref.at[near_rows], kw.at[4 + xl], k_rs.at[4 + xl], behind)
    send(v_ref.at[away_rows], vw.at[2 + xl], v_rs.at[2 + xl], partner)
    send(v_ref.at[near_rows], vw.at[xl], v_rs.at[xl], ahead)
    send(v_ref.at[near_rows], vw.at[4 + xl], v_rs.at[4 + xl], behind)
    send(q_ref.at[away_rows], qw.at[xl], q_rs, partner)
    fetches[0].wait()
    fetches[1].wait()
    own_live = lax.broadcasted_iota(jnp.int32, (ROWS, 128), 0) < cnt_ref[0, place]
    mine = core * 2 + xl
    for block in range(11):
        cols = slice(block * 128, (block + 1) * 128)
        inside = slice(block % 3 * 128, (block % 3 + 1) * 128)
        gl[block // 3, mine, :, inside] = jnp.where(own_live, cot_ref[:, cols].astype(F32), 0.0).astype(BF)
    gl[3, mine, :, 256:384] = jnp.zeros((ROWS, 128), BF)

    for step in ORDER:
        here = gl.at[piece_at(step), mine]
        send(here, here, gl_rs.at[mine, step], partner)
    send(w_ref, wf.at[dp], w_rs.at[dp], across)
    send(w_ref, wf.at[dp], w_rs.at[dp], twin)
    send(gl.at[:, mine], gl.at[:, mine], gl_rs.at[mine, 0], twin)
    for fetch in fetches[2:]:
        fetch.wait()

    arrived(kw.at[away], k_rs.at[away])
    send(kw.at[away], kw.at[1 - xl], k_rs.at[1 - xl], ahead)
    send(kw.at[away], kw.at[5 - xl], k_rs.at[5 - xl], behind)
    arrived(vw.at[away], v_rs.at[away])
    send(vw.at[away], vw.at[1 - xl], v_rs.at[1 - xl], ahead)
    send(vw.at[away], vw.at[5 - xl], v_rs.at[5 - xl], behind)

    frames, live = [], []
    for slot in range(SLOTS):
        shard = lax.rem(2 * pair - 2 + slot + PLACES, PLACES)
        inside = (2 * pair - 2 + slot >= 0) & (2 * pair - 2 + slot < PLACES)
        count = jnp.where(inside, cnt_ref[0, shard], 0)
        frame = lax.shift_right_logical(pid_ref[pl.ds(shard, 1), :], 8) + 2 * (slot - 2)
        frames.append(frame.astype(F32))
        live.append(lax.broadcasted_iota(jnp.int32, (ROWS, 128), 1) < count)
    for half in range(2):
        column = jnp.transpose(jnp.broadcast_to(frames[2 + half], (ROWS, 128)))
        for slot in range(SLOTS):
            seen = live[slot] & (jnp.abs(frames[slot] - column) <= WIN)
            bias[half * 128:(half + 1) * 128, slot * 128:(slot + 1) * 128] = jnp.where(seen, 0.0, MASKED)

    arrived(qw.at[1 - xl], q_rs)
    for half in range(2):
        qn[half * 128:(half + 1) * 128, :] = jnp.transpose(qw[half].astype(F32)).astype(BF)
    for slot in (0, 1, 4, 5):
        arrived(kw.at[slot], k_rs.at[slot])

    def lanes(ref, low, high, first, slots):
        return jnp.concatenate([ref[first + i, low:high, :] for i in range(slots)], axis=1)

    def folded(op, value, old):
        here = op(value[:, :128], value[:, 128:])
        return here if old is None else op(old, here)

    theirs = core * 2 + 1 - xl

    def relay_cotangent(step):
        here = gl.at[piece_at(step), theirs]
        arrived(here, gl_rs.at[theirs, step])
        send(here, here, gl_rs.at[theirs, step], twin)

    for head in range(4):
        low, high = WINDOWS[head]
        q_head = qn[:, low:high] * head_mask(head, 256).astype(BF)
        top = None
        for part in range(3):
            cols = slice(part * 256, part * 256 + 256)
            score = plain(q_head, lanes(kw, low, high, part * 2, 2)) * SCALE + bias[:, cols]
            s_buf[:, cols] = score
            top = folded(jnp.maximum, score, top)
        top = jnp.max(top, axis=1, keepdims=True)
        total = None
        for part in range(3):
            cols = slice(part * 256, part * 256 + 256)
            expon = jnp.exp(s_buf[:, cols] - top)
            s_buf[:, cols] = expon
            total = folded(jnp.add, expon, total)
        inverse = 1.0 / jnp.sum(total, axis=1, keepdims=True)
        for part in range(3):
            cols = slice(part * 256, part * 256 + 256)
            probs[head, :, cols] = (s_buf[:, cols] * inverse).astype(BF)
    relay_cotangent(ORDER[0])
    for slot in (0, 1, 4, 5):
        arrived(vw.at[slot], v_rs.at[slot])
    for head in range(4):
        ctx_acc[head * HEAD:(head + 1) * HEAD, :] = stripe(
            head, last_last(lanes(vw, *STRIPES[head], 0, SLOTS), probs[head]))
    cb[...] = ctx_acc[...].astype(BF)
    core_rows = pl.ds(pl.multiple_of(core * BLOCK, 16), BLOCK)
    send(cb.at[pl.ds(pl.multiple_of((1 - core) * BLOCK, 16), BLOCK)], ct.at[core], c_rs.at[0], twin)
    cw[0] = cb[:, 0:128]
    cw[1] = cb[:, 128:256]
    ct[core] = cb[core_rows, :]
    cf[near_rows, :] = cw[xl]

    def weight_piece(step):
        piece = piece_at(step)
        there = (1 - core) * 2 + 1 - xl
        arrived(gl.at[piece, there], gl_rs.at[there, step])
        part = plain(context, gl[piece].reshape(512, PIECE))
        for tile in range(33):
            row, column = tile % 11 * 16, tile // 11 * 128
            value = part[row:row + 16, column:column + 128].astype(BF)
            if tile < 32:
                dw[piece, tile] = value
            else:
                dwx[piece] = value
        if step:
            send(dw.at[piece], ry.at[step - 1], y_rs.at[step - 1], (dp, piece * 32 + z * 2 + xl))

    def extra_copy():
        return pltpu.make_async_remote_copy(
            src_ref=dwx.at[pl.ds(0, 3)], dst_ref=ryx.at[y], send_sem=y_ss, recv_sem=yx_rs.at[y],
            device_id=(dp, 96 + z * 2 + xl), device_id_type=MESH)

    relay_cotangent(ORDER[1])
    arrived(gl.at[:, (1 - core) * 2 + xl], gl_rs.at[(1 - core) * 2 + xl, 0])
    arrived(ct.at[1 - core], c_rs.at[0])
    context = jnp.concatenate([ct[0], ct[1]], axis=1)
    weight_piece(ORDER[0])
    weight_piece(ORDER[1])
    arrived(wf.at[other], w_rs.at[other])
    send(wf.at[other], wf.at[other], w_rs.at[other], twin)
    relay_cotangent(ORDER[2])
    weight_piece(ORDER[2])

    relay_cotangent(ORDER[3])
    send(cw.at[1 - xl], cf.at[near_rows], c_rs.at[1], partner)
    weight_piece(ORDER[3])

    @pl.when(y != 3)
    def _():
        extra_copy().start()

    arrived(wf.at[dp + 1 - 2 * core], w_rs.at[dp + 1 - 2 * core])
    arrived(wf.at[other + 1 - 2 * core], w_rs.at[other + 1 - 2 * core])
    grad_context = None
    for piece in range(4):
        width = min(PIECE, D - piece * PIECE)
        part = last_last(
            gl[piece, pl.ds(core * 2, 2), :, 0:width].reshape(256, width),
            wf[pl.ds(xl * 2, 2), :, piece * PIECE:piece * PIECE + width].reshape(HALF, width))
        grad_context = part if grad_context is None else grad_context + part
    g_buf[...] = grad_context.astype(BF)
    gt_buf[...] = jnp.transpose(grad_context).astype(BF)

    for head in range(4):
        first, stop = STRIPES[head]
        dv_acc[head * HEAD:(head + 1) * HEAD, :] = stripe(head, plain(gt_buf[first:stop, :], probs[head]))
    for side in range(2):
        vb[side] = dv_acc[:, side * 512:side * 512 + 256].astype(BF)
        send(vb.at[side], rv.at[1 - side], vt_rs.at[1 - side], (behind, ahead)[side])

    for step in range(3):
        arrived(ry.at[step], y_rs.at[step])
    total = dw[y].astype(F32) + ry[0].astype(F32) + ry[1].astype(F32) + ry[2].astype(F32)
    sx[...] = total.astype(BF).reshape(8, 4, 16, 128)

    @pl.when(y == 3)
    def _():
        for source in range(3):
            arrived(ryx.at[source], yx_rs.at[source])
        for tile in range(22, 25):
            own = tile - 22
            total = dwx[own].astype(F32)
            for source in range(3):
                total = total + ryx[source, own].astype(F32)
            sx[tile // 4, tile % 4] = total.astype(BF)

    def stays(half, b):
        return (xh == xl) & (xl == half) & (inner == b)

    def quad_copy(n):
        half, b = lax.div(n, 4), lax.rem(n, 4)
        return pltpu.make_async_remote_copy(
            src_ref=sx.at[n], dst_ref=rx.at[xh * 4 + inner], send_sem=x_ss.at[n], recv_sem=x_rs.at[xh * 4 + inner],
            device_id=quad(xl * 2 + half, b), device_id_type=MESH)

    def quad_start(n, carry):
        @pl.when(jnp.logical_not(stays(lax.div(n, 4), lax.rem(n, 4))))
        def _():
            quad_copy(n).start()

        return carry

    def quad_sent(n, carry):
        @pl.when(jnp.logical_not(stays(lax.div(n, 4), lax.rem(n, 4))))
        def _():
            quad_copy(n).wait_send()

        return carry

    def quad_here(n, carry):
        @pl.when(jnp.logical_not((xh == xl) & (n == xh * 4 + inner)))
        def _():
            arrived(rx.at[n], x_rs.at[n])

        return carry

    lax.fori_loop(0, 8, quad_start, 0)

    @pl.when(xh == xl)
    def _():
        rx[xh * 4 + inner] = sx[xl * 4 + inner]

    def backward(head):
        low, high = WINDOWS[head]
        g_head = g_buf[:, low:high] * head_mask(head, 256).astype(BF)
        delta = None
        for part in range(3):
            cols = slice(part * 256, part * 256 + 256)
            grad_prob = plain(g_head, lanes(vw, low, high, part * 2, 2))
            s_buf[:, cols] = grad_prob
            delta = folded(jnp.add, probs[head, :, cols].astype(F32) * grad_prob, delta)
        delta = jnp.sum(delta, axis=1, keepdims=True)
        for part in range(3):
            cols = slice(part * 256, part * 256 + 256)
            ds_buf[:, cols] = (probs[head, :, cols].astype(F32) * (s_buf[:, cols] - delta)).astype(BF)
        rows = slice(head * HEAD, (head + 1) * HEAD)
        first, stop = STRIPES[head]
        dk_acc[rows, :] = stripe(head, plain(lanes(qw, first, stop, 0, 2), ds_buf[...])) * SCALE
        dq_acc[rows, :] = stripe(head, last_last(lanes(kw, first, stop, 0, SLOTS), ds_buf[...])) * SCALE

    def send_terms(piece):
        block = slice(piece * BLOCK, (piece + 1) * BLOCK)
        for side in range(2):
            cols = slice(side * 512, side * 512 + 256)
            kb[side, piece] = dk_acc[block, cols].astype(BF)
            send(kb.at[side, piece], rk.at[1 - side, piece], kt_rs.at[1 - side, piece], (behind, ahead)[side])

    backward(0)
    backward(1)
    send_terms(0)
    backward(2)
    backward(3)
    dqw[0] = dq_acc[:, 0:128].astype(BF)
    dqw[1] = dq_acc[:, 128:256].astype(BF)
    send(dqw.at[1 - xl], dqf, dq_rs, partner)
    write(dqw.at[xl], gq_hbm.at[near_rows])

    arrived(cf.at[away_rows], c_rs.at[1])
    projected = first_first(cf[...], wf[...].reshape(HW, D))
    for block in range(11):
        cols = slice(block * 128, (block + 1) * 128)
        att_ref[:, cols] = jnp.where(own_live, projected[:, cols], 0.0).astype(BF)
    write(att_ref, att_hbm)

    lax.fori_loop(0, 8, quad_here, 0)
    total = rx[0].astype(F32)
    for source in range(1, 8):
        total = total + rx[source].astype(F32)
    fr[group] = total.astype(BF)
    for step in (2, 1, 3):
        send(fr.at[group], fr.at[group], f_rs.at[group], far(step))
    send_terms(1)

    def sum_values():
        for side in range(2):
            arrived(rv.at[side], vt_rs.at[side])
        value = dv_acc[:, 256:512] + rv[0].astype(F32) + rv[1].astype(F32)
        vs[0] = value[:, 0:128].astype(BF)
        vs[1] = value[:, 128:256].astype(BF)
        send(vs.at[1 - xl], vf, vf_rs, partner)
        write(vs.at[xl], gv_hbm.at[near_rows])

    def key_rows(half, piece):
        return gk_hbm.at[pl.ds(pl.multiple_of(half * HALF + piece * BLOCK, 16), BLOCK)]

    def sum_keys(piece):
        block = slice(piece * BLOCK, (piece + 1) * BLOCK)
        for side in range(2):
            arrived(rk.at[side, piece], kt_rs.at[side, piece])
        value = dk_acc[block, 256:512] + rk[0, piece].astype(F32) + rk[1, piece].astype(F32)
        ks[0, piece] = value[:, 0:128].astype(BF)
        ks[1, piece] = value[:, 128:256].astype(BF)
        send(ks.at[1 - xl, piece], kf.at[piece], kf_rs.at[piece], partner)
        write(ks.at[xl, piece], key_rows(xl, piece))

    sum_values()
    sum_keys(0)
    arrived(dqf, dq_rs)
    write(dqf, gq_hbm.at[away_rows])

    for step in range(1, 4):
        source = lax.rem(group + step, 4)
        arrived(fr.at[source], f_rs.at[source])
    total = fr[0].astype(F32) + fr[1].astype(F32) + fr[2].astype(F32) + fr[3].astype(F32)
    gf[spot, inner] = total.astype(BF)

    def spread(j, carry):
        pltpu.make_async_remote_copy(
            src_ref=gf.at[spot, inner], dst_ref=gf.at[spot, inner], send_sem=z_ss.at[0], recv_sem=z_rs.at[0],
            device_id=quad(xh * 2 + xl, lax.rem(inner + j, 4)), device_id_type=MESH).start()
        return carry

    def share(j, carry):
        pltpu.make_async_remote_copy(
            src_ref=gf.at[spot], dst_ref=gf.at[spot], send_sem=z_ss.at[1], recv_sem=z_rs.at[1],
            device_id=around(j), device_id_type=MESH).start()
        return carry

    three = incoming(gf.at[0, pl.ds(0, 3)], z_rs.at[0], z_ss.at[0])
    seven = incoming(gf.at[pl.ds(0, 7)], z_rs.at[1], z_ss.at[1])
    lax.fori_loop(1, 4, spread, 0)
    sum_keys(1)
    three.wait_recv()
    lax.fori_loop(1, 8, share, 0)

    arrived(vf, vf_rs)
    write(vf, gv_hbm.at[away_rows])
    for piece in range(2):
        arrived(kf.at[piece], kf_rs.at[piece])
        write(kf.at[piece], key_rows(1 - xl, piece))

    seven.wait_recv()
    write(gf, gw_hbm)
    for copy in sent:
        copy.wait_send()
    @pl.when(y != 3)
    def _():
        extra_copy().wait_send()

    lax.fori_loop(0, 8, quad_sent, 0)
    three.wait_send()
    seven.wait_send()
    for copy in written:
        copy.wait()


def hand_over(att_in, gq_in, gk_in, gv_in, gw_in, att_out, gq_out, gk_out, gv_out, gw_out,
              att, gq, gk, gv, tiles, gw, in_sems, out_sems):
    held = (tiles, att, gq, gk, gv)
    reads = [pltpu.make_async_copy(source, target, in_sems.at[i])
             for i, (source, target) in enumerate(zip((gw_in, att_in, gq_in, gk_in, gv_in), held))]
    for read in reads:
        read.start()
    writes = []

    def write(source, target):
        writes.append(pltpu.make_async_copy(source, target, out_sems.at[len(writes)]))
        writes[-1].start()

    reads[0].wait()
    for first, stop in ((0, 6), (6, 11)):
        for tile in range(TILES):
            row, column = tile % 32 % 11, tile // 32 * 3 + tile % 32 // 11
            if tile >= 96 + 22:
                row, column = 10, (tile - 118) * 3 + 2
            if first <= row < stop:
                gw[row * 16:row * 16 + 16, column * 128:(column + 1) * 128] = tiles[
                    tile // 16, tile // 4 % 4, tile % 4].astype(F32)
        rows = pl.ds(first * 16, (stop - first) * 16)
        write(gw.at[rows], gw_out.at[rows])
    for read, source, target in zip(reads[1:], held[1:], (att_out, gq_out, gk_out, gv_out)):
        read.wait()
        write(source, target)
    for copy in writes:
        copy.wait()


def per_device(queries, keys, values, patch_ids, counts, cotangent, w_out):
    hbm = pl.BlockSpec(memory_space=pltpu.HBM)
    tiles = (8, 4, 4, 16, 128)
    halves = (2, HALF, ROWS)
    window = (SLOTS, HALF, ROWS)
    dma = pltpu.SemaphoreType.DMA
    scratch = [
        pltpu.VMEM((PLACES, ROWS), jnp.int32), pltpu.SMEM((1, PLACES), jnp.int32), pltpu.VMEM((ROWS, D), BF),
        pltpu.VMEM((ROWS, D), BF),
        pltpu.VMEM(window, BF), pltpu.VMEM(window, BF), pltpu.VMEM(halves, BF), pltpu.VMEM((256, HALF), BF),
        pltpu.VMEM((4, 4, ROWS, PIECE), BF), pltpu.VMEM((4, BLOCK, D), BF),
        pltpu.VMEM((256, 768), F32), pltpu.VMEM((256, 768), F32),
        pltpu.VMEM((4, 256, 768), BF), pltpu.VMEM((256, 768), BF),
        pltpu.VMEM((HALF, 256), F32), pltpu.VMEM((HALF, 256), BF), pltpu.VMEM(halves, BF), pltpu.VMEM((HW, ROWS), BF),
        pltpu.VMEM((2, BLOCK, 256), BF), pltpu.VMEM((256, HALF), BF), pltpu.VMEM((HALF, 256), BF),
        pltpu.VMEM((HALF, 256), F32), pltpu.VMEM((HALF, 768), F32), pltpu.VMEM((HALF, 768), F32),
        pltpu.VMEM(halves, BF), pltpu.VMEM((HALF, ROWS), BF),
        pltpu.VMEM((2, 2, BLOCK, 256), BF), pltpu.VMEM((2, HALF, 256), BF),
        pltpu.VMEM((2, 2, BLOCK, 256), BF), pltpu.VMEM((2, HALF, 256), BF),
        pltpu.VMEM((2, 2, BLOCK, ROWS), BF), pltpu.VMEM(halves, BF),
        pltpu.VMEM((2, BLOCK, ROWS), BF), pltpu.VMEM((HALF, ROWS), BF),
        pltpu.VMEM((4, 32, 16, 128), BF), pltpu.VMEM((4, 16, 128), BF),
        pltpu.VMEM((3, 32, 16, 128), BF), pltpu.VMEM((3, 3, 16, 128), BF),
        pltpu.VMEM((8, 4, 16, 128), BF), pltpu.VMEM((8, 4, 16, 128), BF),
        pltpu.VMEM((4, 4, 16, 128), BF), pltpu.VMEM(tiles, BF),
        dma((6,)), dma((6,)), dma, dma((4, 4)), dma((4,)), dma((2,)), dma, dma((2, 2)), dma((2,)), dma((2,)), dma,
        dma((3,)), dma((3,)), dma((8,)),
        dma((4,)), dma((2,)),
        dma((48,)), dma, dma((8,)), dma((2,)), dma((7,)), dma((12,)),
    ]
    shapes = (
        jax.ShapeDtypeStruct((ROWS, D), BF),
        jax.ShapeDtypeStruct((HW, ROWS), BF),
        jax.ShapeDtypeStruct((HW, ROWS), BF),
        jax.ShapeDtypeStruct((HW, ROWS), BF),
    )
    outs = pl.pallas_call(
        kernel,
        out_shape=shapes + (jax.ShapeDtypeStruct(tiles, BF),),
        in_specs=[hbm] * 7,
        out_specs=(hbm,) * 5,
        scratch_shapes=scratch,
        compiler_params=pltpu.CompilerParams(
            collective_id=0, has_side_effects=True, vmem_limit_bytes=VMEM_LIMIT),
        cost_estimate=pl.CostEstimate(flops=1500000000, bytes_accessed=4000000, transcendentals=800000),
    )(queries[0].T, keys[0].T, values[0].T, patch_ids.reshape(PLACES, ROWS), counts, cotangent[0], w_out)
    outs = pl.pallas_call(
        hand_over,
        out_shape=shapes + (jax.ShapeDtypeStruct((BLOCK, D), F32),),
        in_specs=[hbm] * 5,
        out_specs=(hbm,) * 5,
        scratch_shapes=[
            pltpu.VMEM((ROWS, D), BF), pltpu.VMEM((HW, ROWS), BF), pltpu.VMEM((HW, ROWS), BF), pltpu.VMEM((HW, ROWS), BF),
            pltpu.VMEM(tiles, BF), pltpu.VMEM((BLOCK, D), F32), dma((5,)), dma((6,))],
        compiler_params=pltpu.CompilerParams(vmem_limit_bytes=VMEM_LIMIT),
    )(*outs)
    attended, grad_queries, grad_keys, grad_values, grad_weight = outs
    return attended[None], grad_queries.T[None], grad_keys.T[None], grad_values.T[None], grad_weight


def solution(mesh):
    placed = (
        P("dp", "ctx", None),
        P("dp", "ctx", None),
        P("dp", "ctx", None),
        P("dp", None),
        P("dp", None),
        P("dp", "ctx", None),
        P("dp", None),
    )
    return jax.shard_map(
        per_device,
        mesh=mesh,
        in_specs=placed,
        out_specs=(
            P("dp", "ctx", None),
            P("dp", "ctx", None),
            P("dp", "ctx", None),
            P("dp", "ctx", None),
            P("dp", None),
        ),
        check_vma=False,
    )
```

```python
import jax
import jax.numpy as jnp
from jax import lax
from jax.experimental import pallas as pl
from jax.experimental.pallas import tpu as pltpu
from jax.sharding import PartitionSpec as P

HEAD = 88
WIN = 4
ROWS = 128
HALF = 352
HW = 704
D = 1408
BLOCK = 176
SLOTS = 6
PLACES = 128
SCALE = HEAD ** -0.5
MASKED = -1e30
TILES = 121
PIECE = 384
ORDER = (1, 3, 2, 0)
VMEM_LIMIT = 61 * 1024 * 1024
MESH = pl.DeviceIdType.MESH
WINDOWS = ((0, 128), (0, 256), (128, 352), (256, 352))
STRIPES = ((0, 96), (80, 176), (176, 272), (256, 352))
BF = jnp.bfloat16
F32 = jnp.float32


def last_last(left, right):
    return lax.dot_general(left, right, (((1,), (1,)), ((), ())), preferred_element_type=F32)


def first_first(left, right):
    return lax.dot_general(left, right, (((0,), (0,)), ((), ())), preferred_element_type=F32)


def plain(left, right):
    return jnp.dot(left, right, preferred_element_type=F32)


def head_mask(head, rows):
    low, high = WINDOWS[head]
    lane = lax.broadcasted_iota(jnp.int32, (rows, high - low), 1) + low
    return jnp.where((lane >= HEAD * head) & (lane < HEAD * (head + 1)), 1.0, 0.0)


def stripe(head, value):
    skip = HEAD * head - STRIPES[head][0]
    return value[skip:skip + HEAD]


def kernel(q_ref, k_ref, v_ref, pid_hbm, cnt_hbm, cot_hbm, w_ref,
           att_hbm, gq_hbm, gk_hbm, gv_hbm, gw_hbm,
           pid_ref, cnt_ref, cot_ref, att_ref,
           kw, vw, qw, qn, gl, wf, bias, s_buf, probs, ds_buf,
           ctx_acc, cb, cw, cf, ct, g_buf, gt_buf, dq_acc, dk_acc, dv_acc, dqw, dqf,
           kb, vb, rk, rv, ks, vs, kf, vf,
           dw, dwx, ry, ryx, sx, rx, fr, gf,
           k_rs, v_rs, q_rs, gl_rs, w_rs, c_rs, dq_rs, kt_rs, vt_rs, kf_rs, vf_rs, y_rs, yx_rs, x_rs, f_rs, z_rs,
           ss, y_ss, x_ss, z_ss, in_sems, out_sems):
    dp = lax.axis_index("dp")
    place = lax.axis_index("ctx")
    xh = lax.div(dp, 2)
    core = lax.rem(dp, 2)
    pair = lax.div(place, 2)
    xl = lax.rem(place, 2)
    y = lax.div(place, 32)
    z = lax.rem(pair, 16)
    group = lax.div(z, 4)
    inner = lax.rem(z, 4)
    spot = y * 2 + xl

    partner = (dp, place + 1 - 2 * xl)
    twin = (dp + 1 - 2 * core, place)
    other = lax.rem(dp + 2, 4)
    across = (other, place + 1 - 2 * xl)
    ahead = (dp, lax.rem(place + 2, PLACES))
    behind = (dp, lax.rem(place + PLACES - 2, PLACES))

    def around(j):
        where = lax.rem(spot + j, 8)
        return (dp, lax.div(where, 2) * 32 + z * 2 + lax.rem(where, 2))

    def quad(x, b):
        return (lax.div(x, 2) * 2 + core, (y * 16 + group * 4 + b) * 2 + lax.rem(x, 2))

    def far(j):
        return (dp, (y * 16 + lax.rem(z + 4 * j, 16)) * 2 + xl)

    near_rows = pl.ds(pl.multiple_of(xl * HALF, 16), HALF)
    away_rows = pl.ds(pl.multiple_of((1 - xl) * HALF, 16), HALF)
    written = []

    def write(source, target):
        written.append(pltpu.make_async_copy(source, target, out_sems.at[len(written)]))
        written[-1].start()

    barrier = pltpu.get_barrier_semaphore()

    def greet(device):
        pl.semaphore_signal(barrier, inc=1, device_id=device, device_id_type=MESH)

    def greet_quad(j, carry):
        at = lax.rem((xh * 2 + xl) * 4 + inner + j, 16)
        greet(quad(lax.div(at, 4), lax.rem(at, 4)))
        return carry

    def greet_around(j, carry):
        greet(around(j))
        return carry

    def greet_far(j, carry):
        greet(far(j))
        return carry

    lax.fori_loop(1, 4, greet_far, 0)
    for device in (ahead, behind, twin):
        greet(device)
    lax.fori_loop(1, 16, greet_quad, 0)
    lax.fori_loop(2 - xl, 8 - xl, greet_around, 0)

    def piece_at(step):
        return lax.rem(y + step, 4)

    fetches = []
    for source, target in (
            (cot_hbm, cot_ref), (cnt_hbm, cnt_ref), (pid_hbm, pid_ref), (k_ref.at[near_rows], kw.at[2 + xl]),
            (q_ref.at[near_rows], qw.at[xl]), (v_ref.at[near_rows], vw.at[2 + xl]), (w_ref, wf.at[dp])):
        fetches.append(pltpu.make_async_copy(source, target, in_sems.at[len(fetches)]))
        fetches[-1].start()

    pl.semaphore_wait(barrier, 27)

    sent = []

    def send(source, target, recv_sem, device):
        copy = pltpu.make_async_remote_copy(
            src_ref=source, dst_ref=target, send_sem=ss.at[len(sent)], recv_sem=recv_sem,
            device_id=device, device_id_type=MESH)
        copy.start()
        sent.append(copy)

    def incoming(ref, recv_sem, send_sem):
        return pltpu.make_async_remote_copy(
            src_ref=ref, dst_ref=ref, send_sem=send_sem, recv_sem=recv_sem,
            device_id=partner, device_id_type=MESH)

    def arrived(ref, recv_sem):
        incoming(ref, recv_sem, ss.at[0]).wait_recv()

    away = 3 - xl
    send(k_ref.at[away_rows], kw.at[2 + xl], k_rs.at[2 + xl], partner)
    send(k_ref.at[near_rows], kw.at[xl], k_rs.at[xl], ahead)
    send(k_ref.at[near_rows], kw.at[4 + xl], k_rs.at[4 + xl], behind)
    send(v_ref.at[away_rows], vw.at[2 + xl], v_rs.at[2 + xl], partner)
    send(v_ref.at[near_rows], vw.at[xl], v_rs.at[xl], ahead)
    send(v_ref.at[near_rows], vw.at[4 + xl], v_rs.at[4 + xl], behind)
    send(q_ref.at[away_rows], qw.at[xl], q_rs, partner)
    fetches[0].wait()
    fetches[1].wait()
    own_live = lax.broadcasted_iota(jnp.int32, (ROWS, 128), 0) < cnt_ref[0, place]
    mine = core * 2 + xl
    for block in range(11):
        cols = slice(block * 128, (block + 1) * 128)
        inside = slice(block % 3 * 128, (block % 3 + 1) * 128)
        gl[block // 3, mine, :, inside] = jnp.where(own_live, cot_ref[:, cols].astype(F32), 0.0).astype(BF)
    gl[3, mine, :, 256:384] = jnp.zeros((ROWS, 128), BF)

    for step in ORDER:
        here = gl.at[piece_at(step), mine]
        send(here, here, gl_rs.at[mine, step], partner)
    send(w_ref, wf.at[dp], w_rs.at[dp], across)
    send(w_ref, wf.at[dp], w_rs.at[dp], twin)
    send(gl.at[:, mine], gl.at[:, mine], gl_rs.at[mine, 0], twin)
    for fetch in fetches[2:]:
        fetch.wait()

    arrived(kw.at[away], k_rs.at[away])
    send(kw.at[away], kw.at[1 - xl], k_rs.at[1 - xl], ahead)
    send(kw.at[away], kw.at[5 - xl], k_rs.at[5 - xl], behind)
    arrived(vw.at[away], v_rs.at[away])
    send(vw.at[away], vw.at[1 - xl], v_rs.at[1 - xl], ahead)
    send(vw.at[away], vw.at[5 - xl], v_rs.at[5 - xl], behind)

    frames, live = [], []
    for slot in range(SLOTS):
        shard = lax.rem(2 * pair - 2 + slot + PLACES, PLACES)
        inside = (2 * pair - 2 + slot >= 0) & (2 * pair - 2 + slot < PLACES)
        count = jnp.where(inside, cnt_ref[0, shard], 0)
        frame = lax.shift_right_logical(pid_ref[pl.ds(shard, 1), :], 8) + 2 * (slot - 2)
        frames.append(frame.astype(F32))
        live.append(lax.broadcasted_iota(jnp.int32, (ROWS, 128), 1) < count)
    for half in range(2):
        column = jnp.transpose(jnp.broadcast_to(frames[2 + half], (ROWS, 128)))
        for slot in range(SLOTS):
            seen = live[slot] & (jnp.abs(frames[slot] - column) <= WIN)
            bias[half * 128:(half + 1) * 128, slot * 128:(slot + 1) * 128] = jnp.where(seen, 0.0, MASKED)

    arrived(qw.at[1 - xl], q_rs)
    for half in range(2):
        qn[half * 128:(half + 1) * 128, :] = jnp.transpose(qw[half].astype(F32)).astype(BF)
    for slot in (0, 1, 4, 5):
        arrived(kw.at[slot], k_rs.at[slot])

    def lanes(ref, low, high, first, slots):
        return jnp.concatenate([ref[first + i, low:high, :] for i in range(slots)], axis=1)

    def folded(op, value, old):
        here = op(value[:, :128], value[:, 128:])
        return here if old is None else op(old, here)

    theirs = core * 2 + 1 - xl

    def relay_cotangent(step):
        here = gl.at[piece_at(step), theirs]
        arrived(here, gl_rs.at[theirs, step])
        send(here, here, gl_rs.at[theirs, step], twin)

    for head in range(4):
        low, high = WINDOWS[head]
        q_head = qn[:, low:high] * head_mask(head, 256).astype(BF)
        top = None
        for part in range(3):
            cols = slice(part * 256, part * 256 + 256)
            score = plain(q_head, lanes(kw, low, high, part * 2, 2)) * SCALE + bias[:, cols]
            s_buf[:, cols] = score
            top = folded(jnp.maximum, score, top)
        top = jnp.max(top, axis=1, keepdims=True)
        total = None
        for part in range(3):
            cols = slice(part * 256, part * 256 + 256)
            expon = jnp.exp(s_buf[:, cols] - top)
            s_buf[:, cols] = expon
            total = folded(jnp.add, expon, total)
        inverse = 1.0 / jnp.sum(total, axis=1, keepdims=True)
        for part in range(3):
            cols = slice(part * 256, part * 256 + 256)
            probs[head, :, cols] = (s_buf[:, cols] * inverse).astype(BF)
    relay_cotangent(ORDER[0])
    for slot in (0, 1, 4, 5):
        arrived(vw.at[slot], v_rs.at[slot])
    for head in range(4):
        ctx_acc[head * HEAD:(head + 1) * HEAD, :] = stripe(
            head, last_last(lanes(vw, *STRIPES[head], 0, SLOTS), probs[head]))
    cb[...] = ctx_acc[...].astype(BF)
    core_rows = pl.ds(pl.multiple_of(core * BLOCK, 16), BLOCK)
    send(cb.at[pl.ds(pl.multiple_of((1 - core) * BLOCK, 16), BLOCK)], ct.at[core], c_rs.at[0], twin)
    cw[0] = cb[:, 0:128]
    cw[1] = cb[:, 128:256]
    ct[core] = cb[core_rows, :]
    cf[near_rows, :] = cw[xl]

    def weight_piece(step):
        piece = piece_at(step)
        there = (1 - core) * 2 + 1 - xl
        arrived(gl.at[piece, there], gl_rs.at[there, step])
        part = plain(context, gl[piece].reshape(512, PIECE))
        for tile in range(33):
            row, column = tile % 11 * 16, tile // 11 * 128
            value = part[row:row + 16, column:column + 128].astype(BF)
            if tile < 32:
                dw[piece, tile] = value
            else:
                dwx[piece] = value
        if step:
            send(dw.at[piece], ry.at[step - 1], y_rs.at[step - 1], (dp, piece * 32 + z * 2 + xl))

    def extra_copy():
        return pltpu.make_async_remote_copy(
            src_ref=dwx.at[pl.ds(0, 3)], dst_ref=ryx.at[y], send_sem=y_ss, recv_sem=yx_rs.at[y],
            device_id=(dp, 96 + z * 2 + xl), device_id_type=MESH)

    relay_cotangent(ORDER[1])
    arrived(gl.at[:, (1 - core) * 2 + xl], gl_rs.at[(1 - core) * 2 + xl, 0])
    arrived(ct.at[1 - core], c_rs.at[0])
    context = jnp.concatenate([ct[0], ct[1]], axis=1)
    weight_piece(ORDER[0])
    weight_piece(ORDER[1])
    arrived(wf.at[other], w_rs.at[other])
    send(wf.at[other], wf.at[other], w_rs.at[other], twin)
    relay_cotangent(ORDER[2])
    weight_piece(ORDER[2])

    relay_cotangent(ORDER[3])
    send(cw.at[1 - xl], cf.at[near_rows], c_rs.at[1], partner)
    weight_piece(ORDER[3])

    @pl.when(y != 3)
    def _():
        extra_copy().start()

    arrived(wf.at[dp + 1 - 2 * core], w_rs.at[dp + 1 - 2 * core])
    arrived(wf.at[other + 1 - 2 * core], w_rs.at[other + 1 - 2 * core])
    grad_context = None
    for piece in range(4):
        width = min(PIECE, D - piece * PIECE)
        part = last_last(
            gl[piece, pl.ds(core * 2, 2), :, 0:width].reshape(256, width),
            wf[pl.ds(xl * 2, 2), :, piece * PIECE:piece * PIECE + width].reshape(HALF, width))
        grad_context = part if grad_context is None else grad_context + part
    g_buf[...] = grad_context.astype(BF)
    gt_buf[...] = jnp.transpose(grad_context).astype(BF)

    for head in range(4):
        first, stop = STRIPES[head]
        dv_acc[head * HEAD:(head + 1) * HEAD, :] = stripe(head, plain(gt_buf[first:stop, :], probs[head]))
    for side in range(2):
        vb[side] = dv_acc[:, side * 512:side * 512 + 256].astype(BF)
        send(vb.at[side], rv.at[1 - side], vt_rs.at[1 - side], (behind, ahead)[side])

    for step in range(3):
        arrived(ry.at[step], y_rs.at[step])
    total = dw[y].astype(F32) + ry[0].astype(F32) + ry[1].astype(F32) + ry[2].astype(F32)
    sx[...] = total.astype(BF).reshape(8, 4, 16, 128)

    @pl.when(y == 3)
    def _():
        for source in range(3):
            arrived(ryx.at[source], yx_rs.at[source])
        for tile in range(22, 25):
            own = tile - 22
            total = dwx[own].astype(F32)
            for source in range(3):
                total = total + ryx[source, own].astype(F32)
            sx[tile // 4, tile % 4] = total.astype(BF)

    def stays(half, b):
        return (xh == xl) & (xl == half) & (inner == b)

    def quad_copy(n):
        half, b = lax.div(n, 4), lax.rem(n, 4)
        return pltpu.make_async_remote_copy(
            src_ref=sx.at[n], dst_ref=rx.at[xh * 4 + inner], send_sem=x_ss.at[n], recv_sem=x_rs.at[xh * 4 + inner],
            device_id=quad(xl * 2 + half, b), device_id_type=MESH)

    def quad_start(n, carry):
        @pl.when(jnp.logical_not(stays(lax.div(n, 4), lax.rem(n, 4))))
        def _():
            quad_copy(n).start()

        return carry

    def quad_sent(n, carry):
        @pl.when(jnp.logical_not(stays(lax.div(n, 4), lax.rem(n, 4))))
        def _():
            quad_copy(n).wait_send()

        return carry

    def quad_here(n, carry):
        @pl.when(jnp.logical_not((xh == xl) & (n == xh * 4 + inner)))
        def _():
            arrived(rx.at[n], x_rs.at[n])

        return carry

    lax.fori_loop(0, 8, quad_start, 0)

    @pl.when(xh == xl)
    def _():
        rx[xh * 4 + inner] = sx[xl * 4 + inner]

    def backward(head):
        low, high = WINDOWS[head]
        g_head = g_buf[:, low:high] * head_mask(head, 256).astype(BF)
        delta = None
        for part in range(3):
            cols = slice(part * 256, part * 256 + 256)
            grad_prob = plain(g_head, lanes(vw, low, high, part * 2, 2))
            s_buf[:, cols] = grad_prob
            delta = folded(jnp.add, probs[head, :, cols].astype(F32) * grad_prob, delta)
        delta = jnp.sum(delta, axis=1, keepdims=True)
        for part in range(3):
            cols = slice(part * 256, part * 256 + 256)
            ds_buf[:, cols] = (probs[head, :, cols].astype(F32) * (s_buf[:, cols] - delta)).astype(BF)
        rows = slice(head * HEAD, (head + 1) * HEAD)
        first, stop = STRIPES[head]
        dk_acc[rows, :] = stripe(head, plain(lanes(qw, first, stop, 0, 2), ds_buf[...])) * SCALE
        dq_acc[rows, :] = stripe(head, last_last(lanes(kw, first, stop, 0, SLOTS), ds_buf[...])) * SCALE

    def send_terms(piece):
        block = slice(piece * BLOCK, (piece + 1) * BLOCK)
        for side in range(2):
            cols = slice(side * 512, side * 512 + 256)
            kb[side, piece] = dk_acc[block, cols].astype(BF)
            send(kb.at[side, piece], rk.at[1 - side, piece], kt_rs.at[1 - side, piece], (behind, ahead)[side])

    backward(0)
    backward(1)
    send_terms(0)
    backward(2)
    backward(3)
    dqw[0] = dq_acc[:, 0:128].astype(BF)
    dqw[1] = dq_acc[:, 128:256].astype(BF)
    send(dqw.at[1 - xl], dqf, dq_rs, partner)
    write(dqw.at[xl], gq_hbm.at[near_rows])

    arrived(cf.at[away_rows], c_rs.at[1])
    projected = first_first(cf[...], wf[...].reshape(HW, D))
    for block in range(11):
        cols = slice(block * 128, (block + 1) * 128)
        att_ref[:, cols] = jnp.where(own_live, projected[:, cols], 0.0).astype(BF)
    write(att_ref, att_hbm)

    lax.fori_loop(0, 8, quad_here, 0)
    total = rx[0].astype(F32)
    for source in range(1, 8):
        total = total + rx[source].astype(F32)
    fr[group] = total.astype(BF)
    for step in (2, 1, 3):
        send(fr.at[group], fr.at[group], f_rs.at[group], far(step))
    send_terms(1)

    def sum_values():
        for side in range(2):
            arrived(rv.at[side], vt_rs.at[side])
        value = dv_acc[:, 256:512] + rv[0].astype(F32) + rv[1].astype(F32)
        vs[0] = value[:, 0:128].astype(BF)
        vs[1] = value[:, 128:256].astype(BF)
        send(vs.at[1 - xl], vf, vf_rs, partner)
        write(vs.at[xl], gv_hbm.at[near_rows])

    def key_rows(half, piece):
        return gk_hbm.at[pl.ds(pl.multiple_of(half * HALF + piece * BLOCK, 16), BLOCK)]

    def sum_keys(piece):
        block = slice(piece * BLOCK, (piece + 1) * BLOCK)
        for side in range(2):
            arrived(rk.at[side, piece], kt_rs.at[side, piece])
        value = dk_acc[block, 256:512] + rk[0, piece].astype(F32) + rk[1, piece].astype(F32)
        ks[0, piece] = value[:, 0:128].astype(BF)
        ks[1, piece] = value[:, 128:256].astype(BF)
        send(ks.at[1 - xl, piece], kf.at[piece], kf_rs.at[piece], partner)
        write(ks.at[xl, piece], key_rows(xl, piece))

    sum_values()
    sum_keys(0)
    arrived(dqf, dq_rs)
    write(dqf, gq_hbm.at[away_rows])

    for step in range(1, 4):
        source = lax.rem(group + step, 4)
        arrived(fr.at[source], f_rs.at[source])
    total = fr[0].astype(F32) + fr[1].astype(F32) + fr[2].astype(F32) + fr[3].astype(F32)
    gf[spot, inner] = total.astype(BF)

    def spread(j, carry):
        pltpu.make_async_remote_copy(
            src_ref=gf.at[spot, inner], dst_ref=gf.at[spot, inner], send_sem=z_ss.at[0], recv_sem=z_rs.at[0],
            device_id=quad(xh * 2 + xl, lax.rem(inner + j, 4)), device_id_type=MESH).start()
        return carry

    def share(j, carry):
        pltpu.make_async_remote_copy(
            src_ref=gf.at[spot], dst_ref=gf.at[spot], send_sem=z_ss.at[1], recv_sem=z_rs.at[1],
            device_id=around(j), device_id_type=MESH).start()
        return carry

    three = incoming(gf.at[0, pl.ds(0, 3)], z_rs.at[0], z_ss.at[0])
    seven = incoming(gf.at[pl.ds(0, 7)], z_rs.at[1], z_ss.at[1])
    lax.fori_loop(1, 4, spread, 0)
    sum_keys(1)
    three.wait_recv()
    lax.fori_loop(1, 8, share, 0)

    arrived(vf, vf_rs)
    write(vf, gv_hbm.at[away_rows])
    for piece in range(2):
        arrived(kf.at[piece], kf_rs.at[piece])
        write(kf.at[piece], key_rows(1 - xl, piece))

    seven.wait_recv()
    write(gf, gw_hbm)
    for copy in sent:
        copy.wait_send()
    @pl.when(y != 3)
    def _():
        extra_copy().wait_send()

    lax.fori_loop(0, 8, quad_sent, 0)
    three.wait_send()
    seven.wait_send()
    for copy in written:
        copy.wait()


def hand_over(att_in, gq_in, gk_in, gv_in, gw_in, att_out, gq_out, gk_out, gv_out, gw_out,
              att, gq, gk, gv, tiles, gw, in_sems, out_sems):
    held = (tiles, att, gq, gk, gv)
    outs = (gw_out, att_out, gq_out, gk_out, gv_out)
    reads = [pltpu.make_async_copy(source, target, in_sems.at[i])
             for i, (source, target) in enumerate(zip((gw_in, att_in, gq_in, gk_in, gv_in), held))]
    writes = [pltpu.make_async_copy(source, target, out_sems.at[i])
              for i, (source, target) in enumerate(zip((gw,) + held[1:], outs))]
    for read in reads:
        read.start()
    for read, copy in list(zip(reads, writes))[1:]:
        read.wait()
        copy.start()
    reads[0].wait()
    for tile in range(TILES):
        row, column = tile % 32 % 11, tile // 32 * 3 + tile % 32 // 11
        if tile >= 96 + 22:
            row, column = 10, (tile - 118) * 3 + 2
        gw[row * 16:row * 16 + 16, column * 128:(column + 1) * 128] = tiles[
            tile // 16, tile // 4 % 4, tile % 4].astype(F32)
    writes[0].start()
    for copy in writes:
        copy.wait()


def per_device(queries, keys, values, patch_ids, counts, cotangent, w_out):
    hbm = pl.BlockSpec(memory_space=pltpu.HBM)
    tiles = (8, 4, 4, 16, 128)
    halves = (2, HALF, ROWS)
    window = (SLOTS, HALF, ROWS)
    dma = pltpu.SemaphoreType.DMA
    scratch = [
        pltpu.VMEM((PLACES, ROWS), jnp.int32), pltpu.SMEM((1, PLACES), jnp.int32), pltpu.VMEM((ROWS, D), BF),
        pltpu.VMEM((ROWS, D), BF),
        pltpu.VMEM(window, BF), pltpu.VMEM(window, BF), pltpu.VMEM(halves, BF), pltpu.VMEM((256, HALF), BF),
        pltpu.VMEM((4, 4, ROWS, PIECE), BF), pltpu.VMEM((4, BLOCK, D), BF),
        pltpu.VMEM((256, 768), F32), pltpu.VMEM((256, 768), F32),
        pltpu.VMEM((4, 256, 768), BF), pltpu.VMEM((256, 768), BF),
        pltpu.VMEM((HALF, 256), F32), pltpu.VMEM((HALF, 256), BF), pltpu.VMEM(halves, BF), pltpu.VMEM((HW, ROWS), BF),
        pltpu.VMEM((2, BLOCK, 256), BF), pltpu.VMEM((256, HALF), BF), pltpu.VMEM((HALF, 256), BF),
        pltpu.VMEM((HALF, 256), F32), pltpu.VMEM((HALF, 768), F32), pltpu.VMEM((HALF, 768), F32),
        pltpu.VMEM(halves, BF), pltpu.VMEM((HALF, ROWS), BF),
        pltpu.VMEM((2, 2, BLOCK, 256), BF), pltpu.VMEM((2, HALF, 256), BF),
        pltpu.VMEM((2, 2, BLOCK, 256), BF), pltpu.VMEM((2, HALF, 256), BF),
        pltpu.VMEM((2, 2, BLOCK, ROWS), BF), pltpu.VMEM(halves, BF),
        pltpu.VMEM((2, BLOCK, ROWS), BF), pltpu.VMEM((HALF, ROWS), BF),
        pltpu.VMEM((4, 32, 16, 128), BF), pltpu.VMEM((4, 16, 128), BF),
        pltpu.VMEM((3, 32, 16, 128), BF), pltpu.VMEM((3, 3, 16, 128), BF),
        pltpu.VMEM((8, 4, 16, 128), BF), pltpu.VMEM((8, 4, 16, 128), BF),
        pltpu.VMEM((4, 4, 16, 128), BF), pltpu.VMEM(tiles, BF),
        dma((6,)), dma((6,)), dma, dma((4, 4)), dma((4,)), dma((2,)), dma, dma((2, 2)), dma((2,)), dma((2,)), dma,
        dma((3,)), dma((3,)), dma((8,)),
        dma((4,)), dma((2,)),
        dma((48,)), dma, dma((8,)), dma((2,)), dma((7,)), dma((12,)),
    ]
    shapes = (
        jax.ShapeDtypeStruct((ROWS, D), BF),
        jax.ShapeDtypeStruct((HW, ROWS), BF),
        jax.ShapeDtypeStruct((HW, ROWS), BF),
        jax.ShapeDtypeStruct((HW, ROWS), BF),
    )
    outs = pl.pallas_call(
        kernel,
        out_shape=shapes + (jax.ShapeDtypeStruct(tiles, BF),),
        in_specs=[hbm] * 7,
        out_specs=(hbm,) * 5,
        scratch_shapes=scratch,
        compiler_params=pltpu.CompilerParams(
            collective_id=0, has_side_effects=True, vmem_limit_bytes=VMEM_LIMIT),
        cost_estimate=pl.CostEstimate(flops=1500000000, bytes_accessed=4000000, transcendentals=800000),
    )(queries[0].T, keys[0].T, values[0].T, patch_ids.reshape(PLACES, ROWS), counts, cotangent[0], w_out)
    outs = pl.pallas_call(
        hand_over,
        out_shape=shapes + (jax.ShapeDtypeStruct((BLOCK, D), F32),),
        in_specs=[hbm] * 5,
        out_specs=(hbm,) * 5,
        scratch_shapes=[
            pltpu.VMEM((ROWS, D), BF), pltpu.VMEM((HW, ROWS), BF), pltpu.VMEM((HW, ROWS), BF), pltpu.VMEM((HW, ROWS), BF),
            pltpu.VMEM(tiles, BF), pltpu.VMEM((BLOCK, D), F32), dma((5,)), dma((5,))],
        compiler_params=pltpu.CompilerParams(vmem_limit_bytes=VMEM_LIMIT),
    )(*outs)
    attended, grad_queries, grad_keys, grad_values, grad_weight = outs
    return attended[None], grad_queries.T[None], grad_keys.T[None], grad_values.T[None], grad_weight


def solution(mesh):
    placed = (
        P("dp", "ctx", None),
        P("dp", "ctx", None),
        P("dp", "ctx", None),
        P("dp", None),
        P("dp", None),
        P("dp", "ctx", None),
        P("dp", None),
    )
    return jax.shard_map(
        per_device,
        mesh=mesh,
        in_specs=placed,
        out_specs=(
            P("dp", "ctx", None),
            P("dp", "ctx", None),
            P("dp", "ctx", None),
            P("dp", "ctx", None),
            P("dp", None),
        ),
        check_vma=False,
    )
```
